512 devices in a mesh: row: 16 (over x, z_hi, core), lon: 32 (over y, z_lo).
Axes of the slice: x: 4, y: 4, z: 16 (z_hi: 2, z_lo: 8; z = z_hi * 8 + z_lo), core: 2. Of those that a mesh axis runs over, the one named last changes fastest.
Arguments:
- coarse: bfloat16 [128, 12, 32], P('lon')
- src_blocks: int32 [512, 4], P(('row', 'lon')), may hold values from 0 to 127, as said below
- slot_counts: int32 [512], P(('row', 'lon')), may hold values from 1 to 4
- remap_tiles: bfloat16 [512, 4, 32, 1024], P(('row', 'lon'))
- conv_a: float32 [3, 3, 12, 128], replicated, may hold values from -0.625 to 0.625
- conv_b: float32 [3, 3, 128, 128], replicated, may hold values from -0.1875 to 0.1875
- gain_a: float32 [128], replicated, may hold values from 0.5 to 1.5
- shift_a: float32 [128], replicated, may hold values from -3 to 3
- gain_b: float32 [128], replicated, may hold values from 0.5 to 1.5
- shift_b: float32 [128], replicated, may hold values from -3 to 3
Outputs:
- level_out: bfloat16 [128, 4096, 128], P('row', 'lon')
The draws below stay inside these ranges and needn't reach their ends.
Inputs may be any that keep to these rules, and one draw needn't show every extreme that they name: `src_blocks`: block b is held by longitude index b // 4; every slot of a tile on longitude index l names a block held by longitude index l - 1, l or l + 1 (periodic). Slots at or past the tile's count are unused.
All inputs are finite; a program needn't handle non-finite values.
Results may differ from the reference program's by a relative error of at most 0.0022.
Values may be sent and summed in bfloat16 or wider, within the bound.
A program may use at most 64 MiB of HBM per device.

```python
import jax
import jax.numpy as jnp
from jax import lax

ROWS_DEV = 8
COLS_DEV = 128
VARS = 12
CH = 128
GROUPS = 32
SLOTS = 4
BCELLS = 32
BLK_DEV = 4
TILES = 512
NBLK = 128
CELLS = 1024
ROWS = 128
COLS = 4096
N_ROW = 16
N_LON = 32


def draw_coarse(key, part):
    key = jax.random.fold_in(key, 17)
    first, second = jax.random.split(key)
    offset = jax.random.uniform(first, (1, VARS, 1), jnp.float32, -0.25, 0.25)
    base = jax.random.normal(second, (NBLK, VARS, BCELLS), jnp.float32)
    return (base + offset).astype(jnp.bfloat16)


def draw_src_blocks(key, part):
    key = jax.random.fold_in(key, 11)
    offsets = jax.random.randint(key, (TILES, SLOTS), 0, 3 * BLK_DEV)
    offsets = offsets.at[0, 0].set(BLK_DEV).at[0, 1].set(BLK_DEV - 1)
    offsets = offsets.at[0, 2].set(0).at[0, SLOTS - 1].set(3 * BLK_DEV - 1)
    lon_place = jnp.arange(TILES, dtype=jnp.int32) % N_LON
    return jnp.mod((lon_place[:, None] - 1) * BLK_DEV + offsets, NBLK).astype(jnp.int32)


def draw_slot_counts(key, part):
    key = jax.random.fold_in(key, 23)
    drawn = jax.random.randint(key, (TILES,), 1, SLOTS + 1)
    return drawn.at[0].set(SLOTS).at[1].set(1).astype(jnp.int32)


def draw_remap_tiles(key, part):
    key = jax.random.fold_in(key, 13)
    entries = jax.random.uniform(key, (TILES, SLOTS, BCELLS, CELLS), jnp.float32)
    ramp = jnp.arange(TILES, dtype=jnp.float32) / (TILES - 1)
    scale = 1.0 + 2.0 * ramp
    return (scale[:, None, None, None] * (entries - 0.35) * (2.0 / (SLOTS * BCELLS) ** 0.5)).astype(jnp.bfloat16)


def scatter_about(own_key, dims, width, bound, kind=jnp.bfloat16):
    values = width * jax.random.normal(own_key, dims, jnp.float32)
    return jnp.clip(values, min=-bound, max=bound).astype(kind)


def setup_inputs(seed: int = 0) -> dict:
    key_of = jax.random.split(jax.random.key(seed), 11)
    coarse = draw_coarse(jax.random.fold_in(key_of[10], 71), 0)
    src_blocks = draw_src_blocks(jax.random.fold_in(key_of[10], 71), 0)
    slot_counts = draw_slot_counts(jax.random.fold_in(key_of[10], 71), 0)
    remap_tiles = draw_remap_tiles(jax.random.fold_in(key_of[10], 71), 0)
    conv_a = scatter_about(key_of[4], (3, 3, VARS, CH), (9 * VARS) ** -0.5, 0.625, jnp.float32)
    conv_b = scatter_about(key_of[5], (3, 3, CH, CH), (9 * CH) ** -0.5, 0.1875, jnp.float32)
    gain_a = jnp.clip(jax.random.uniform(key_of[6], (CH,), jnp.float32, 0.5, 1.5), 0.5, 1.5)
    shift_a = scatter_about(key_of[7], (CH,), 0.5, 3.0, jnp.float32)
    gain_b = jnp.clip(jax.random.uniform(key_of[8], (CH,), jnp.float32, 0.5, 1.5), 0.5, 1.5)
    shift_b = scatter_about(key_of[9], (CH,), 0.5, 3.0, jnp.float32)
    return dict(coarse=coarse, src_blocks=src_blocks, slot_counts=slot_counts, remap_tiles=remap_tiles, conv_a=conv_a, conv_b=conv_b, gain_a=gain_a, shift_a=shift_a, gain_b=gain_b, shift_b=shift_b)


eps = 1e-05

def conv_wrap(field, weights):
    padded = jnp.concatenate([field[:, -1:], field, field[:, :1]], axis=1)
    padded = jnp.pad(padded, ((1, 1), (0, 0), (0, 0)))
    result = lax.conv_general_dilated(padded[None], weights, (1, 1), 'VALID', dimension_numbers=('NHWC', 'HWIO', 'NHWC'), precision=lax.Precision.HIGHEST)
    return result[0]

def group_norm(field, gain, shift):
    shape_whole = field.shape
    grouped = field.reshape(shape_whole[0], shape_whole[1], GROUPS, CH // GROUPS)
    average = lax.optimization_barrier(jnp.mean(grouped, axis=(0, 1, 3)))
    centered = grouped - average[:, None]
    spread = lax.optimization_barrier(jnp.mean(centered * centered, axis=(0, 1, 3)))
    normed = centered * lax.rsqrt(spread + eps)[:, None]
    normed = normed.reshape(shape_whole) * gain + shift
    return jax.nn.silu(normed)

def reference(coarse, src_blocks, slot_counts, remap_tiles, conv_a, conv_b, gain_a, shift_a, gain_b, shift_b):

    def one_tile(inputs):
        sources, number, weights = inputs
        blocks = coarse[sources].astype(jnp.float32)
        live_slot = jnp.arange(SLOTS) < number
        blocks = jnp.where(live_slot[:, None, None], blocks, jnp.float32(0.0))
        return jnp.einsum('kvb,kbc->vc', blocks, weights.astype(jnp.float32), precision=lax.Precision.HIGHEST)
    tiles_out = lax.map(one_tile, (src_blocks, slot_counts, remap_tiles))
    fine_field = tiles_out.reshape(N_ROW, N_LON, VARS, ROWS_DEV, COLS_DEV)
    fine_field = jnp.transpose(fine_field, (0, 3, 1, 4, 2)).reshape(ROWS, COLS, VARS)
    hidden_a = conv_wrap(fine_field, conv_a)
    activ_a = group_norm(hidden_a, gain_a, shift_a)
    hidden_b = conv_wrap(activ_a, conv_b)
    return group_norm(hidden_b, gain_b, shift_b).astype(jnp.bfloat16)
```

```python
import jax
import jax.numpy as jnp
from jax import lax
from jax.experimental import pallas as pl
from jax.experimental.pallas import tpu as pltpu
from jax.sharding import PartitionSpec as P

ROWS_DEV = 8
COLS_DEV = 128
VARS = 12
CH = 128
GROUPS = 32
SLOTS = 4
BCELLS = 32
BLK_DEV = 4
NBLK = 128
PER_GROUP = CH // GROUPS
MESH = pl.DeviceIdType.MESH
F32 = jnp.float32
BF16 = jnp.bfloat16

eps = 1e-05


def coords():
    row = lax.axis_index("row")
    lon = lax.axis_index("lon")
    core = lax.rem(row, 2)
    z_hi = lax.rem(lax.div(row, 2), 2)
    x = lax.div(row, 4)
    y = lax.div(lon, 8)
    z = z_hi * 8 + lax.rem(lon, 8)
    return row, lon, x, y, z, core


def device_at(x, y, z, core):
    return (x * 4 + lax.div(z, 8) * 2 + core, y * 8 + lax.rem(z, 8))


def moved(value, step, count):
    return lax.rem(value + step, count) if step else value


def along_z(place):
    _, _, x, y, z, core = place
    steps = sorted(range(1, 16), key=lambda d: -min(d, 16 - d))
    return [device_at(x, y, moved(z, d, 16), core) for d in steps]


def across(place):
    _, _, x, y, z, core = place
    steps = [(a, b, c) for a in range(4) for b in range(4) for c in range(2) if a or b or c]
    steps.sort(key=lambda s: -(min(s[0], 4 - s[0]) + min(s[1], 4 - s[1])))
    return [device_at(moved(x, a, 4), moved(y, b, 4), z, moved(core, c, 2)) for a, b, c in steps]


def coarse_neighbours(place):
    _, _, x, y, z, core = place
    z_lo = lax.rem(z, 8)
    y_up = lax.rem(y + lax.div(z_lo + 1, 8), 4)
    y_down = lax.rem(y + 3 + lax.div(z_lo + 7, 8), 4)
    up = device_at(x, y_up, lax.rem(z + 1, 16), core)
    down = device_at(x, y_down, lax.rem(z + 15, 16), core)
    return up, down


def iota(shape, dim):
    return lax.broadcasted_iota(jnp.int32, shape, dim)


def split(value):
    high = value.astype(BF16)
    low = (value - high.astype(F32)).astype(BF16)
    return high, low


def dot(a, b, dims=((1,), (0,))):
    return lax.dot_general(a, b, (dims, ((), ())), preferred_element_type=F32)


def over_group(row):
    lane = iota(row.shape, 1)
    near = jnp.where((lane & 1) == 0, pltpu.roll(row, CH - 1, 1), pltpu.roll(row, 1, 1))
    row = row + near
    far = jnp.where((lane & 2) == 0, pltpu.roll(row, CH - 2, 1), pltpu.roll(row, 2, 1))
    return row + far


def local_stats(rows, cells):
    total = sum(jnp.sum(r, axis=0, keepdims=True) for r in rows)
    mean = over_group(total) * (1.0 / (cells * PER_GROUP))
    dev = sum(jnp.sum((r - mean) * (r - mean), axis=0, keepdims=True) for r in rows)
    return mean, over_group(dev)


def merge(mean, dev, others, cells):
    count = others.shape[0] + 1
    means = others[:, 0:1, :]
    whole = (mean + jnp.sum(means, axis=0)) * (1.0 / count)
    off = means - whole
    own = mean - whole
    spread = own * own + jnp.sum(off * off, axis=0)
    return whole, dev + jnp.sum(others[:, 1:2, :], axis=0) + (cells * PER_GROUP) * spread


LEFT, MAIN, RIGHT, WIDE = 8, 16, 144, 160


def kernel(
    src_ref, cnt_ref, coarse_ref, remap_ref, ca_ref, cb_ref, vec_ref,
    hb_ref, fin_ref,
    coarse_v, remap_v, ca_v, cb_v, vec_v,
    tt, crit_out, far_out, crit, far,
    sel, edges, wa32, wa, wb,
    xs, gs, ha, act, hb,
    stat, buf_x, buf_z,
    in_sem, out_sem, send_sem, recv_sem,
):
    place = coords()
    row, lon = place[0], place[1]
    z_mates = along_z(place)
    xy_mates = across(place)
    up, down = coarse_neighbours(place)
    row_up, row_down = lax.rem(row + 15, 16), lax.rem(row + 1, 16)
    lon_left, lon_right = lax.rem(lon + 31, 32), lax.rem(lon + 1, 32)
    halo = [
        (row_down, lon), (row_up, lon),
        (row, lon_right), (row, lon_left),
        (row_down, lon_right), (row_up, lon_right),
        (row_down, lon_left), (row_up, lon_left),
    ]
    barrier = pltpu.get_barrier_semaphore()
    partners = halo + [up, down] + z_mates + xy_mates
    for mate in partners:
        pl.semaphore_signal(barrier, inc=1, device_id=mate, device_id_type=MESH)

    loads = [
        pltpu.make_async_copy(coarse_ref, coarse_v, in_sem.at[0]),
        pltpu.make_async_copy(remap_ref, remap_v, in_sem.at[1]),
        pltpu.make_async_copy(ca_ref, ca_v, in_sem.at[2]),
        pltpu.make_async_copy(cb_ref, cb_v, in_sem.at[3]),
        pltpu.make_async_copy(vec_ref, vec_v, in_sem.at[4]),
    ]
    for load in loads:
        load.start()

    lane = iota((1, 128), 1)
    target = jnp.full((1, 128), -1, jnp.int32)
    for k in range(SLOTS):
        local = lax.rem(src_ref[0, k] - (lon - 1) * BLK_DEV + 2 * NBLK, NBLK)
        first = jnp.where(k < cnt_ref[0], local * BCELLS, -1024)
        target = jnp.where(lane // BCELLS == k, first + (lane & (BCELLS - 1)), target)
    sel[...] = jnp.where(iota((3 * 128, 128), 0) == target, 1.0, 0.0).astype(BF16)

    loads[0].wait()
    tile = jnp.zeros((VARS, 128), F32)
    for b in range(BLK_DEV):
        put = jnp.where(iota((BCELLS, 128), 0) + b * BCELLS == iota((BCELLS, 128), 1), 1.0, 0.0)
        tile = tile + dot(coarse_v[b], put.astype(BF16))
    pad = jnp.concatenate([tile, jnp.zeros((16 - VARS, 128), F32)], axis=0)
    tt[1] = pad.astype(BF16)

    loads[1].wait()
    ri = lane >> 3
    ci = lane & 7
    col = jnp.where(ci == 6, 126, jnp.where(ci == 7, 127, jnp.where(ci < 2, ci, -4096)))
    rw = jnp.where(ri < 2, ri + 6, jnp.where(ri < 10, ri - 2, jnp.where(ri < 12, ri - 10, -4096)))
    cell = rw * COLS_DEV + col
    pick = jnp.where(iota((1024, 128), 0) == cell, 1.0, 0.0).astype(BF16)
    edges[:, 512:640] = dot(remap_v[...], pick).astype(BF16)
    edges[:, 0:256] = remap_v[:, 0:256]
    edges[:, 256:512] = remap_v[:, 768:1024]

    pl.semaphore_wait(barrier, len(partners))

    for slot, mate in ((0, up), (2, down)):
        pltpu.make_async_remote_copy(
            src_ref=tt.at[1], dst_ref=tt.at[slot], send_sem=send_sem.at[0], recv_sem=recv_sem.at[0 if slot == 0 else 1],
            device_id=mate, device_id_type=MESH,
        ).start()
    middle = dot(tt[1], sel[128:256, :])

    loads[2].wait()
    wa32[...] = jnp.zeros_like(wa32)
    for dy in range(3):
        for part in range(3):
            first = (dy * 3 + part) * VARS
            for dx in range(3):
                wa32[first : first + VARS, dx * CH : (dx + 1) * CH] = ca_v[dy, dx]
    line = iota((128, 3 * CH), 0)
    twelfth = (line * 43) >> 9
    part_of = twelfth - 3 * ((twelfth * 11) >> 5)
    whole = wa32[...]
    high, low = split(whole)
    wa[...] = jnp.where(part_of == 2, low.astype(F32), high.astype(F32)).astype(BF16)

    twelfth_l = (lane * 43) >> 9
    var_l = jnp.where(lane < 9 * VARS, lane - 12 * twelfth_l, 4096)
    part_l = twelfth_l - 3 * ((twelfth_l * 11) >> 5)
    want = jnp.where(part_l == 1, var_l + 16, var_l)
    spread_msg = jnp.where(iota((32, 128), 0) == want, 1.0, 0.0).astype(BF16)
    spread_var = jnp.where(iota((16, 128), 0) == var_l, 1.0, 0.0).astype(BF16)

    for slot in (0, 2):
        pltpu.make_async_remote_copy(
            src_ref=tt.at[1], dst_ref=tt.at[slot], send_sem=send_sem.at[0], recv_sem=recv_sem.at[0 if slot == 0 else 1],
            device_id=up, device_id_type=MESH,
        ).wait_recv()
    blocks = middle + dot(tt[0], sel[0:128, :]) + dot(tt[2], sel[256:384, :])
    blocks = blocks.astype(BF16)

    fine_edges = dot(blocks, edges[...])
    high, low = split(fine_edges)
    for slot, first in ((0, 384), (1, 0), (2, 512)):
        crit_out[slot, 0:16, :] = high[:, first : first + 128]
        crit_out[slot, 16:32, :] = low[:, first : first + 128]
    for slot, first in ((0, 256), (1, 128)):
        far_out[slot, 0:16, :] = high[:, first : first + 128]
        far_out[slot, 16:32, :] = low[:, first : first + 128]
    for slot, mate in enumerate(halo):
        pltpu.make_async_remote_copy(
            src_ref=crit_out.at[min(slot, 2)], dst_ref=crit.at[slot], send_sem=send_sem.at[1], recv_sem=recv_sem.at[2],
            device_id=mate, device_id_type=MESH,
        ).start()
    for slot in range(2):
        pltpu.make_async_remote_copy(
            src_ref=far_out.at[slot], dst_ref=far.at[slot], send_sem=send_sem.at[2], recv_sem=recv_sem.at[3],
            device_id=halo[slot], device_id_type=MESH,
        ).start()

    spread_blocks = dot(blocks, spread_var, ((0,), (0,))).astype(BF16)
    fine = dot(remap_v[...], spread_blocks, ((0,), (0,)))
    high, low = split(fine)
    packed = jnp.where(part_l == 1, low.astype(F32), high.astype(F32)).astype(BF16)
    xs[2:10] = packed.reshape(ROWS_DEV, COLS_DEV, 128)

    third = jnp.broadcast_to(lane, (128, 128))

    def patches(before, here, after, lanes):
        before = jnp.where(lanes < 3 * VARS, before.astype(F32), 0.0)
        here = jnp.where((lanes >= 3 * VARS) & (lanes < 6 * VARS), here.astype(F32), 0.0)
        after = jnp.where(lanes >= 6 * VARS, after.astype(F32), 0.0)
        return (before + here + after).astype(BF16)

    def taps(out_rows):
        field = [patches(xs[i], xs[i + 1], xs[i + 2], third) for i in out_rows]
        result = dot(jnp.concatenate(field, axis=0), wa[...])
        for n, i in enumerate(out_rows):
            for dx in range(3):
                gs[dx, i, MAIN:RIGHT, :] = result[n * 128 : (n + 1) * 128, dx * CH : (dx + 1) * CH]

    def joined(i, first, size):
        return gs[0, i, first - 1 : first - 1 + size, :] + gs[1, i, first : first + size, :] + gs[2, i, first + 1 : first + 1 + size, :]

    taps(list(range(2, 8)))

    loads[3].wait()
    for dy in range(3):
        for dx in range(3):
            high, low = split(cb_v[dy, dx])
            span = slice(dx * CH, (dx + 1) * CH)
            wb[dy * 384 : dy * 384 + 128, span] = high
            wb[dy * 384 + 128 : dy * 384 + 256, span] = high
            wb[dy * 384 + 256 : dy * 384 + 384, span] = low
    loads[4].wait()

    not_first = jnp.where(row > 0, 1.0, 0.0).astype(F32)
    not_last = jnp.where(row < 15, 1.0, 0.0).astype(F32)
    pltpu.make_async_copy(crit, crit, recv_sem.at[2]).wait()
    top = crit[0].astype(F32) * not_first
    bottom = crit[1].astype(F32) * not_last
    left = jnp.where(
        ri < 2, crit[4].astype(F32) * not_first, jnp.where(ri < 10, crit[2].astype(F32), crit[5].astype(F32) * not_last)
    )
    right = jnp.where(
        ri < 2, crit[6].astype(F32) * not_first, jnp.where(ri < 10, crit[3].astype(F32), crit[7].astype(F32) * not_last)
    )
    sides = jnp.where(ci >= 4, left, right)
    around = jnp.concatenate([top, bottom, sides], axis=1).astype(BF16)
    placed = dot(around, spread_msg, ((0,), (0,))).astype(BF16)
    xs[1] = placed[0:128]
    xs[10] = placed[128:256]
    side = placed[256:352].astype(F32).reshape(12, 8, 128)
    side_lane = jnp.broadcast_to(lane.reshape(1, 1, 128), (10, 8, 128))
    side_patches = patches(side[0:10], side[1:11], side[2:12], side_lane).reshape(80, 128)
    side_taps = dot(side_patches, wa[...]).reshape(10, 8, 3 * CH)
    for dx in range(3):
        piece = side_taps[:, :, dx * CH : (dx + 1) * CH]
        gs[dx, :, LEFT:MAIN, :] = piece
        gs[dx, :, RIGHT : RIGHT + 8, :] = piece
    taps([1, 8])
    for i in range(1, 9):
        ha[i, MAIN:RIGHT, :] = joined(i, MAIN, 128)

    def all_reduce(turn, mean, dev, beside):
        cells = ROWS_DEV * COLS_DEV
        for stage, (mates, buf) in enumerate(((xy_mates, buf_x), (z_mates, buf_z))):
            sem = 4 + turn * 2 + stage
            stat[turn, stage, 0:1, :] = mean
            stat[turn, stage, 1:2, :] = dev
            for j, mate in enumerate(mates):
                pltpu.make_async_remote_copy(
                    src_ref=stat.at[turn, stage], dst_ref=buf.at[turn, j], send_sem=send_sem.at[sem - 1], recv_sem=recv_sem.at[sem],
                    device_id=mate, device_id_type=MESH,
                ).start()
            if stage == 0:
                beside()
            pltpu.make_async_copy(buf.at[turn], buf.at[turn], recv_sem.at[sem]).wait()
            mean, dev = merge(mean, dev, buf[turn], cells)
            cells = cells * (len(mates) + 1)
        return mean, lax.rsqrt(dev * (1.0 / (cells * PER_GROUP)) + eps)

    def around_a():
        pltpu.make_async_copy(far, far, recv_sem.at[3]).wait()
        beyond = jnp.concatenate([far[0].astype(F32) * not_first, far[1].astype(F32) * not_last], axis=1).astype(BF16)
        placed = dot(beyond, spread_msg, ((0,), (0,))).astype(BF16)
        xs[0] = placed[0:128]
        xs[11] = placed[128:256]
        taps([0, 9])
        for i in (0, 9):
            ha[i, MAIN:RIGHT, :] = joined(i, MAIN, 128)
        for i in range(10):
            ha[i, LEFT:MAIN, :] = joined(i, LEFT, 8)
            ha[i, RIGHT : RIGHT + 8, :] = joined(i, RIGHT, 8)

    mean, dev = local_stats([ha[i, MAIN:RIGHT, :] for i in range(1, 9)], ROWS_DEV * COLS_DEV)
    mean, inverse = all_reduce(0, mean, dev, around_a)

    scale = inverse * vec_v[0:1, :]
    shift = vec_v[1:2, :]
    for i in range(10):
        for first, size, at in ((MAIN, 128, 0), (LEFT, 16, 128)):
            if size == 128:
                value = ha[i, MAIN:RIGHT, :]
            else:
                value = jnp.concatenate([ha[i, RIGHT : RIGHT + 8, :], ha[i, LEFT:MAIN, :]], axis=0)
            normed = (value - mean) * scale + shift
            half = normed * 0.5
            value = half + half * jnp.tanh(half)
            if i == 0:
                value = value * not_first
            if i == 9:
                value = value * not_last
            high, low = split(value)
            act[i, at : at + size, 0:128] = high
            act[i, at : at + size, 128:256] = low
            act[i, at : at + size, 256:384] = high

    field = jnp.concatenate([act[0:8], act[1:9], act[2:10]], axis=2).reshape(8 * 144, 9 * CH)
    result = dot(field, wb[...]).reshape(8, 144, 3 * CH)
    for dx in range(3):
        span = slice(dx * CH, (dx + 1) * CH)
        gs[dx, 0:8, MAIN:RIGHT, :] = result[:, 0:128, span]
        gs[dx, 0:8, RIGHT : RIGHT + 8, :] = result[:, 128:136, span]
        gs[dx, 0:8, LEFT:MAIN, :] = result[:, 136:144, span]
    for i in range(8):
        hb[i] = joined(i, MAIN, 128)
    store = pltpu.make_async_copy(hb, hb_ref, out_sem)
    store.start()
    mean, dev = local_stats([hb[i] for i in range(8)], ROWS_DEV * COLS_DEV)
    mean, inverse = all_reduce(1, mean, dev, lambda: None)
    fin_ref[0:1, :] = mean
    fin_ref[1:2, :] = inverse * vec_v[2:3, :]
    store.wait()

    pltpu.make_async_copy(tt.at[pl.ds(0, 2)], tt.at[pl.ds(0, 2)], send_sem.at[0]).wait()
    pltpu.make_async_copy(crit, crit, send_sem.at[1]).wait()
    pltpu.make_async_copy(far, far, send_sem.at[2]).wait()
    for turn in range(2):
        pltpu.make_async_copy(buf_x.at[turn], buf_x.at[turn], send_sem.at[3 + 2 * turn]).wait()
        pltpu.make_async_copy(buf_z.at[turn], buf_z.at[turn], send_sem.at[4 + 2 * turn]).wait()


def per_device(
    coarse, src_blocks, slot_counts, remap_tiles, conv_a, conv_b, gain_a, shift_a, gain_b, shift_b
):
    anywhere = pl.BlockSpec(memory_space=pl.ANY)
    scalar = pl.BlockSpec(memory_space=pltpu.SMEM)
    vectors = jnp.stack([gain_a, shift_a, gain_b, shift_b])
    hidden, final = pl.pallas_call(
        kernel,
        name="stem",
        out_shape=(
            jax.ShapeDtypeStruct((ROWS_DEV, COLS_DEV, CH), F32),
            jax.ShapeDtypeStruct((2, CH), F32),
        ),
        in_specs=[scalar, scalar, anywhere, anywhere, anywhere, anywhere, anywhere],
        out_specs=(anywhere, pl.BlockSpec(memory_space=pltpu.VMEM)),
        scratch_shapes=[
            pltpu.VMEM((BLK_DEV, VARS, BCELLS), BF16),
            pltpu.VMEM((128, 1024), BF16),
            pltpu.VMEM((3, 3, VARS, CH), F32),
            pltpu.VMEM((3, 3, CH, CH), F32),
            pltpu.VMEM((4, CH), F32),
            pltpu.VMEM((3, 16, 128), BF16),
            pltpu.VMEM((3, 32, 128), BF16),
            pltpu.VMEM((2, 32, 128), BF16),
            pltpu.VMEM((8, 32, 128), BF16),
            pltpu.VMEM((2, 32, 128), BF16),
            pltpu.VMEM((384, 128), BF16),
            pltpu.VMEM((128, 640), BF16),
            pltpu.VMEM((128, 3 * CH), F32),
            pltpu.VMEM((128, 3 * CH), BF16),
            pltpu.VMEM((9 * CH, 3 * CH), BF16),
            pltpu.VMEM((12, COLS_DEV, 128), BF16),
            pltpu.VMEM((3, 10, WIDE, CH), F32),
            pltpu.VMEM((10, WIDE, CH), F32),
            pltpu.VMEM((10, 144, 3 * CH), BF16),
            pltpu.VMEM((ROWS_DEV, COLS_DEV, CH), F32),
            pltpu.VMEM((2, 2, 2, CH), F32),
            pltpu.VMEM((2, 31, 2, CH), F32),
            pltpu.VMEM((2, 15, 2, CH), F32),
            pltpu.SemaphoreType.DMA((5,)),
            pltpu.SemaphoreType.DMA,
            pltpu.SemaphoreType.DMA((7,)),
            pltpu.SemaphoreType.DMA((8,)),
        ],
        compiler_params=pltpu.CompilerParams(
            collective_id=0, has_side_effects=True, vmem_limit_bytes=40 * 1024 * 1024
        ),
    )(
        src_blocks, slot_counts, coarse, remap_tiles.reshape(SLOTS * BCELLS, 1024),
        conv_a, conv_b, vectors,
    )
    normed = (hidden - final[0]) * final[1] + shift_b
    return jax.nn.silu(normed).astype(BF16)


def solution(mesh):
    return jax.shard_map(
        per_device,
        mesh=mesh,
        in_specs=(
            P("lon", None, None),
            P(("row", "lon"), None),
            P(("row", "lon")),
            P(("row", "lon"), None, None, None),
            P(),
            P(),
            P(),
            P(),
            P(),
            P(),
        ),
        out_specs=P("row", "lon", None),
        check_vma=False,
    )
```

```python
import jax
import jax.numpy as jnp
from jax import lax
from jax.experimental import pallas as pl
from jax.experimental.pallas import tpu as pltpu
from jax.sharding import PartitionSpec as P

ROWS_DEV = 8
COLS_DEV = 128
VARS = 12
CH = 128
GROUPS = 32
SLOTS = 4
BCELLS = 32
BLK_DEV = 4
NBLK = 128
PER_GROUP = CH // GROUPS
MESH = pl.DeviceIdType.MESH
F32 = jnp.float32
BF16 = jnp.bfloat16

eps = 1e-05


def coords():
    row = lax.axis_index("row")
    lon = lax.axis_index("lon")
    core = lax.rem(row, 2)
    z_hi = lax.rem(lax.div(row, 2), 2)
    x = lax.div(row, 4)
    y = lax.div(lon, 8)
    z = z_hi * 8 + lax.rem(lon, 8)
    return row, lon, x, y, z, core


def device_at(x, y, z, core):
    return (x * 4 + lax.div(z, 8) * 2 + core, y * 8 + lax.rem(z, 8))


def moved(value, step, count):
    return lax.rem(value + step, count) if step else value


def along_z(place):
    _, _, x, y, z, core = place
    steps = [(d, c) for d in range(16) for c in range(2) if d or c]
    steps.sort(key=lambda s: -min(s[0], 16 - s[0]))
    return [device_at(x, y, moved(z, d, 16), moved(core, c, 2)) for d, c in steps]


def across(place):
    _, _, x, y, z, core = place
    steps = [(a, b) for a in range(4) for b in range(4) if a or b]
    steps.sort(key=lambda s: -(min(s[0], 4 - s[0]) + min(s[1], 4 - s[1])))
    return [device_at(moved(x, a, 4), moved(y, b, 4), z, core) for a, b in steps]


def coarse_neighbours(place):
    _, _, x, y, z, core = place
    z_lo = lax.rem(z, 8)
    y_up = lax.rem(y + lax.div(z_lo + 1, 8), 4)
    y_down = lax.rem(y + 3 + lax.div(z_lo + 7, 8), 4)
    up = device_at(x, y_up, lax.rem(z + 1, 16), core)
    down = device_at(x, y_down, lax.rem(z + 15, 16), core)
    return up, down


def iota(shape, dim):
    return lax.broadcasted_iota(jnp.int32, shape, dim)


def split(value):
    high = value.astype(BF16)
    low = (value - high.astype(F32)).astype(BF16)
    return high, low


def dot(a, b, dims=((1,), (0,))):
    return lax.dot_general(a, b, (dims, ((), ())), preferred_element_type=F32)


def over_group(row):
    lane = iota(row.shape, 1)
    near = jnp.where((lane & 1) == 0, pltpu.roll(row, CH - 1, 1), pltpu.roll(row, 1, 1))
    row = row + near
    far = jnp.where((lane & 2) == 0, pltpu.roll(row, CH - 2, 1), pltpu.roll(row, 2, 1))
    return row + far


def local_stats(rows, cells):
    total = sum(jnp.sum(r, axis=0, keepdims=True) for r in rows)
    mean = over_group(total) * (1.0 / (cells * PER_GROUP))
    dev = sum(jnp.sum((r - mean) * (r - mean), axis=0, keepdims=True) for r in rows)
    return mean, over_group(dev)


def merge(mean, dev, others, cells):
    count = others.shape[0] + 1
    means = others[:, 0:1, :]
    whole = (mean + jnp.sum(means, axis=0)) * (1.0 / count)
    off = means - whole
    own = mean - whole
    spread = own * own + jnp.sum(off * off, axis=0)
    return whole, dev + jnp.sum(others[:, 1:2, :], axis=0) + (cells * PER_GROUP) * spread


LEFT, MAIN, RIGHT, WIDE = 8, 16, 144, 160


def kernel(
    src_ref, cnt_ref, coarse_ref, remap_ref, ca_ref, cb_ref, gain_a_ref, shift_a_ref, gain_b_ref, shift_b_ref,
    hb_ref, fin_ref,
    coarse_v, remap_v, ca_v, cb_v, vec_v,
    tt, crit_out, far_out, crit, far,
    sel, edges, wa32, wa, wb,
    xs, gs, ha, act, hb,
    stat, buf_x, buf_z,
    in_sem, out_sem, send_sem, recv_sem,
):
    place = coords()
    row, lon = place[0], place[1]
    z_mates = along_z(place)
    xy_mates = across(place)
    up, down = coarse_neighbours(place)
    row_up, row_down = lax.rem(row + 15, 16), lax.rem(row + 1, 16)
    lon_left, lon_right = lax.rem(lon + 31, 32), lax.rem(lon + 1, 32)
    halo = [
        (row_down, lon), (row_up, lon),
        (row, lon_right), (row, lon_left),
        (row_down, lon_right), (row_up, lon_right),
        (row_down, lon_left), (row_up, lon_left),
    ]
    barrier = pltpu.get_barrier_semaphore()
    partners = halo + [up, down] + z_mates + xy_mates
    for mate in partners:
        pl.semaphore_signal(barrier, inc=1, device_id=mate, device_id_type=MESH)

    loads = [
        pltpu.make_async_copy(coarse_ref, coarse_v, in_sem.at[0]),
        pltpu.make_async_copy(remap_ref, remap_v, in_sem.at[1]),
        pltpu.make_async_copy(ca_ref, ca_v, in_sem.at[2]),
        pltpu.make_async_copy(cb_ref, cb_v, in_sem.at[3]),
    ]
    for i, ref in enumerate((gain_a_ref, shift_a_ref, gain_b_ref, shift_b_ref)):
        loads.append(pltpu.make_async_copy(ref, vec_v.at[i], in_sem.at[4 + i]))
    for load in loads:
        load.start()

    lane = iota((1, 128), 1)
    target = jnp.full((1, 128), -1, jnp.int32)
    for k in range(SLOTS):
        local = lax.rem(src_ref[0, k] - (lon - 1) * BLK_DEV + 2 * NBLK, NBLK)
        first = jnp.where(k < cnt_ref[0], local * BCELLS, -1024)
        target = jnp.where(lane // BCELLS == k, first + (lane & (BCELLS - 1)), target)
    sel[...] = jnp.where(iota((3 * 128, 128), 0) == target, 1.0, 0.0).astype(BF16)

    loads[0].wait()
    held = coarse_v[...].astype(F32)
    tile = jnp.zeros((VARS, 128), F32)
    for b in range(BLK_DEV):
        put = jnp.where(iota((BCELLS, 128), 0) + b * BCELLS == iota((BCELLS, 128), 1), 1.0, 0.0)
        tile = tile + dot(held[:, b, :].astype(BF16), put.astype(BF16))
    pad = jnp.concatenate([tile, jnp.zeros((16 - VARS, 128), F32)], axis=0)
    tt[1] = pad.astype(BF16)

    loads[1].wait()
    ri = lane >> 3
    ci = lane & 7
    col = jnp.where(ci == 6, 126, jnp.where(ci == 7, 127, jnp.where(ci < 2, ci, -4096)))
    rw = jnp.where(ri < 2, ri + 6, jnp.where(ri < 10, ri - 2, jnp.where(ri < 12, ri - 10, -4096)))
    cell = rw * COLS_DEV + col
    pick = jnp.where(iota((1024, 128), 0) == cell, 1.0, 0.0).astype(BF16)
    edges[:, 512:640] = dot(remap_v[...], pick).astype(BF16)
    edges[:, 0:256] = remap_v[:, 0:256]
    edges[:, 256:512] = remap_v[:, 768:1024]

    pl.semaphore_wait(barrier, len(partners))

    for slot, mate in ((0, up), (2, down)):
        pltpu.make_async_remote_copy(
            src_ref=tt.at[1], dst_ref=tt.at[slot], send_sem=send_sem.at[0], recv_sem=recv_sem.at[0 if slot == 0 else 1],
            device_id=mate, device_id_type=MESH,
        ).start()
    middle = dot(tt[1], sel[128:256, :])

    loads[2].wait()
    wa32[...] = jnp.zeros_like(wa32)
    for dy in range(3):
        for part in range(3):
            first = (dy * 3 + part) * VARS
            for dx in range(3):
                wa32[first : first + VARS, dx * CH : (dx + 1) * CH] = ca_v[dy, dx]
    line = iota((128, 3 * CH), 0)
    twelfth = (line * 43) >> 9
    part_of = twelfth - 3 * ((twelfth * 11) >> 5)
    whole = wa32[...]
    high, low = split(whole)
    wa[...] = jnp.where(part_of == 2, low.astype(F32), high.astype(F32)).astype(BF16)

    twelfth_l = (lane * 43) >> 9
    var_l = jnp.where(lane < 9 * VARS, lane - 12 * twelfth_l, 4096)
    part_l = twelfth_l - 3 * ((twelfth_l * 11) >> 5)
    want = jnp.where(part_l == 1, var_l + 16, var_l)
    spread_msg = jnp.where(iota((32, 128), 0) == want, 1.0, 0.0).astype(BF16)
    spread_var = jnp.where(iota((16, 128), 0) == var_l, 1.0, 0.0).astype(BF16)

    for slot in (0, 2):
        pltpu.make_async_remote_copy(
            src_ref=tt.at[1], dst_ref=tt.at[slot], send_sem=send_sem.at[0], recv_sem=recv_sem.at[0 if slot == 0 else 1],
            device_id=up, device_id_type=MESH,
        ).wait_recv()
    blocks = middle + dot(tt[0], sel[0:128, :]) + dot(tt[2], sel[256:384, :])
    blocks = blocks.astype(BF16)

    fine_edges = dot(blocks, edges[...])
    high, low = split(fine_edges)
    for slot, first in ((0, 384), (1, 0), (2, 512)):
        crit_out[slot, 0:16, :] = high[:, first : first + 128]
        crit_out[slot, 16:32, :] = low[:, first : first + 128]
    for slot, first in ((0, 256), (1, 128)):
        far_out[slot, 0:16, :] = high[:, first : first + 128]
        far_out[slot, 16:32, :] = low[:, first : first + 128]
    for slot, mate in enumerate(halo):
        pltpu.make_async_remote_copy(
            src_ref=crit_out.at[min(slot, 2)], dst_ref=crit.at[slot], send_sem=send_sem.at[1], recv_sem=recv_sem.at[2],
            device_id=mate, device_id_type=MESH,
        ).start()
    for slot in range(2):
        pltpu.make_async_remote_copy(
            src_ref=far_out.at[slot], dst_ref=far.at[slot], send_sem=send_sem.at[2], recv_sem=recv_sem.at[3],
            device_id=halo[slot], device_id_type=MESH,
        ).start()

    spread_blocks = dot(blocks, spread_var, ((0,), (0,))).astype(BF16)
    fine = dot(remap_v[...], spread_blocks, ((0,), (0,)))
    high, low = split(fine)
    packed = jnp.where(part_l == 1, low.astype(F32), high.astype(F32)).astype(BF16)
    xs[2:10] = packed.reshape(ROWS_DEV, COLS_DEV, 128)

    third = jnp.broadcast_to(lane, (128, 128))

    def patches(before, here, after, lanes):
        before = jnp.where(lanes < 3 * VARS, before.astype(F32), 0.0)
        here = jnp.where((lanes >= 3 * VARS) & (lanes < 6 * VARS), here.astype(F32), 0.0)
        after = jnp.where(lanes >= 6 * VARS, after.astype(F32), 0.0)
        return (before + here + after).astype(BF16)

    def taps(out_rows):
        field = [patches(xs[i], xs[i + 1], xs[i + 2], third) for i in out_rows]
        result = dot(jnp.concatenate(field, axis=0), wa[...])
        for n, i in enumerate(out_rows):
            for dx in range(3):
                gs[dx, i, MAIN:RIGHT, :] = result[n * 128 : (n + 1) * 128, dx * CH : (dx + 1) * CH]

    def joined(i, first, size):
        return gs[0, i, first - 1 : first - 1 + size, :] + gs[1, i, first : first + size, :] + gs[2, i, first + 1 : first + 1 + size, :]

    taps(list(range(2, 8)))

    loads[3].wait()
    for dy in range(3):
        for dx in range(3):
            high, low = split(cb_v[dy, dx])
            span = slice(dx * CH, (dx + 1) * CH)
            wb[dy * 384 : dy * 384 + 128, span] = high
            wb[dy * 384 + 128 : dy * 384 + 256, span] = high
            wb[dy * 384 + 256 : dy * 384 + 384, span] = low
    for load in loads[4:]:
        load.wait()

    not_first = jnp.where(row > 0, 1.0, 0.0).astype(F32)
    not_last = jnp.where(row < 15, 1.0, 0.0).astype(F32)
    pltpu.make_async_copy(crit, crit, recv_sem.at[2]).wait()
    top = crit[0].astype(F32) * not_first
    bottom = crit[1].astype(F32) * not_last
    left = jnp.where(
        ri < 2, crit[4].astype(F32) * not_first, jnp.where(ri < 10, crit[2].astype(F32), crit[5].astype(F32) * not_last)
    )
    right = jnp.where(
        ri < 2, crit[6].astype(F32) * not_first, jnp.where(ri < 10, crit[3].astype(F32), crit[7].astype(F32) * not_last)
    )
    sides = jnp.where(ci >= 4, left, right)
    around = jnp.concatenate([top, bottom, sides], axis=1).astype(BF16)
    placed = dot(around, spread_msg, ((0,), (0,))).astype(BF16)
    xs[1] = placed[0:128]
    xs[10] = placed[128:256]
    side = placed[256:352].astype(F32).reshape(12, 8, 128)
    side_lane = jnp.broadcast_to(lane.reshape(1, 1, 128), (10, 8, 128))
    side_patches = patches(side[0:10], side[1:11], side[2:12], side_lane).reshape(80, 128)
    side_taps = dot(side_patches, wa[...]).reshape(10, 8, 3 * CH)
    for dx in range(3):
        piece = side_taps[:, :, dx * CH : (dx + 1) * CH]
        gs[dx, :, LEFT:MAIN, :] = piece
        gs[dx, :, RIGHT : RIGHT + 8, :] = piece
    taps([1, 8])
    for i in range(1, 9):
        ha[i, MAIN:RIGHT, :] = joined(i, MAIN, 128)

    def all_reduce(turn, mean, dev, beside):
        cells = ROWS_DEV * COLS_DEV
        for stage, (mates, buf) in enumerate(((z_mates, buf_z), (xy_mates, buf_x))):
            sem = 4 + turn * 2 + stage
            stat[turn, stage, 0:1, :] = mean
            stat[turn, stage, 1:2, :] = dev
            for j, mate in enumerate(mates):
                pltpu.make_async_remote_copy(
                    src_ref=stat.at[turn, stage], dst_ref=buf.at[turn, j], send_sem=send_sem.at[sem - 1], recv_sem=recv_sem.at[sem],
                    device_id=mate, device_id_type=MESH,
                ).start()
            if stage == 0:
                beside()
            pltpu.make_async_copy(buf.at[turn], buf.at[turn], recv_sem.at[sem]).wait()
            mean, dev = merge(mean, dev, buf[turn], cells)
            cells = cells * (len(mates) + 1)
        return mean, lax.rsqrt(dev * (1.0 / (cells * PER_GROUP)) + eps)

    def around_a():
        pltpu.make_async_copy(far, far, recv_sem.at[3]).wait()
        beyond = jnp.concatenate([far[0].astype(F32) * not_first, far[1].astype(F32) * not_last], axis=1).astype(BF16)
        placed = dot(beyond, spread_msg, ((0,), (0,))).astype(BF16)
        xs[0] = placed[0:128]
        xs[11] = placed[128:256]
        taps([0, 9])
        for i in (0, 9):
            ha[i, MAIN:RIGHT, :] = joined(i, MAIN, 128)
        for i in range(10):
            ha[i, LEFT:MAIN, :] = joined(i, LEFT, 8)
            ha[i, RIGHT : RIGHT + 8, :] = joined(i, RIGHT, 8)

    mean, dev = local_stats([ha[i, MAIN:RIGHT, :] for i in range(1, 9)], ROWS_DEV * COLS_DEV)
    mean, inverse = all_reduce(0, mean, dev, around_a)

    scale = inverse * vec_v[0]
    shift = vec_v[1]
    for i in range(10):
        for first, size, at in ((MAIN, 128, 0), (LEFT, 16, 128)):
            if size == 128:
                value = ha[i, MAIN:RIGHT, :]
            else:
                value = jnp.concatenate([ha[i, RIGHT : RIGHT + 8, :], ha[i, LEFT:MAIN, :]], axis=0)
            normed = (value - mean) * scale + shift
            half = normed * 0.5
            value = half + half * jnp.tanh(half)
            if i == 0:
                value = value * not_first
            if i == 9:
                value = value * not_last
            high, low = split(value)
            act[i, at : at + size, 0:128] = high
            act[i, at : at + size, 128:256] = low
            act[i, at : at + size, 256:384] = high

    field = jnp.concatenate([act[0:8], act[1:9], act[2:10]], axis=2).reshape(8 * 144, 9 * CH)
    result = dot(field, wb[...]).reshape(8, 144, 3 * CH)
    for dx in range(3):
        span = slice(dx * CH, (dx + 1) * CH)
        gs[dx, 0:8, MAIN:RIGHT, :] = result[:, 0:128, span]
        gs[dx, 0:8, RIGHT : RIGHT + 8, :] = result[:, 128:136, span]
        gs[dx, 0:8, LEFT:MAIN, :] = result[:, 136:144, span]
    for i in range(8):
        hb[i] = joined(i, MAIN, 128)
    store = pltpu.make_async_copy(hb, hb_ref, out_sem)
    store.start()
    mean, dev = local_stats([hb[i] for i in range(8)], ROWS_DEV * COLS_DEV)
    mean, inverse = all_reduce(1, mean, dev, lambda: None)
    fin_ref[0:1, :] = mean
    fin_ref[1:2, :] = inverse * vec_v[2]
    fin_ref[2:3, :] = vec_v[3]
    store.wait()

    pltpu.make_async_copy(tt.at[pl.ds(0, 2)], tt.at[pl.ds(0, 2)], send_sem.at[0]).wait()
    pltpu.make_async_copy(crit, crit, send_sem.at[1]).wait()
    pltpu.make_async_copy(far, far, send_sem.at[2]).wait()
    for turn in range(2):
        pltpu.make_async_copy(buf_z.at[turn], buf_z.at[turn], send_sem.at[3 + 2 * turn]).wait()
        pltpu.make_async_copy(buf_x.at[turn], buf_x.at[turn], send_sem.at[4 + 2 * turn]).wait()


def per_device(
    coarse, src_blocks, slot_counts, remap_tiles, conv_a, conv_b, gain_a, shift_a, gain_b, shift_b
):
    anywhere = pl.BlockSpec(memory_space=pl.ANY)
    scalar = pl.BlockSpec(memory_space=pltpu.SMEM)
    vectors = [v.reshape(1, CH) for v in (gain_a, shift_a, gain_b, shift_b)]
    hidden, final = pl.pallas_call(
        kernel,
        name="stem",
        out_shape=(
            pltpu.VMEM((ROWS_DEV, COLS_DEV, CH), F32),
            pltpu.VMEM((3, CH), F32),
        ),
        in_specs=[scalar, scalar] + [anywhere] * 8,
        out_specs=(anywhere, pl.BlockSpec(memory_space=pltpu.VMEM)),
        scratch_shapes=[
            pltpu.VMEM((VARS, BLK_DEV, BCELLS), BF16),
            pltpu.VMEM((128, 1024), BF16),
            pltpu.VMEM((3, 3, VARS, CH), F32),
            pltpu.VMEM((3, 3, CH, CH), F32),
            pltpu.VMEM((4, 1, CH), F32),
            pltpu.VMEM((3, 16, 128), BF16),
            pltpu.VMEM((3, 32, 128), BF16),
            pltpu.VMEM((2, 32, 128), BF16),
            pltpu.VMEM((8, 32, 128), BF16),
            pltpu.VMEM((2, 32, 128), BF16),
            pltpu.VMEM((384, 128), BF16),
            pltpu.VMEM((128, 640), BF16),
            pltpu.VMEM((128, 3 * CH), F32),
            pltpu.VMEM((128, 3 * CH), BF16),
            pltpu.VMEM((9 * CH, 3 * CH), BF16),
            pltpu.VMEM((12, COLS_DEV, 128), BF16),
            pltpu.VMEM((3, 10, WIDE, CH), F32),
            pltpu.VMEM((10, WIDE, CH), F32),
            pltpu.VMEM((10, 144, 3 * CH), BF16),
            pltpu.VMEM((ROWS_DEV, COLS_DEV, CH), F32),
            pltpu.VMEM((2, 2, 2, CH), F32),
            pltpu.VMEM((2, 15, 2, CH), F32),
            pltpu.VMEM((2, 31, 2, CH), F32),
            pltpu.SemaphoreType.DMA((8,)),
            pltpu.SemaphoreType.DMA,
            pltpu.SemaphoreType.DMA((7,)),
            pltpu.SemaphoreType.DMA((8,)),
        ],
        compiler_params=pltpu.CompilerParams(
            collective_id=0, has_side_effects=True, vmem_limit_bytes=60 * 1024 * 1024
        ),
    )(
        src_blocks, slot_counts, jnp.transpose(coarse, (1, 0, 2)), remap_tiles.reshape(SLOTS * BCELLS, 1024),
        conv_a, conv_b, *vectors,
    )
    normed = (hidden - final[0]) * final[1] + final[2]
    return jax.nn.silu(normed).astype(BF16)


def solution(mesh):
    return jax.shard_map(
        per_device,
        mesh=mesh,
        in_specs=(
            P("lon", None, None),
            P(("row", "lon"), None),
            P(("row", "lon")),
            P(("row", "lon"), None, None, None),
            P(),
            P(),
            P(),
            P(),
            P(),
            P(),
        ),
        out_specs=P("row", "lon", None),
        check_vma=False,
    )
```

```python
import jax
import jax.numpy as jnp
from jax import lax
from jax.experimental import pallas as pl
from jax.experimental.pallas import tpu as pltpu
from jax.sharding import PartitionSpec as P

ROWS_DEV = 8
COLS_DEV = 128
VARS = 12
CH = 128
GROUPS = 32
SLOTS = 4
BCELLS = 32
BLK_DEV = 4
NBLK = 128
PER_GROUP = CH // GROUPS
MESH = pl.DeviceIdType.MESH
F32 = jnp.float32
BF16 = jnp.bfloat16

eps = 1e-05


def coords():
    row = lax.axis_index("row")
    lon = lax.axis_index("lon")
    core = lax.rem(row, 2)
    z_hi = lax.rem(lax.div(row, 2), 2)
    x = lax.div(row, 4)
    y = lax.div(lon, 8)
    z = z_hi * 8 + lax.rem(lon, 8)
    return row, lon, x, y, z, core


def device_at(x, y, z, core):
    return (x * 4 + lax.div(z, 8) * 2 + core, y * 8 + lax.rem(z, 8))


def moved(value, step, count):
    return lax.rem(value + step, count) if step else value


def along_z(place):
    _, _, x, y, z, core = place
    steps = [(d, c) for d in range(16) for c in range(2) if d or c]
    steps.sort(key=lambda s: -min(s[0], 16 - s[0]))
    return [device_at(x, y, moved(z, d, 16), moved(core, c, 2)) for d, c in steps]


def across(place):
    _, _, x, y, z, core = place
    steps = [(a, b) for a in range(4) for b in range(4) if a or b]
    steps.sort(key=lambda s: -(min(s[0], 4 - s[0]) + min(s[1], 4 - s[1])))
    return [device_at(moved(x, a, 4), moved(y, b, 4), z, core) for a, b in steps]


def coarse_mates(place):
    _, _, x, y, z, core = place
    z_lo = lax.rem(z, 8)
    mates = []
    for step in (2, 1, -1, -2):
        turn = lax.rem(y + 3 + lax.div(z_lo + 8 + step, 8), 4)
        mates.append(device_at(x, turn, lax.rem(z + 16 + step, 16), core))
    return mates


def iota(shape, dim):
    return lax.broadcasted_iota(jnp.int32, shape, dim)


def split(value):
    high = value.astype(BF16)
    low = (value - high.astype(F32)).astype(BF16)
    return high, low


def dot(a, b, dims=((1,), (0,))):
    return lax.dot_general(a, b, (dims, ((), ())), preferred_element_type=F32)


def over_group(row):
    lane = iota(row.shape, 1)
    near = jnp.where((lane & 1) == 0, pltpu.roll(row, CH - 1, 1), pltpu.roll(row, 1, 1))
    row = row + near
    far = jnp.where((lane & 2) == 0, pltpu.roll(row, CH - 2, 1), pltpu.roll(row, 2, 1))
    return row + far


def local_stats(rows, cells):
    total = sum(jnp.sum(r, axis=0, keepdims=True) for r in rows)
    mean = over_group(total) * (1.0 / (cells * PER_GROUP))
    dev = sum(jnp.sum((r - mean) * (r - mean), axis=0, keepdims=True) for r in rows)
    return mean, over_group(dev)


def merge(mean, dev, others, cells):
    count = others.shape[0] + 1
    means = others[:, 0:1, :]
    whole = (mean + jnp.sum(means, axis=0)) * (1.0 / count)
    off = means - whole
    own = mean - whole
    spread = own * own + jnp.sum(off * off, axis=0)
    return whole, dev + jnp.sum(others[:, 1:2, :], axis=0) + (cells * PER_GROUP) * spread


LEFT, MAIN, RIGHT, WIDE = 8, 16, 144, 160


def kernel(
    src_ref, cnt_ref, coarse_ref, remap_ref, ca_ref, cb_ref, gain_a_ref, shift_a_ref, gain_b_ref, shift_b_ref,
    hb_ref, fin_ref,
    coarse_v, remap_v, ca_v, cb_v, vec_v,
    tt, near_out, corner_out, far_out, near, corner, far,
    copies, choices, wa32, wa, wb,
    xs, gs, ha, act, hb,
    stat, buf_x, buf_z,
    in_sem, out_sem, send_sem, recv_sem,
):
    place = coords()
    row, lon = place[0], place[1]
    z_mates = along_z(place)
    xy_mates = across(place)
    lon_mates = coarse_mates(place)
    row_up, row_down = lax.rem(row + 15, 16), lax.rem(row + 1, 16)
    lon_left, lon_right = lax.rem(lon + 31, 32), lax.rem(lon + 1, 32)
    halo = [
        (row_down, lon), (row_up, lon),
        (row, lon_right), (row, lon_left),
        (row_down, lon_right), (row_up, lon_right),
        (row_down, lon_left), (row_up, lon_left),
    ]
    barrier = pltpu.get_barrier_semaphore()
    partners = halo + lon_mates + z_mates + xy_mates
    for mate in partners:
        pl.semaphore_signal(barrier, inc=1, device_id=mate, device_id_type=MESH)

    loads = [
        pltpu.make_async_copy(coarse_ref, coarse_v, in_sem.at[0]),
        pltpu.make_async_copy(remap_ref, remap_v, in_sem.at[1]),
        pltpu.make_async_copy(ca_ref, ca_v, in_sem.at[2]),
        pltpu.make_async_copy(cb_ref, cb_v, in_sem.at[3]),
    ]
    for i, ref in enumerate((gain_a_ref, shift_a_ref, gain_b_ref, shift_b_ref)):
        loads.append(pltpu.make_async_copy(ref, vec_v.at[i], in_sem.at[4 + i]))
    for load in loads:
        load.start()

    lane = iota((1, 128), 1)
    own_choice = jnp.zeros((1, 128), F32)
    for k in range(SLOTS):
        local = lax.rem(src_ref[0, k] - (lon - 1) * BLK_DEV + 2 * NBLK, NBLK)
        local = jnp.where(k < cnt_ref[0], local, -64)
        own_choice = jnp.where((lane >> 5) == k, local.astype(F32), own_choice)
    choice_tile = jnp.broadcast_to(own_choice, (16, 128)).astype(BF16)

    for q in range(BLK_DEV):
        want = q * BCELLS + (lane & (BCELLS - 1))
        copies[:, q * 128 : (q + 1) * 128] = jnp.where(iota((128, 128), 0) == want, 1.0, 0.0).astype(BF16)

    loads[0].wait()
    held = coarse_v[...].astype(F32)
    tile = jnp.zeros((VARS, 128), F32)
    for b in range(BLK_DEV):
        put = jnp.where(iota((BCELLS, 128), 0) + b * BCELLS == iota((BCELLS, 128), 1), 1.0, 0.0)
        tile = tile + dot(held[:, b, :].astype(BF16), put.astype(BF16))
    pad = jnp.concatenate([tile, jnp.zeros((16 - VARS, 128), F32)], axis=0)
    tt[2] = pad.astype(BF16)

    loads[1].wait()
    near_out[0, 0:128, :] = remap_v[:, 896:1024]
    near_out[1, 0:128, :] = remap_v[:, 0:128]
    ri = lane >> 3
    ci = lane & 7
    col = jnp.where(ci == 6, 126, jnp.where(ci == 7, 127, jnp.where(ci < 2, ci, -4096)))
    rw = jnp.where((ri >= 2) & (ri < 10), ri - 2, -4096)
    cell = rw * COLS_DEV + col
    pick = jnp.where(iota((1024, 128), 0) == cell, 1.0, 0.0).astype(BF16)
    near_out[2, 0:128, :] = dot(remap_v[...], pick).astype(BF16)
    for i in range(3):
        near_out[i, 128:144, :] = choice_tile
    for i, (row0, col0) in enumerate(((6, 126), (0, 126), (6, 0), (0, 0))):
        at = iota((16, 1024), 0)
        cell = (row0 + (at >> 1)) * COLS_DEV + col0 + (at & 1)
        pick = jnp.where((iota((16, 1024), 1) == cell) & (at < 4), 1.0, 0.0).astype(BF16)
        cells = dot(pick, remap_v[...], ((1,), (1,)))
        corner_out[i] = jnp.where(iota((16, 128), 0) < 8, cells, own_choice).astype(BF16)

    loads[2].wait()
    wa32[...] = jnp.zeros_like(wa32)
    for dy in range(3):
        for part in range(3):
            first = (dy * 3 + part) * VARS
            for dx in range(3):
                wa32[first : first + VARS, dx * CH : (dx + 1) * CH] = ca_v[dy, dx]
    line = iota((128, 3 * CH), 0)
    twelfth = (line * 43) >> 9
    part_of = twelfth - 3 * ((twelfth * 11) >> 5)
    whole = wa32[...]
    high, low = split(whole)
    wa[...] = jnp.where(part_of == 2, low.astype(F32), high.astype(F32)).astype(BF16)

    twelfth_l = (lane * 43) >> 9
    var_l = jnp.where(lane < 9 * VARS, lane - 12 * twelfth_l, 4096)
    part_l = twelfth_l - 3 * ((twelfth_l * 11) >> 5)
    want = jnp.where(part_l == 1, var_l + 16, var_l)
    spread_msg = jnp.where(iota((32, 128), 0) == want, 1.0, 0.0).astype(BF16)
    spread_var = jnp.where(iota((16, 128), 0) == var_l, 1.0, 0.0).astype(BF16)
    not_first = jnp.where(row > 0, 1.0, 0.0).astype(F32)
    not_last = jnp.where(row < 15, 1.0, 0.0).astype(F32)

    pl.semaphore_wait(barrier, len(partners))

    for slot in (0, 1):
        pltpu.make_async_remote_copy(
            src_ref=near_out.at[slot], dst_ref=near.at[slot], send_sem=send_sem.at[0], recv_sem=recv_sem.at[0],
            device_id=halo[slot], device_id_type=MESH,
        ).start()
    for slot in range(4):
        pltpu.make_async_remote_copy(
            src_ref=corner_out.at[slot], dst_ref=corner.at[slot], send_sem=send_sem.at[1], recv_sem=recv_sem.at[1],
            device_id=halo[4 + slot], device_id_type=MESH,
        ).start()
    for slot in (2, 3):
        pltpu.make_async_remote_copy(
            src_ref=near_out.at[2], dst_ref=near.at[slot], send_sem=send_sem.at[0], recv_sem=recv_sem.at[0],
            device_id=halo[slot], device_id_type=MESH,
        ).start()
    along_lon = [
        pltpu.make_async_remote_copy(
            src_ref=tt.at[2], dst_ref=tt.at[slot], send_sem=send_sem.at[7], recv_sem=recv_sem.at[8 + i],
            device_id=mate, device_id_type=MESH,
        )
        for i, (slot, mate) in enumerate(zip((0, 1, 3, 4), lon_mates))
    ]
    for copy in along_lon:
        copy.start()

    loads[3].wait()
    for dy in range(3):
        for dx in range(3):
            high, low = split(cb_v[dy, dx])
            span = slice(dx * CH, (dx + 1) * CH)
            wb[dy * 384 : dy * 384 + 128, span] = high
            wb[dy * 384 + 128 : dy * 384 + 256, span] = high
            wb[dy * 384 + 256 : dy * 384 + 384, span] = low
    for load in loads[4:]:
        load.wait()

    for copy in along_lon:
        copy.wait_recv()
    choices[...] = dot(tt[...].reshape(80, 128), copies[...])

    def chosen(choice, first_tile):
        total = jnp.zeros((16, 128), F32)
        for j in range(3 * BLK_DEV):
            t, q = first_tile + j // BLK_DEV, j % BLK_DEV
            total = jnp.where(choice == j, choices[t * 16 : t * 16 + 16, q * 128 : (q + 1) * 128], total)
        return total

    blocks = chosen(own_choice, 1).astype(BF16)

    for slot, first in ((0, 768), (1, 128)):
        high, low = split(dot(blocks, remap_v[:, first : first + 128]))
        far_out[slot, 0:16, :] = high
        far_out[slot, 16:32, :] = low
        pltpu.make_async_remote_copy(
            src_ref=far_out.at[slot], dst_ref=far.at[slot], send_sem=send_sem.at[2], recv_sem=recv_sem.at[3],
            device_id=halo[slot], device_id_type=MESH,
        ).start()

    spread_blocks = dot(blocks, spread_var, ((0,), (0,))).astype(BF16)
    fine = dot(remap_v[...], spread_blocks, ((0,), (0,)))
    high, low = split(fine)
    packed = jnp.where(part_l == 1, low.astype(F32), high.astype(F32)).astype(BF16)
    xs[2:10] = packed.reshape(ROWS_DEV, COLS_DEV, 128)

    third = jnp.broadcast_to(lane, (128, 128))

    def patches(before, here, after, lanes):
        before = jnp.where(lanes < 3 * VARS, before.astype(F32), 0.0)
        here = jnp.where((lanes >= 3 * VARS) & (lanes < 6 * VARS), here.astype(F32), 0.0)
        after = jnp.where(lanes >= 6 * VARS, after.astype(F32), 0.0)
        return (before + here + after).astype(BF16)

    def taps(out_rows):
        field = [patches(xs[i], xs[i + 1], xs[i + 2], third) for i in out_rows]
        result = dot(jnp.concatenate(field, axis=0), wa[...])
        for n, i in enumerate(out_rows):
            for dx in range(3):
                gs[dx, i, MAIN:RIGHT, :] = result[n * 128 : (n + 1) * 128, dx * CH : (dx + 1) * CH]

    def joined(i, first, size):
        return gs[0, i, first - 1 : first - 1 + size, :] + gs[1, i, first : first + size, :] + gs[2, i, first + 1 : first + 1 + size, :]

    taps(list(range(2, 8)))

    pltpu.make_async_copy(corner, corner, recv_sem.at[1]).wait()
    pltpu.make_async_copy(near, near, recv_sem.at[0]).wait()

    def near_fine(slot, first_tile):
        held = chosen(near[slot, 128:129, :].astype(F32), first_tile)
        return dot(held.astype(BF16), near[slot, 0:128, :])

    top = near_fine(0, 1) * not_first
    bottom = near_fine(1, 1) * not_last
    sides = jnp.where(ci >= 4, near_fine(2, 0), near_fine(3, 2))
    for slot, first_tile, known, first_lane in (
        (0, 0, not_first, 6), (1, 0, not_last, 86), (2, 2, not_first, 0), (3, 2, not_last, 80),
    ):
        tile = corner[slot].astype(F32)
        held = chosen(tile[8:9, :], first_tile) * known
        for n in range(4):
            value = jnp.sum(held * tile[n : n + 1, :], axis=1, keepdims=True)
            sides = jnp.where(lane == first_lane + (n >> 1) * 8 + (n & 1), value, sides)
    high, low = split(jnp.concatenate([top, bottom, sides], axis=1))
    around = jnp.concatenate([high, low], axis=0)
    placed = dot(around, spread_msg, ((0,), (0,))).astype(BF16)
    xs[1] = placed[0:128]
    xs[10] = placed[128:256]
    side = placed[256:352].astype(F32).reshape(12, 8, 128)
    side_lane = jnp.broadcast_to(lane.reshape(1, 1, 128), (10, 8, 128))
    side_patches = patches(side[0:10], side[1:11], side[2:12], side_lane).reshape(80, 128)
    side_taps = dot(side_patches, wa[...]).reshape(10, 8, 3 * CH)
    for dx in range(3):
        piece = side_taps[:, :, dx * CH : (dx + 1) * CH]
        gs[dx, :, LEFT:MAIN, :] = piece
        gs[dx, :, RIGHT : RIGHT + 8, :] = piece
    taps([1, 8])
    for i in range(1, 9):
        ha[i, MAIN:RIGHT, :] = joined(i, MAIN, 128)

    def all_reduce(turn, mean, dev, beside):
        cells = ROWS_DEV * COLS_DEV
        for stage, (mates, buf) in enumerate(((z_mates, buf_z), (xy_mates, buf_x))):
            sem = 4 + turn * 2 + stage
            stat[turn, stage, 0:1, :] = mean
            stat[turn, stage, 1:2, :] = dev
            for j, mate in enumerate(mates):
                pltpu.make_async_remote_copy(
                    src_ref=stat.at[turn, stage], dst_ref=buf.at[turn, j], send_sem=send_sem.at[sem - 1], recv_sem=recv_sem.at[sem],
                    device_id=mate, device_id_type=MESH,
                ).start()
            if stage == 0:
                beside()
            pltpu.make_async_copy(buf.at[turn], buf.at[turn], recv_sem.at[sem]).wait()
            mean, dev = merge(mean, dev, buf[turn], cells)
            cells = cells * (len(mates) + 1)
        return mean, lax.rsqrt(dev * (1.0 / (cells * PER_GROUP)) + eps)

    def around_a():
        pltpu.make_async_copy(far, far, recv_sem.at[3]).wait()
        beyond = jnp.concatenate([far[0].astype(F32) * not_first, far[1].astype(F32) * not_last], axis=1).astype(BF16)
        placed = dot(beyond, spread_msg, ((0,), (0,))).astype(BF16)
        xs[0] = placed[0:128]
        xs[11] = placed[128:256]
        taps([0, 9])
        for i in (0, 9):
            ha[i, MAIN:RIGHT, :] = joined(i, MAIN, 128)
        for i in range(10):
            ha[i, LEFT:MAIN, :] = joined(i, LEFT, 8)
            ha[i, RIGHT : RIGHT + 8, :] = joined(i, RIGHT, 8)

    mean, dev = local_stats([ha[i, MAIN:RIGHT, :] for i in range(1, 9)], ROWS_DEV * COLS_DEV)
    mean, inverse = all_reduce(0, mean, dev, around_a)

    scale = inverse * vec_v[0]
    shift = vec_v[1]
    for i in range(10):
        for first, size, at in ((MAIN, 128, 0), (LEFT, 16, 128)):
            if size == 128:
                value = ha[i, MAIN:RIGHT, :]
            else:
                value = jnp.concatenate([ha[i, RIGHT : RIGHT + 8, :], ha[i, LEFT:MAIN, :]], axis=0)
            normed = (value - mean) * scale + shift
            half = normed * 0.5
            value = half + half * jnp.tanh(half)
            if i == 0:
                value = value * not_first
            if i == 9:
                value = value * not_last
            high, low = split(value)
            act[i, at : at + size, 0:128] = high
            act[i, at : at + size, 128:256] = low
            act[i, at : at + size, 256:384] = high

    field = jnp.concatenate([act[0:8], act[1:9], act[2:10]], axis=2).reshape(8 * 144, 9 * CH)
    result = dot(field, wb[...]).reshape(8, 144, 3 * CH)
    for dx in range(3):
        span = slice(dx * CH, (dx + 1) * CH)
        gs[dx, 0:8, MAIN:RIGHT, :] = result[:, 0:128, span]
        gs[dx, 0:8, RIGHT : RIGHT + 8, :] = result[:, 128:136, span]
        gs[dx, 0:8, LEFT:MAIN, :] = result[:, 136:144, span]
    for i in range(8):
        hb[i] = joined(i, MAIN, 128)
    store = pltpu.make_async_copy(hb, hb_ref, out_sem)
    store.start()
    mean, dev = local_stats([hb[i] for i in range(8)], ROWS_DEV * COLS_DEV)
    mean, inverse = all_reduce(1, mean, dev, lambda: None)
    fin_ref[0:1, :] = mean
    fin_ref[1:2, :] = inverse * vec_v[2]
    fin_ref[2:3, :] = vec_v[3]
    store.wait()

    pltpu.make_async_copy(near, near, send_sem.at[0]).wait()
    pltpu.make_async_copy(corner, corner, send_sem.at[1]).wait()
    pltpu.make_async_copy(tt.at[pl.ds(0, 4)], tt.at[pl.ds(0, 4)], send_sem.at[7]).wait()
    pltpu.make_async_copy(far, far, send_sem.at[2]).wait()
    for turn in range(2):
        pltpu.make_async_copy(buf_z.at[turn], buf_z.at[turn], send_sem.at[3 + 2 * turn]).wait()
        pltpu.make_async_copy(buf_x.at[turn], buf_x.at[turn], send_sem.at[4 + 2 * turn]).wait()


def per_device(
    coarse, src_blocks, slot_counts, remap_tiles, conv_a, conv_b, gain_a, shift_a, gain_b, shift_b
):
    anywhere = pl.BlockSpec(memory_space=pl.ANY)
    scalar = pl.BlockSpec(memory_space=pltpu.SMEM)
    vectors = [v.reshape(1, CH) for v in (gain_a, shift_a, gain_b, shift_b)]
    hidden, final = pl.pallas_call(
        kernel,
        name="stem",
        out_shape=(
            pltpu.VMEM((ROWS_DEV, COLS_DEV, CH), F32),
            pltpu.VMEM((3, CH), F32),
        ),
        in_specs=[scalar, scalar] + [anywhere] * 8,
        out_specs=(anywhere, pl.BlockSpec(memory_space=pltpu.VMEM)),
        scratch_shapes=[
            pltpu.VMEM((VARS, BLK_DEV, BCELLS), BF16),
            pltpu.VMEM((128, 1024), BF16),
            pltpu.VMEM((3, 3, VARS, CH), F32),
            pltpu.VMEM((3, 3, CH, CH), F32),
            pltpu.VMEM((4, 1, CH), F32),
            pltpu.VMEM((5, 16, 128), BF16),
            pltpu.VMEM((3, 144, 128), BF16),
            pltpu.VMEM((4, 16, 128), BF16),
            pltpu.VMEM((2, 32, 128), BF16),
            pltpu.VMEM((4, 144, 128), BF16),
            pltpu.VMEM((4, 16, 128), BF16),
            pltpu.VMEM((2, 32, 128), BF16),
            pltpu.VMEM((128, BLK_DEV * 128), BF16),
            pltpu.VMEM((80, BLK_DEV * 128), F32),
            pltpu.VMEM((128, 3 * CH), F32),
            pltpu.VMEM((128, 3 * CH), BF16),
            pltpu.VMEM((9 * CH, 3 * CH), BF16),
            pltpu.VMEM((12, COLS_DEV, 128), BF16),
            pltpu.VMEM((3, 10, WIDE, CH), F32),
            pltpu.VMEM((10, WIDE, CH), F32),
            pltpu.VMEM((10, 144, 3 * CH), BF16),
            pltpu.VMEM((ROWS_DEV, COLS_DEV, CH), F32),
            pltpu.VMEM((2, 2, 2, CH), F32),
            pltpu.VMEM((2, 15, 2, CH), F32),
            pltpu.VMEM((2, 31, 2, CH), F32),
            pltpu.SemaphoreType.DMA((8,)),
            pltpu.SemaphoreType.DMA,
            pltpu.SemaphoreType.DMA((8,)),
            pltpu.SemaphoreType.DMA((12,)),
        ],
        compiler_params=pltpu.CompilerParams(
            collective_id=0, has_side_effects=True, vmem_limit_bytes=60 * 1024 * 1024
        ),
    )(
        src_blocks, slot_counts, jnp.transpose(coarse, (1, 0, 2)), remap_tiles.reshape(SLOTS * BCELLS, 1024),
        conv_a, conv_b, *vectors,
    )
    normed = (hidden - final[0]) * final[1] + final[2]
    return jax.nn.silu(normed).astype(BF16)


def solution(mesh):
    return jax.shard_map(
        per_device,
        mesh=mesh,
        in_specs=(
            P("lon", None, None),
            P(("row", "lon"), None),
            P(("row", "lon")),
            P(("row", "lon"), None, None, None),
            P(),
            P(),
            P(),
            P(),
            P(),
            P(),
        ),
        out_specs=P("row", "lon", None),
        check_vma=False,
    )
```

```python
import jax
import jax.numpy as jnp
from jax import lax
from jax.experimental import pallas as pl
from jax.experimental.pallas import tpu as pltpu
from jax.sharding import PartitionSpec as P

ROWS_DEV = 8
COLS_DEV = 128
VARS = 12
CH = 128
GROUPS = 32
SLOTS = 4
BCELLS = 32
BLK_DEV = 4
NBLK = 128
PER_GROUP = CH // GROUPS
MESH = pl.DeviceIdType.MESH
F32 = jnp.float32
BF16 = jnp.bfloat16

eps = 1e-05


def coords():
    row = lax.axis_index("row")
    lon = lax.axis_index("lon")
    core = lax.rem(row, 2)
    z_hi = lax.rem(lax.div(row, 2), 2)
    x = lax.div(row, 4)
    y = lax.div(lon, 8)
    z = z_hi * 8 + lax.rem(lon, 8)
    return row, lon, x, y, z, core


def device_at(x, y, z, core):
    return (x * 4 + lax.div(z, 8) * 2 + core, y * 8 + lax.rem(z, 8))


def moved(value, step, count):
    return lax.rem(value + step, count) if step else value


def along_z(place):
    _, _, x, y, z, core = place
    steps = [(d, c) for d in range(16) for c in range(2) if d or c]
    steps.sort(key=lambda s: -min(s[0], 16 - s[0]))
    return [device_at(x, y, moved(z, d, 16), moved(core, c, 2)) for d, c in steps]


def across(place):
    _, _, x, y, z, core = place
    steps = [(a, b) for a in range(4) for b in range(4) if a or b]
    steps.sort(key=lambda s: -(min(s[0], 4 - s[0]) + min(s[1], 4 - s[1])))
    return [device_at(moved(x, a, 4), moved(y, b, 4), z, core) for a, b in steps]


def coarse_mates(place):
    _, _, x, y, z, core = place
    z_lo = lax.rem(z, 8)
    mates = []
    for step in (2, 1, -1, -2):
        turn = lax.rem(y + 3 + lax.div(z_lo + 8 + step, 8), 4)
        mates.append(device_at(x, turn, lax.rem(z + 16 + step, 16), core))
    return mates


def iota(shape, dim):
    return lax.broadcasted_iota(jnp.int32, shape, dim)


def split(value):
    high = value.astype(BF16)
    low = (value - high.astype(F32)).astype(BF16)
    return high, low


def dot(a, b, dims=((1,), (0,))):
    return lax.dot_general(a, b, (dims, ((), ())), preferred_element_type=F32)


def over_group(row):
    lane = iota(row.shape, 1)
    near = jnp.where((lane & 1) == 0, pltpu.roll(row, CH - 1, 1), pltpu.roll(row, 1, 1))
    row = row + near
    far = jnp.where((lane & 2) == 0, pltpu.roll(row, CH - 2, 1), pltpu.roll(row, 2, 1))
    return row + far


def local_stats(rows, cells):
    total = sum(jnp.sum(r, axis=0, keepdims=True) for r in rows)
    mean = over_group(total) * (1.0 / (cells * PER_GROUP))
    dev = sum(jnp.sum((r - mean) * (r - mean), axis=0, keepdims=True) for r in rows)
    return mean, over_group(dev)


def merge(mean, dev, others, cells):
    count = others.shape[0] + 1
    means = others[:, 0:1, :]
    whole = (mean + jnp.sum(means, axis=0)) * (1.0 / count)
    off = means - whole
    own = mean - whole
    spread = own * own + jnp.sum(off * off, axis=0)
    return whole, dev + jnp.sum(others[:, 1:2, :], axis=0) + (cells * PER_GROUP) * spread


LEFT, MAIN, RIGHT, WIDE = 8, 16, 144, 160


def kernel(
    src_ref, cnt_ref, coarse_ref, remap_ref, ca_ref, cb_ref, gain_a_ref, shift_a_ref, gain_b_ref, shift_b_ref,
    hb_ref, fin_ref,
    coarse_v, remap_v, ca_v, cb_v, vec_v,
    tt, row_out, col_out, corner_out, mate_out, next_out,
    row_in, col_in, corner_in, mate_in, next_in,
    copies, choices, side, wa32, wa, wb,
    xs, gs, ha, act, hb,
    stat, buf_x, buf_z,
    in_sem, out_sem, send_sem, recv_sem,
):
    place = coords()
    row, lon = place[0], place[1]
    z_mates = along_z(place)
    xy_mates = across(place)
    lon_mates = coarse_mates(place)
    row_up, row_down = lax.rem(row + 15, 16), lax.rem(row + 1, 16)
    lon_left, lon_right = lax.rem(lon + 31, 32), lax.rem(lon + 1, 32)
    halo = [
        (row_down, lon), (row_up, lon),
        (row, lon_right), (row, lon_left),
        (row_down, lon_right), (row_up, lon_right),
        (row_down, lon_left), (row_up, lon_left),
    ]
    odd = lax.rem(row, 2)
    core_mate = (row + 1 - 2 * odd, lon)
    far_mate = (lax.rem(row + 2 * odd + 15, 16), lon)
    barrier = pltpu.get_barrier_semaphore()
    partners = halo + lon_mates + z_mates + xy_mates
    for mate in partners:
        pl.semaphore_signal(barrier, inc=1, device_id=mate, device_id_type=MESH)

    loads = [
        pltpu.make_async_copy(coarse_ref, coarse_v, in_sem.at[0]),
        pltpu.make_async_copy(remap_ref, remap_v, in_sem.at[1]),
        pltpu.make_async_copy(ca_ref, ca_v, in_sem.at[2]),
        pltpu.make_async_copy(cb_ref, cb_v, in_sem.at[3]),
    ]
    for i, ref in enumerate((gain_a_ref, shift_a_ref, gain_b_ref, shift_b_ref)):
        loads.append(pltpu.make_async_copy(ref, vec_v.at[i], in_sem.at[4 + i]))
    for load in loads:
        load.start()

    lane = iota((1, 128), 1)
    own_choice = jnp.zeros((1, 128), F32)
    for k in range(SLOTS):
        local = lax.rem(src_ref[0, k] - (lon - 1) * BLK_DEV + 2 * NBLK, NBLK)
        local = jnp.where(k < cnt_ref[0], local, -64)
        own_choice = jnp.where((lane >> 5) == k, local.astype(F32), own_choice)
    choice_tile = jnp.broadcast_to(own_choice, (16, 128)).astype(BF16)

    for q in range(BLK_DEV):
        want = q * BCELLS + (lane & (BCELLS - 1))
        copies[:, q * 128 : (q + 1) * 128] = jnp.where(iota((128, 128), 0) == want, 1.0, 0.0).astype(BF16)

    loads[0].wait()
    held = coarse_v[...].astype(F32)
    tile = jnp.zeros((VARS, 128), F32)
    for b in range(BLK_DEV):
        put = jnp.where(iota((BCELLS, 128), 0) + b * BCELLS == iota((BCELLS, 128), 1), 1.0, 0.0)
        tile = tile + dot(held[:, b, :].astype(BF16), put.astype(BF16))
    pad = jnp.concatenate([tile, jnp.zeros((16 - VARS, 128), F32)], axis=0)
    tt[2] = pad.astype(BF16)

    loads[1].wait()
    at = iota((224, 1), 0)
    inner = at & 15
    cell = jnp.where(at < 128, at + odd * (7 * COLS_DEV), -1)
    column = (inner & 7) * COLS_DEV + (inner >> 3)
    cell = jnp.where((at >= 128) & (at < 144), column + 126, cell)
    cell = jnp.where((at >= 144) & (at < 160), column, cell)
    for i, (row0, col0) in enumerate(((6, 126), (0, 126), (6, 0), (0, 0))):
        here = (at >= 160 + 16 * i) & (at < 164 + 16 * i)
        cell = jnp.where(here, (row0 + (inner >> 1)) * COLS_DEV + col0 + (inner & 1), cell)
    pick = jnp.where(iota((224, 1024), 1) == cell, 1.0, 0.0).astype(BF16)
    weights = dot(pick, remap_v[...], ((1,), (1,))).astype(BF16)
    row_out[0:128, :] = weights[0:128]
    row_out[128:144, :] = choice_tile
    for i in range(2):
        col_out[i, 0:16, :] = weights[128 + 16 * i : 144 + 16 * i]
        col_out[i, 16:32, :] = choice_tile
    for i in range(4):
        cells = weights[160 + 16 * i : 176 + 16 * i].astype(F32)
        corner_out[i] = jnp.where(iota((16, 128), 0) < 8, cells, own_choice).astype(BF16)
    side[...] = jnp.zeros_like(side)

    loads[2].wait()
    wa32[...] = jnp.zeros_like(wa32)
    for dy in range(3):
        for part in range(3):
            first = (dy * 3 + part) * VARS
            for dx in range(3):
                wa32[first : first + VARS, dx * CH : (dx + 1) * CH] = ca_v[dy, dx]
    line = iota((128, 3 * CH), 0)
    twelfth = (line * 43) >> 9
    part_of = twelfth - 3 * ((twelfth * 11) >> 5)
    whole = wa32[...]
    high, low = split(whole)
    wa[...] = jnp.where(part_of == 2, low.astype(F32), high.astype(F32)).astype(BF16)

    twelfth_l = (lane * 43) >> 9
    var_l = jnp.where(lane < 9 * VARS, lane - 12 * twelfth_l, 4096)
    part_l = twelfth_l - 3 * ((twelfth_l * 11) >> 5)
    want = jnp.where(part_l == 1, var_l + 16, var_l)
    spread_msg = jnp.where(iota((32, 128), 0) == want, 1.0, 0.0).astype(BF16)
    spread_var = jnp.where(iota((16, 128), 0) == var_l, 1.0, 0.0).astype(BF16)
    not_first = jnp.where(row > 0, 1.0, 0.0).astype(F32)
    not_last = jnp.where(row < 15, 1.0, 0.0).astype(F32)

    pl.semaphore_wait(barrier, len(partners))

    def send(src, dst, mate, out, into):
        copy = pltpu.make_async_remote_copy(
            src_ref=src, dst_ref=dst, send_sem=send_sem.at[out], recv_sem=recv_sem.at[into],
            device_id=mate, device_id_type=MESH,
        )
        copy.start()

    send(row_out, row_in, far_mate, 0, 0)
    for i in range(4):
        send(corner_out.at[i], corner_in.at[i], halo[4 + i], 1, 1)
    for i in range(2):
        send(col_out.at[i], col_in.at[i], halo[2 + i], 8, 2)
    along_lon = [
        pltpu.make_async_remote_copy(
            src_ref=tt.at[2], dst_ref=tt.at[slot], send_sem=send_sem.at[7], recv_sem=recv_sem.at[8 + i],
            device_id=mate, device_id_type=MESH,
        )
        for i, (slot, mate) in enumerate(zip((0, 1, 3, 4), lon_mates))
    ]
    for copy in along_lon:
        copy.start()

    loads[3].wait()
    for dy in range(3):
        for dx in range(3):
            high, low = split(cb_v[dy, dx])
            span = slice(dx * CH, (dx + 1) * CH)
            wb[dy * 384 : dy * 384 + 128, span] = high
            wb[dy * 384 + 128 : dy * 384 + 256, span] = high
            wb[dy * 384 + 256 : dy * 384 + 384, span] = low
    for load in loads[4:]:
        load.wait()

    for copy in along_lon:
        copy.wait_recv()
    choices[...] = dot(tt[...].reshape(80, 128), copies[...])

    def chosen(choice, first_tile):
        total = jnp.zeros((16, 128), F32)
        for j in range(3 * BLK_DEV):
            t, q = first_tile + j // BLK_DEV, j % BLK_DEV
            total = jnp.where(choice == j, choices[t * 16 : t * 16 + 16, q * 128 : (q + 1) * 128], total)
        return total

    blocks = chosen(own_choice, 1).astype(BF16)

    four = jnp.concatenate([remap_v[:, 0:256], remap_v[:, 768:1024]], axis=1)
    four = dot(blocks, four)
    is_odd = odd == 1
    mate_out[0] = jnp.where(is_odd, four[:, 0:128], four[:, 384:512])
    mate_out[1] = jnp.where(is_odd, four[:, 128:256], four[:, 256:384])
    next_out[...] = jnp.where(is_odd, four[:, 256:384], four[:, 128:256])
    send(mate_out, mate_in, core_mate, 2, 3)
    send(next_out, next_in, far_mate, 9, 12)

    spread_blocks = dot(blocks, spread_var, ((0,), (0,))).astype(BF16)
    fine = dot(remap_v[...], spread_blocks, ((0,), (0,)))
    high, low = split(fine)
    packed = jnp.where(part_l == 1, low.astype(F32), high.astype(F32)).astype(BF16)
    xs[2:10] = packed.reshape(ROWS_DEV, COLS_DEV, 128)

    third = jnp.broadcast_to(lane, (128, 128))

    def patches(before, here, after, lanes):
        before = jnp.where(lanes < 3 * VARS, before.astype(F32), 0.0)
        here = jnp.where((lanes >= 3 * VARS) & (lanes < 6 * VARS), here.astype(F32), 0.0)
        after = jnp.where(lanes >= 6 * VARS, after.astype(F32), 0.0)
        return (before + here + after).astype(BF16)

    def taps(out_rows):
        field = [patches(xs[i], xs[i + 1], xs[i + 2], third) for i in out_rows]
        result = dot(jnp.concatenate(field, axis=0), wa[...])
        for n, i in enumerate(out_rows):
            for dx in range(3):
                gs[dx, i, MAIN:RIGHT, :] = result[n * 128 : (n + 1) * 128, dx * CH : (dx + 1) * CH]

    def joined(i, first, size):
        return gs[0, i, first - 1 : first - 1 + size, :] + gs[1, i, first : first + size, :] + gs[2, i, first + 1 : first + 1 + size, :]

    taps(list(range(2, 8)))

    def placed(fine):
        high, low = split(fine)
        return dot(jnp.concatenate([high, low], axis=0), spread_msg, ((0,), (0,))).astype(BF16)

    pltpu.make_async_copy(mate_in, mate_in, recv_sem.at[3]).wait()
    xs[10 - 9 * odd] = placed(mate_in[0])
    xs[11 - 11 * odd] = placed(mate_in[1])

    pltpu.make_async_copy(col_in, col_in, recv_sem.at[2]).wait()
    pltpu.make_async_copy(corner_in, corner_in, recv_sem.at[1]).wait()
    pltpu.make_async_copy(row_in, row_in, recv_sem.at[0]).wait()
    far_known = jnp.where(is_odd, not_last, not_first)

    def fine_of(cells, choice, first_tile, known):
        held = chosen(choice.astype(F32), first_tile) * known
        return dot(cells, held.astype(BF16), ((1,), (1,)))

    parts = [
        fine_of(row_in[0:128, :], row_in[128:129, :], 1, far_known),
        fine_of(col_in[0, 0:16, :], col_in[0, 16:17, :], 0, 1.0),
        fine_of(col_in[1, 0:16, :], col_in[1, 16:17, :], 2, 1.0),
    ]
    for i, (first_tile, known) in enumerate(((0, not_first), (0, not_last), (2, not_first), (2, not_last))):
        parts.append(fine_of(corner_in[i], corner_in[i, 8:9, :], first_tile, known))
    high, low = split(jnp.concatenate(parts, axis=0))
    cells = dot(jnp.concatenate([high, low], axis=1), spread_msg)
    xs[1 + 9 * odd] = cells[0:128].astype(BF16)
    for i, first in enumerate((6, 0)):
        for n in range(16):
            line = ((n & 7) + 2) * 8 + first + (n >> 3)
            side[line : line + 1, :] = cells[128 + 16 * i + n : 129 + 16 * i + n]
    for i, first in enumerate((6, 86, 0, 80)):
        for n in range(4):
            line = first + (n >> 1) * 8 + (n & 1)
            side[line : line + 1, :] = cells[160 + 16 * i + n : 161 + 16 * i + n]
    edge = side[...].reshape(12, 8, 128)
    side_lane = jnp.broadcast_to(lane.reshape(1, 1, 128), (10, 8, 128))
    side_patches = patches(edge[0:10], edge[1:11], edge[2:12], side_lane).reshape(80, 128)
    side_taps = dot(side_patches, wa[...]).reshape(10, 8, 3 * CH)
    for dx in range(3):
        piece = side_taps[:, :, dx * CH : (dx + 1) * CH]
        gs[dx, :, LEFT:MAIN, :] = piece
        gs[dx, :, RIGHT : RIGHT + 8, :] = piece
    taps([1, 8])
    for i in range(1, 9):
        ha[i, MAIN:RIGHT, :] = joined(i, MAIN, 128)

    def all_reduce(turn, mean, dev, beside):
        cells = ROWS_DEV * COLS_DEV
        for stage, (mates, buf) in enumerate(((z_mates, buf_z), (xy_mates, buf_x))):
            sem = 4 + turn * 2 + stage
            stat[turn, stage, 0:1, :] = mean
            stat[turn, stage, 1:2, :] = dev
            for j, mate in enumerate(mates):
                pltpu.make_async_remote_copy(
                    src_ref=stat.at[turn, stage], dst_ref=buf.at[turn, j], send_sem=send_sem.at[sem - 1], recv_sem=recv_sem.at[sem],
                    device_id=mate, device_id_type=MESH,
                ).start()
            if stage == 0:
                beside()
            pltpu.make_async_copy(buf.at[turn], buf.at[turn], recv_sem.at[sem]).wait()
            mean, dev = merge(mean, dev, buf[turn], cells)
            cells = cells * (len(mates) + 1)
        return mean, lax.rsqrt(dev * (1.0 / (cells * PER_GROUP)) + eps)

    def around_a():
        pltpu.make_async_copy(next_in, next_in, recv_sem.at[12]).wait()
        xs[11 * odd] = placed(next_in[...] * far_known)
        taps([0, 9])
        for i in (0, 9):
            ha[i, MAIN:RIGHT, :] = joined(i, MAIN, 128)
        for i in range(10):
            ha[i, LEFT:MAIN, :] = joined(i, LEFT, 8)
            ha[i, RIGHT : RIGHT + 8, :] = joined(i, RIGHT, 8)

    mean, dev = local_stats([ha[i, MAIN:RIGHT, :] for i in range(1, 9)], ROWS_DEV * COLS_DEV)
    mean, inverse = all_reduce(0, mean, dev, around_a)

    scale = inverse * vec_v[0]
    shift = vec_v[1]
    for i in range(10):
        for first, size, at in ((MAIN, 128, 0), (LEFT, 16, 128)):
            if size == 128:
                value = ha[i, MAIN:RIGHT, :]
            else:
                value = jnp.concatenate([ha[i, RIGHT : RIGHT + 8, :], ha[i, LEFT:MAIN, :]], axis=0)
            normed = (value - mean) * scale + shift
            half = normed * 0.5
            value = half + half * jnp.tanh(half)
            if i == 0:
                value = value * not_first
            if i == 9:
                value = value * not_last
            high, low = split(value)
            act[i, at : at + size, 0:128] = high
            act[i, at : at + size, 128:256] = low
            act[i, at : at + size, 256:384] = high

    field = jnp.concatenate([act[0:8], act[1:9], act[2:10]], axis=2).reshape(8 * 144, 9 * CH)
    result = dot(field, wb[...]).reshape(8, 144, 3 * CH)
    for dx in range(3):
        span = slice(dx * CH, (dx + 1) * CH)
        gs[dx, 0:8, MAIN:RIGHT, :] = result[:, 0:128, span]
        gs[dx, 0:8, RIGHT : RIGHT + 8, :] = result[:, 128:136, span]
        gs[dx, 0:8, LEFT:MAIN, :] = result[:, 136:144, span]
    for i in range(8):
        hb[i] = joined(i, MAIN, 128)
    store = pltpu.make_async_copy(hb, hb_ref, out_sem)
    store.start()
    mean, dev = local_stats([hb[i] for i in range(8)], ROWS_DEV * COLS_DEV)
    mean, inverse = all_reduce(1, mean, dev, lambda: None)
    fin_ref[0:1, :] = mean
    fin_ref[1:2, :] = inverse * vec_v[2]
    fin_ref[2:3, :] = vec_v[3]
    store.wait()

    pltpu.make_async_copy(row_in, row_in, send_sem.at[0]).wait()
    pltpu.make_async_copy(corner_in, corner_in, send_sem.at[1]).wait()
    pltpu.make_async_copy(col_in, col_in, send_sem.at[8]).wait()
    pltpu.make_async_copy(mate_in, mate_in, send_sem.at[2]).wait()
    pltpu.make_async_copy(next_in, next_in, send_sem.at[9]).wait()
    pltpu.make_async_copy(tt.at[pl.ds(0, 4)], tt.at[pl.ds(0, 4)], send_sem.at[7]).wait()
    for turn in range(2):
        pltpu.make_async_copy(buf_z.at[turn], buf_z.at[turn], send_sem.at[3 + 2 * turn]).wait()
        pltpu.make_async_copy(buf_x.at[turn], buf_x.at[turn], send_sem.at[4 + 2 * turn]).wait()


def per_device(
    coarse, src_blocks, slot_counts, remap_tiles, conv_a, conv_b, gain_a, shift_a, gain_b, shift_b
):
    anywhere = pl.BlockSpec(memory_space=pl.ANY)
    scalar = pl.BlockSpec(memory_space=pltpu.SMEM)
    vectors = [v.reshape(1, CH) for v in (gain_a, shift_a, gain_b, shift_b)]
    hidden, final = pl.pallas_call(
        kernel,
        name="stem",
        out_shape=(
            pltpu.VMEM((ROWS_DEV, COLS_DEV, CH), F32),
            pltpu.VMEM((3, CH), F32),
        ),
        in_specs=[scalar, scalar] + [anywhere] * 8,
        out_specs=(anywhere, pl.BlockSpec(memory_space=pltpu.VMEM)),
        scratch_shapes=[
            pltpu.VMEM((VARS, BLK_DEV, BCELLS), BF16),
            pltpu.VMEM((128, 1024), BF16),
            pltpu.VMEM((3, 3, VARS, CH), F32),
            pltpu.VMEM((3, 3, CH, CH), F32),
            pltpu.VMEM((4, 1, CH), F32),
            pltpu.VMEM((5, 16, 128), BF16),
            pltpu.VMEM((144, 128), BF16),
            pltpu.VMEM((2, 32, 128), BF16),
            pltpu.VMEM((4, 16, 128), BF16),
            pltpu.VMEM((2, 16, 128), F32),
            pltpu.VMEM((16, 128), F32),
            pltpu.VMEM((144, 128), BF16),
            pltpu.VMEM((2, 32, 128), BF16),
            pltpu.VMEM((4, 16, 128), BF16),
            pltpu.VMEM((2, 16, 128), F32),
            pltpu.VMEM((16, 128), F32),
            pltpu.VMEM((128, BLK_DEV * 128), BF16),
            pltpu.VMEM((80, BLK_DEV * 128), F32),
            pltpu.VMEM((96, 128), F32),
            pltpu.VMEM((128, 3 * CH), F32),
            pltpu.VMEM((128, 3 * CH), BF16),
            pltpu.VMEM((9 * CH, 3 * CH), BF16),
            pltpu.VMEM((12, COLS_DEV, 128), BF16),
            pltpu.VMEM((3, 10, WIDE, CH), F32),
            pltpu.VMEM((10, WIDE, CH), F32),
            pltpu.VMEM((10, 144, 3 * CH), BF16),
            pltpu.VMEM((ROWS_DEV, COLS_DEV, CH), F32),
            pltpu.VMEM((2, 2, 2, CH), F32),
            pltpu.VMEM((2, 15, 2, CH), F32),
            pltpu.VMEM((2, 31, 2, CH), F32),
            pltpu.SemaphoreType.DMA((8,)),
            pltpu.SemaphoreType.DMA,
            pltpu.SemaphoreType.DMA((10,)),
            pltpu.SemaphoreType.DMA((13,)),
        ],
        compiler_params=pltpu.CompilerParams(
            collective_id=0, has_side_effects=True, vmem_limit_bytes=60 * 1024 * 1024
        ),
    )(
        src_blocks, slot_counts, jnp.transpose(coarse, (1, 0, 2)), remap_tiles.reshape(SLOTS * BCELLS, 1024),
        conv_a, conv_b, *vectors,
    )
    normed = (hidden - final[0]) * final[1] + final[2]
    return jax.nn.silu(normed).astype(BF16)


def solution(mesh):
    return jax.shard_map(
        per_device,
        mesh=mesh,
        in_specs=(
            P("lon", None, None),
            P(("row", "lon"), None),
            P(("row", "lon")),
            P(("row", "lon"), None, None, None),
            P(),
            P(),
            P(),
            P(),
            P(),
            P(),
        ),
        out_specs=P("row", "lon", None),
        check_vma=False,
    )
```

```python
import jax
import jax.numpy as jnp
from jax import lax
from jax.experimental import pallas as pl
from jax.experimental.pallas import tpu as pltpu
from jax.sharding import PartitionSpec as P

ROWS_DEV = 8
COLS_DEV = 128
VARS = 12
CH = 128
GROUPS = 32
SLOTS = 4
BCELLS = 32
BLK_DEV = 4
NBLK = 128
PER_GROUP = CH // GROUPS
MESH = pl.DeviceIdType.MESH
F32 = jnp.float32
BF16 = jnp.bfloat16

eps = 1e-05


def coords():
    row = lax.axis_index("row")
    lon = lax.axis_index("lon")
    core = lax.rem(row, 2)
    z_hi = lax.rem(lax.div(row, 2), 2)
    x = lax.div(row, 4)
    y = lax.div(lon, 8)
    z = z_hi * 8 + lax.rem(lon, 8)
    return row, lon, x, y, z, core


def device_at(x, y, z, core):
    return (x * 4 + lax.div(z, 8) * 2 + core, y * 8 + lax.rem(z, 8))


def moved(value, step, count):
    return lax.rem(value + step, count) if step else value


def along_z(place):
    _, _, x, y, z, core = place
    steps = [(d, c) for d in range(16) for c in range(2) if d or c]
    steps.sort(key=lambda s: -min(s[0], 16 - s[0]))
    return [device_at(x, y, moved(z, d, 16), moved(core, c, 2)) for d, c in steps]


def across(place):
    _, _, x, y, z, core = place
    steps = [(a, b) for a in range(4) for b in range(4) if a or b]
    steps.sort(key=lambda s: -(min(s[0], 4 - s[0]) + min(s[1], 4 - s[1])))
    return [device_at(moved(x, a, 4), moved(y, b, 4), z, core) for a, b in steps]


def coarse_mates(place):
    _, _, x, y, z, core = place
    z_lo = lax.rem(z, 8)
    mates = []
    for step in (2, 1, -1, -2):
        turn = lax.rem(y + 3 + lax.div(z_lo + 8 + step, 8), 4)
        mates.append(device_at(x, turn, lax.rem(z + 16 + step, 16), core))
    return mates


def iota(shape, dim):
    return lax.broadcasted_iota(jnp.int32, shape, dim)


def split(value):
    high = value.astype(BF16)
    low = (value - high.astype(F32)).astype(BF16)
    return high, low


def dot(a, b, dims=((1,), (0,))):
    return lax.dot_general(a, b, (dims, ((), ())), preferred_element_type=F32)


def over_group(row):
    place = iota(row.shape, 1) & (PER_GROUP - 1)
    total = row
    for step in range(1, PER_GROUP):
        after = pltpu.roll(row, CH - step, 1)
        before = pltpu.roll(row, step, 1)
        total = total + jnp.where(place < PER_GROUP - step, after, 0.0) + jnp.where(place >= step, before, 0.0)
    return total


def local_stats(rows):
    cells = len(rows) * rows[0].shape[0]
    about = jnp.sum(rows[0], axis=0, keepdims=True) * (1.0 / rows[0].shape[0])
    first, second = 0.0, 0.0
    for r in rows:
        off = r - about
        first = first + off
        second = second + off * off
    first = jnp.sum(first, axis=0, keepdims=True)
    mean_off = first * (1.0 / cells)
    dev = jnp.sum(second, axis=0, keepdims=True) - first * mean_off
    return about + mean_off, dev


def to_groups(mean, dev, cells):
    whole = over_group(mean) * (1.0 / PER_GROUP)
    apart = mean - whole
    spread = over_group(dev + cells * (apart * apart)) * (1.0 / (cells * PER_GROUP))
    return whole, lax.rsqrt(spread + eps)


def merge(mean, dev, others, cells):
    count = others.shape[0] + 1
    means = others[:, 0:1, :]
    whole = (mean + jnp.sum(means, axis=0)) * (1.0 / count)
    off = means - whole
    own = mean - whole
    spread = own * own + jnp.sum(off * off, axis=0)
    return whole, dev + jnp.sum(others[:, 1:2, :], axis=0) + cells * spread


LEFT, MAIN, RIGHT, WIDE = 8, 16, 144, 160


def prepare_b(cb_v, wba, wbb):
    for dy in range(3):
        for dx in range(2):
            span = slice(dx * CH, (dx + 1) * CH)
            high, low = split(cb_v[dy, dx])
            wba[dy * 256 : dy * 256 + 128, span] = high
            wba[dy * 256 + 128 : dy * 256 + 256, span] = high
            wba[768 + dy * 128 : 896 + dy * 128, span] = low
        high, low = split(cb_v[dy, 2])
        for part, value in enumerate((high, high, low)):
            if dy < 2:
                wbb[part * 256 + dy * 128 : part * 256 + dy * 128 + 128, 0:CH] = value
            else:
                wbb[part * 256 : part * 256 + 128, CH : 2 * CH] = jnp.zeros((CH, CH), BF16)
                wbb[part * 256 + 128 : part * 256 + 256, CH : 2 * CH] = value


def activate(value, mean, scale, shift):
    half = ((value - mean) * scale + shift) * 0.5
    return half + half * jnp.tanh(half)


def second_conv(ha, hl, act, gs, hb, wba, wbb, mean, scale, shift, not_first, not_last):
    for i in range(10):
        value = activate(ha[i, MAIN:RIGHT, :], mean, scale, shift)
        if i == 0:
            value = value * not_first
        if i == 9:
            value = value * not_last
        act[i, :, 0:128], act[i, :, 128:256] = split(value)
    known = iota((16, 1), 0)
    known = jnp.where(known == 0, not_first, jnp.where(known == 9, not_last, 1.0))
    for i in range(2):
        hl[i, 0:16, :] = activate(hl[i, 0:16, :], mean, scale, shift) * known

    def side(i, dy):
        return split(hl[i, dy : dy + 16, :])

    def rows(first, size, part):
        return act[first : first + size, :, part * 128 : part * 128 + 128].reshape(size * 128, 128)

    pieces = [act[dy : dy + 8].reshape(1024, 256) for dy in range(3)] + [rows(dy, 8, 0) for dy in range(3)]
    at_side = [side(0, dy) for dy in range(3)]
    at_side = [part for pair in at_side for part in pair] + [pair[0] for pair in at_side]
    field = jnp.concatenate([jnp.concatenate(pieces, axis=1), jnp.concatenate(at_side, axis=1)], axis=0)
    early = dot(field, wba[...])

    pieces = [rows(0, 9, 0), rows(1, 9, 0), rows(0, 9, 1), rows(1, 9, 1), rows(0, 9, 0), rows(1, 9, 0)]
    (high0, low0), (high1, low1) = side(1, 0), side(1, 1)
    at_side = [high0, high1, low0, low1, high0, high1]
    field = jnp.concatenate([jnp.concatenate(pieces, axis=1), jnp.concatenate(at_side, axis=1)], axis=0)
    late = dot(field, wbb[...])

    for i in range(8):
        gs[0, i, MAIN:RIGHT, :] = early[i * 128 : (i + 1) * 128, 0:128]
        gs[0, i, MAIN - 1 : MAIN, :] = early[1024 + i : 1025 + i, 0:128]
        gs[2, i, MAIN:RIGHT, :] = late[i * 128 : (i + 1) * 128, 0:128] + late[(i + 1) * 128 : (i + 2) * 128, 128:256]
        gs[2, i, RIGHT : RIGHT + 1, :] = late[1152 + i : 1153 + i, 0:128] + late[1153 + i : 1154 + i, 128:256]
        hb[i] = gs[0, i, MAIN - 1 : RIGHT - 1, :] + early[i * 128 : (i + 1) * 128, 128:256] + gs[2, i, MAIN + 1 : RIGHT + 1, :]


def kernel(
    src_hbm, cnt_ref, coarse_ref, remap_ref, ca_ref, cb_ref, gain_a_ref, shift_a_ref, gain_b_ref, shift_b_ref,
    hb_ref, fin_ref,
    src_ref, coarse_v, remap_v, ca_v, cb_v, vec_v,
    tt, row_out, col_out, corner_out, mate_out, next_out,
    row_in, col_in, corner_in, mate_in, next_in,
    copies, choices, side, wa32, wa, wba, wbb,
    xs, gs, ha, hl, act, hb,
    stat, buf_x, buf_z,
    in_sem, out_sem, send_sem, recv_sem,
):
    place = coords()
    row, lon = place[0], place[1]
    z_mates = along_z(place)
    xy_mates = across(place)
    lon_mates = coarse_mates(place)
    row_up, row_down = lax.rem(row + 15, 16), lax.rem(row + 1, 16)
    lon_left, lon_right = lax.rem(lon + 31, 32), lax.rem(lon + 1, 32)
    halo = [
        (row_down, lon), (row_up, lon),
        (row, lon_right), (row, lon_left),
        (row_down, lon_right), (row_up, lon_right),
        (row_down, lon_left), (row_up, lon_left),
    ]
    odd = lax.rem(row, 2)
    core_mate = (row + 1 - 2 * odd, lon)
    far_mate = (lax.rem(row + 2 * odd + 15, 16), lon)
    barrier = pltpu.get_barrier_semaphore()
    partners = halo + lon_mates + z_mates + xy_mates
    for mate in partners:
        pl.semaphore_signal(barrier, inc=1, device_id=mate, device_id_type=MESH)

    loads = [
        pltpu.make_async_copy(coarse_ref, coarse_v, in_sem.at[0]),
        pltpu.make_async_copy(remap_ref, remap_v, in_sem.at[1]),
        pltpu.make_async_copy(ca_ref, ca_v, in_sem.at[2]),
        pltpu.make_async_copy(cb_ref, cb_v, in_sem.at[3]),
    ]
    for i, ref in enumerate((gain_a_ref, shift_a_ref, gain_b_ref, shift_b_ref)):
        loads.append(pltpu.make_async_copy(ref, vec_v.at[i], in_sem.at[4 + i]))
    sources = pltpu.make_async_copy(src_hbm, src_ref, in_sem.at[8])
    for load in [sources] + loads:
        load.start()

    sources.wait()
    lane = iota((1, 128), 1)
    own_choice = jnp.zeros((1, 128), F32)
    for k in range(SLOTS):
        local = lax.rem(src_ref[0, k] - (lon - 1) * BLK_DEV + 2 * NBLK, NBLK)
        local = jnp.where(k < cnt_ref[0], local, -64)
        own_choice = jnp.where((lane >> 5) == k, local.astype(F32), own_choice)
    choice_tile = jnp.broadcast_to(own_choice, (16, 128)).astype(BF16)

    for q in range(BLK_DEV):
        want = q * BCELLS + (lane & (BCELLS - 1))
        copies[:, q * 128 : (q + 1) * 128] = jnp.where(iota((128, 128), 0) == want, 1.0, 0.0).astype(BF16)

    loads[0].wait()
    held = coarse_v[...].astype(F32)
    tile = jnp.zeros((VARS, 128), F32)
    for b in range(BLK_DEV):
        put = jnp.where(iota((BCELLS, 128), 0) + b * BCELLS == iota((BCELLS, 128), 1), 1.0, 0.0)
        tile = tile + dot(held[:, b, :].astype(BF16), put.astype(BF16))
    pad = jnp.concatenate([tile, jnp.zeros((16 - VARS, 128), F32)], axis=0)
    tt[2] = pad.astype(BF16)

    loads[1].wait()
    at = iota((224, 1), 0)
    inner = at & 15
    cell = jnp.where(at < 128, at + odd * (7 * COLS_DEV), -1)
    column = (inner & 7) * COLS_DEV + (inner >> 3)
    cell = jnp.where((at >= 128) & (at < 144), column + 126, cell)
    cell = jnp.where((at >= 144) & (at < 160), column, cell)
    for i, (row0, col0) in enumerate(((6, 126), (0, 126), (6, 0), (0, 0))):
        here = (at >= 160 + 16 * i) & (at < 164 + 16 * i)
        cell = jnp.where(here, (row0 + (inner >> 1)) * COLS_DEV + col0 + (inner & 1), cell)
    pick = jnp.where(iota((224, 1024), 1) == cell, 1.0, 0.0).astype(BF16)
    weights = dot(pick, remap_v[...], ((1,), (1,))).astype(BF16)
    row_out[0:128, :] = weights[0:128]
    row_out[128:144, :] = choice_tile
    for i in range(2):
        col_out[i, 0:16, :] = weights[128 + 16 * i : 144 + 16 * i]
        col_out[i, 16:32, :] = choice_tile
    for i in range(4):
        cells = weights[160 + 16 * i : 176 + 16 * i].astype(F32)
        corner_out[i] = jnp.where(iota((16, 128), 0) < 8, cells, own_choice).astype(BF16)
    side[...] = jnp.zeros_like(side)
    hl[...] = jnp.zeros_like(hl)

    loads[2].wait()
    wa32[...] = jnp.zeros_like(wa32)
    for dy in range(3):
        for part in range(3):
            first = (dy * 3 + part) * VARS
            for dx in range(3):
                wa32[first : first + VARS, dx * CH : (dx + 1) * CH] = ca_v[dy, dx]
    line = iota((128, 3 * CH), 0)
    twelfth = (line * 43) >> 9
    part_of = twelfth - 3 * ((twelfth * 11) >> 5)
    whole = wa32[...]
    high, low = split(whole)
    wa[...] = jnp.where(part_of == 2, low.astype(F32), high.astype(F32)).astype(BF16)

    twelfth_l = (lane * 43) >> 9
    var_l = jnp.where(lane < 9 * VARS, lane - 12 * twelfth_l, 4096)
    part_l = twelfth_l - 3 * ((twelfth_l * 11) >> 5)
    want = jnp.where(part_l == 1, var_l + 16, var_l)
    spread_msg = jnp.where(iota((32, 128), 0) == want, 1.0, 0.0).astype(BF16)
    spread_var = jnp.where(iota((16, 128), 0) == var_l, 1.0, 0.0).astype(BF16)
    not_first = jnp.where(row > 0, 1.0, 0.0).astype(F32)
    not_last = jnp.where(row < 15, 1.0, 0.0).astype(F32)

    pl.semaphore_wait(barrier, len(partners))

    def send(src, dst, mate, out, into):
        copy = pltpu.make_async_remote_copy(
            src_ref=src, dst_ref=dst, send_sem=send_sem.at[out], recv_sem=recv_sem.at[into],
            device_id=mate, device_id_type=MESH,
        )
        copy.start()

    send(row_out, row_in, far_mate, 0, 0)
    for i in range(4):
        send(corner_out.at[i], corner_in.at[i], halo[4 + i], 1, 1)
    for i in range(2):
        send(col_out.at[i], col_in.at[i], halo[2 + i], 8, 2)
    along_lon = [
        pltpu.make_async_remote_copy(
            src_ref=tt.at[2], dst_ref=tt.at[slot], send_sem=send_sem.at[7], recv_sem=recv_sem.at[8 + i],
            device_id=mate, device_id_type=MESH,
        )
        for i, (slot, mate) in enumerate(zip((0, 1, 3, 4), lon_mates))
    ]
    for copy in along_lon:
        copy.start()

    for copy in along_lon:
        copy.wait_recv()
    choices[...] = dot(tt[...].reshape(80, 128), copies[...])

    def chosen(choice, first_tile):
        total = jnp.zeros((16, 128), F32)
        for j in range(3 * BLK_DEV):
            t, q = first_tile + j // BLK_DEV, j % BLK_DEV
            total = jnp.where(choice == j, choices[t * 16 : t * 16 + 16, q * 128 : (q + 1) * 128], total)
        return total

    blocks = chosen(own_choice, 1).astype(BF16)

    four = jnp.concatenate([remap_v[:, 0:256], remap_v[:, 768:1024]], axis=1)
    four = dot(blocks, four)
    is_odd = odd == 1
    mate_out[0] = jnp.where(is_odd, four[:, 0:128], four[:, 384:512])
    mate_out[1] = jnp.where(is_odd, four[:, 128:256], four[:, 256:384])
    next_out[...] = jnp.where(is_odd, four[:, 256:384], four[:, 128:256])
    send(mate_out, mate_in, core_mate, 2, 3)
    send(next_out, next_in, far_mate, 9, 12)

    spread_blocks = dot(blocks, spread_var, ((0,), (0,))).astype(BF16)
    fine = dot(remap_v[...], spread_blocks, ((0,), (0,)))
    high, low = split(fine)
    packed = jnp.where(part_l == 1, low.astype(F32), high.astype(F32)).astype(BF16)
    xs[2:10] = packed.reshape(ROWS_DEV, COLS_DEV, 128)

    third = jnp.broadcast_to(lane, (128, 128))

    def patches(before, here, after, lanes):
        before = jnp.where(lanes < 3 * VARS, before.astype(F32), 0.0)
        here = jnp.where((lanes >= 3 * VARS) & (lanes < 6 * VARS), here.astype(F32), 0.0)
        after = jnp.where(lanes >= 6 * VARS, after.astype(F32), 0.0)
        return (before + here + after).astype(BF16)

    def taps(out_rows):
        field = [patches(xs[i], xs[i + 1], xs[i + 2], third) for i in out_rows]
        result = dot(jnp.concatenate(field, axis=0), wa[...])
        for n, i in enumerate(out_rows):
            for dx in range(3):
                gs[dx, i, MAIN:RIGHT, :] = result[n * 128 : (n + 1) * 128, dx * CH : (dx + 1) * CH]

    def joined(i, first, size):
        return gs[0, i, first - 1 : first - 1 + size, :] + gs[1, i, first : first + size, :] + gs[2, i, first + 1 : first + 1 + size, :]

    taps(list(range(2, 8)))

    def placed(fine):
        high, low = split(fine)
        return dot(jnp.concatenate([high, low], axis=0), spread_msg, ((0,), (0,))).astype(BF16)

    pltpu.make_async_copy(mate_in, mate_in, recv_sem.at[3]).wait()
    xs[10 - 9 * odd] = placed(mate_in[0])
    xs[11 - 11 * odd] = placed(mate_in[1])

    pltpu.make_async_copy(col_in, col_in, recv_sem.at[2]).wait()
    pltpu.make_async_copy(corner_in, corner_in, recv_sem.at[1]).wait()
    pltpu.make_async_copy(row_in, row_in, recv_sem.at[0]).wait()
    far_known = jnp.where(is_odd, not_last, not_first)

    def fine_of(cells, choice, first_tile, known):
        held = chosen(choice.astype(F32), first_tile) * known
        return dot(cells, held.astype(BF16), ((1,), (1,)))

    parts = [
        fine_of(row_in[0:128, :], row_in[128:129, :], 1, far_known),
        fine_of(col_in[0, 0:16, :], col_in[0, 16:17, :], 0, 1.0),
        fine_of(col_in[1, 0:16, :], col_in[1, 16:17, :], 2, 1.0),
    ]
    for i, (first_tile, known) in enumerate(((0, not_first), (0, not_last), (2, not_first), (2, not_last))):
        parts.append(fine_of(corner_in[i], corner_in[i, 8:9, :], first_tile, known))
    high, low = split(jnp.concatenate(parts, axis=0))
    cells = dot(jnp.concatenate([high, low], axis=1), spread_msg)
    xs[1 + 9 * odd] = cells[0:128].astype(BF16)
    for i, first in enumerate((6, 0)):
        for n in range(16):
            line = ((n & 7) + 2) * 8 + first + (n >> 3)
            side[line : line + 1, :] = cells[128 + 16 * i + n : 129 + 16 * i + n]
    for i, first in enumerate((6, 86, 0, 80)):
        for n in range(4):
            line = first + (n >> 1) * 8 + (n & 1)
            side[line : line + 1, :] = cells[160 + 16 * i + n : 161 + 16 * i + n]
    edge = side[...].reshape(12, 8, 128)
    side_lane = jnp.broadcast_to(lane.reshape(1, 1, 128), (10, 8, 128))
    side_patches = patches(edge[0:10], edge[1:11], edge[2:12], side_lane).reshape(80, 128)
    side_taps = dot(side_patches, wa[...]).reshape(10, 8, 3 * CH)
    for dx in range(3):
        piece = side_taps[:, :, dx * CH : (dx + 1) * CH]
        gs[dx, :, LEFT:MAIN, :] = piece
        gs[dx, :, RIGHT : RIGHT + 8, :] = piece
    taps([1, 8])
    for i in range(1, 9):
        ha[i, MAIN:RIGHT, :] = joined(i, MAIN, 128)

    def all_reduce(turn, mean, dev, beside):
        cells = ROWS_DEV * COLS_DEV
        for stage, (mates, buf) in enumerate(((z_mates, buf_z), (xy_mates, buf_x))):
            sem = 4 + turn * 2 + stage
            stat[turn, stage, 0:1, :] = mean
            stat[turn, stage, 1:2, :] = dev
            for j, mate in enumerate(mates):
                pltpu.make_async_remote_copy(
                    src_ref=stat.at[turn, stage], dst_ref=buf.at[turn, j], send_sem=send_sem.at[sem - 1], recv_sem=recv_sem.at[sem],
                    device_id=mate, device_id_type=MESH,
                ).start()
            if stage == 0:
                beside()
            pltpu.make_async_copy(buf.at[turn], buf.at[turn], recv_sem.at[sem]).wait()
            mean, dev = merge(mean, dev, buf[turn], cells)
            cells = cells * (len(mates) + 1)
        return to_groups(mean, dev, cells)

    def around_a():
        for load in loads[3:]:
            load.wait()
        prepare_b(cb_v, wba, wbb)
        pltpu.make_async_copy(next_in, next_in, recv_sem.at[12]).wait()
        xs[11 * odd] = placed(next_in[...] * far_known)
        taps([0, 9])
        for i in (0, 9):
            ha[i, MAIN:RIGHT, :] = joined(i, MAIN, 128)
        for i in range(10):
            hl[0, i : i + 1, :] = joined(i, MAIN - 1, 1)
            hl[1, i : i + 1, :] = joined(i, RIGHT, 1)

    mean, dev = local_stats([ha[i, MAIN:RIGHT, :] for i in range(1, 9)])
    mean, inverse = all_reduce(0, mean, dev, around_a)

    second_conv(ha, hl, act, gs, hb, wba, wbb, mean, inverse * vec_v[0], vec_v[1], not_first, not_last)
    store = pltpu.make_async_copy(hb, hb_ref, out_sem)
    store.start()
    mean, dev = local_stats([hb[i] for i in range(8)])
    mean, inverse = all_reduce(1, mean, dev, lambda: None)
    fin_ref[0:1, :] = mean
    fin_ref[1:2, :] = inverse * vec_v[2]
    fin_ref[2:3, :] = vec_v[3]
    store.wait()

    pltpu.make_async_copy(row_in, row_in, send_sem.at[0]).wait()
    pltpu.make_async_copy(corner_in, corner_in, send_sem.at[1]).wait()
    pltpu.make_async_copy(col_in, col_in, send_sem.at[8]).wait()
    pltpu.make_async_copy(mate_in, mate_in, send_sem.at[2]).wait()
    pltpu.make_async_copy(next_in, next_in, send_sem.at[9]).wait()
    pltpu.make_async_copy(tt.at[pl.ds(0, 4)], tt.at[pl.ds(0, 4)], send_sem.at[7]).wait()
    for turn in range(2):
        pltpu.make_async_copy(buf_z.at[turn], buf_z.at[turn], send_sem.at[3 + 2 * turn]).wait()
        pltpu.make_async_copy(buf_x.at[turn], buf_x.at[turn], send_sem.at[4 + 2 * turn]).wait()


def per_device(
    coarse, src_blocks, slot_counts, remap_tiles, conv_a, conv_b, gain_a, shift_a, gain_b, shift_b
):
    anywhere = pl.BlockSpec(memory_space=pl.ANY)
    vectors = [v.reshape(1, CH) for v in (gain_a, shift_a, gain_b, shift_b)]
    hidden, final = pl.pallas_call(
        kernel,
        name="stem",
        out_shape=(
            pltpu.VMEM((ROWS_DEV, COLS_DEV, CH), F32),
            pltpu.VMEM((3, CH), F32),
        ),
        in_specs=[anywhere, pl.BlockSpec(memory_space=pltpu.SMEM)] + [anywhere] * 8,
        out_specs=(anywhere, pl.BlockSpec(memory_space=pltpu.VMEM)),
        scratch_shapes=[
            pltpu.SMEM((1, SLOTS), jnp.int32),
            pltpu.VMEM((VARS, BLK_DEV, BCELLS), BF16),
            pltpu.VMEM((128, 1024), BF16),
            pltpu.VMEM((3, 3, VARS, CH), F32),
            pltpu.VMEM((3, 3, CH, CH), F32),
            pltpu.VMEM((4, 1, CH), F32),
            pltpu.VMEM((5, 16, 128), BF16),
            pltpu.VMEM((144, 128), BF16),
            pltpu.VMEM((2, 32, 128), BF16),
            pltpu.VMEM((4, 16, 128), BF16),
            pltpu.VMEM((2, 16, 128), F32),
            pltpu.VMEM((16, 128), F32),
            pltpu.VMEM((144, 128), BF16),
            pltpu.VMEM((2, 32, 128), BF16),
            pltpu.VMEM((4, 16, 128), BF16),
            pltpu.VMEM((2, 16, 128), F32),
            pltpu.VMEM((16, 128), F32),
            pltpu.VMEM((128, BLK_DEV * 128), BF16),
            pltpu.VMEM((80, BLK_DEV * 128), F32),
            pltpu.VMEM((96, 128), F32),
            pltpu.VMEM((128, 3 * CH), F32),
            pltpu.VMEM((128, 3 * CH), BF16),
            pltpu.VMEM((9 * CH, 2 * CH), BF16),
            pltpu.VMEM((6 * CH, 2 * CH), BF16),
            pltpu.VMEM((12, COLS_DEV, 128), BF16),
            pltpu.VMEM((3, 10, WIDE, CH), F32),
            pltpu.VMEM((10, WIDE, CH), F32),
            pltpu.VMEM((2, 24, CH), F32),
            pltpu.VMEM((10, COLS_DEV, 2 * CH), BF16),
            pltpu.VMEM((ROWS_DEV, COLS_DEV, CH), F32),
            pltpu.VMEM((2, 2, 2, CH), F32),
            pltpu.VMEM((2, 15, 2, CH), F32),
            pltpu.VMEM((2, 31, 2, CH), F32),
            pltpu.SemaphoreType.DMA((9,)),
            pltpu.SemaphoreType.DMA,
            pltpu.SemaphoreType.DMA((10,)),
            pltpu.SemaphoreType.DMA((13,)),
        ],
        compiler_params=pltpu.CompilerParams(
            collective_id=0, has_side_effects=True, vmem_limit_bytes=60 * 1024 * 1024
        ),
    )(
        src_blocks, slot_counts, jnp.transpose(coarse, (1, 0, 2)), remap_tiles.reshape(SLOTS * BCELLS, 1024),
        conv_a, conv_b, *vectors,
    )
    normed = (hidden - final[0]) * final[1] + final[2]
    return jax.nn.silu(normed).astype(BF16)


def solution(mesh):
    return jax.shard_map(
        per_device,
        mesh=mesh,
        in_specs=(
            P("lon", None, None),
            P(("row", "lon"), None),
            P(("row", "lon")),
            P(("row", "lon"), None, None, None),
            P(),
            P(),
            P(),
            P(),
            P(),
            P(),
        ),
        out_specs=P("row", "lon", None),
        check_vma=False,
    )
```

```python
import jax
import jax.numpy as jnp
from jax import lax
from jax.experimental import pallas as pl
from jax.experimental.pallas import tpu as pltpu
from jax.sharding import PartitionSpec as P

ROWS_DEV = 8
COLS_DEV = 128
VARS = 12
CH = 128
GROUPS = 32
SLOTS = 4
BCELLS = 32
BLK_DEV = 4
NBLK = 128
PER_GROUP = CH // GROUPS
MESH = pl.DeviceIdType.MESH
F32 = jnp.float32
BF16 = jnp.bfloat16

eps = 1e-05


def coords():
    row = lax.axis_index("row")
    lon = lax.axis_index("lon")
    core = lax.rem(row, 2)
    z_hi = lax.rem(lax.div(row, 2), 2)
    x = lax.div(row, 4)
    y = lax.div(lon, 8)
    z = z_hi * 8 + lax.rem(lon, 8)
    return row, lon, x, y, z, core


def device_at(x, y, z, core):
    return (x * 4 + lax.div(z, 8) * 2 + core, y * 8 + lax.rem(z, 8))


def moved(value, step, count):
    return lax.rem(value + step, count) if step else value


def along_z(place):
    _, _, x, y, z, core = place
    steps = [(d, c) for d in range(16) for c in range(2) if d or c]
    steps.sort(key=lambda s: -min(s[0], 16 - s[0]))
    return [device_at(x, y, moved(z, d, 16), moved(core, c, 2)) for d, c in steps]


def across(place):
    _, _, x, y, z, core = place
    steps = [(a, b) for a in range(4) for b in range(4) if a or b]
    steps.sort(key=lambda s: -(min(s[0], 4 - s[0]) + min(s[1], 4 - s[1])))
    return [device_at(moved(x, a, 4), moved(y, b, 4), z, core) for a, b in steps]


def coarse_mates(place):
    _, _, x, y, z, core = place
    z_lo = lax.rem(z, 8)
    mates = []
    for step in (2, 1, -1, -2):
        turn = lax.rem(y + 3 + lax.div(z_lo + 8 + step, 8), 4)
        mates.append(device_at(x, turn, lax.rem(z + 16 + step, 16), core))
    return mates


def iota(shape, dim):
    return lax.broadcasted_iota(jnp.int32, shape, dim)


def split(value):
    high = value.astype(BF16)
    low = (value - high.astype(F32)).astype(BF16)
    return high, low


def dot(a, b, dims=((1,), (0,))):
    return lax.dot_general(a, b, (dims, ((), ())), preferred_element_type=F32)


def over_group(row):
    place = iota(row.shape, 1) & (PER_GROUP - 1)
    total = row
    for step in range(1, PER_GROUP):
        after = pltpu.roll(row, CH - step, 1)
        before = pltpu.roll(row, step, 1)
        total = total + jnp.where(place < PER_GROUP - step, after, 0.0) + jnp.where(place >= step, before, 0.0)
    return total


def local_stats(rows, extra=()):
    size = rows[0].shape[0]
    about = jnp.sum(rows[0], axis=0, keepdims=True) * (1.0 / size)
    first, second = 0.0, 0.0
    lines = jnp.asarray(len(rows), F32)
    for r in rows:
        off = r - about
        first = first + off
        second = second + off * off
    for r, counts in extra:
        off = jnp.where(counts, r - about, 0.0)
        first = first + off
        second = second + off * off
        lines = lines + jnp.where(counts, 1.0, 0.0)
    cells = jnp.full((1, CH), lines * size)
    first = jnp.sum(first, axis=0, keepdims=True)
    mean_off = first / cells
    dev = jnp.sum(second, axis=0, keepdims=True) - first * mean_off
    return about + mean_off, dev, cells


def to_groups(mean, dev, cells):
    whole = over_group(mean) * (1.0 / PER_GROUP)
    apart = mean - whole
    spread = over_group(dev + cells * (apart * apart)) * (1.0 / (cells * PER_GROUP))
    return whole, lax.rsqrt(spread + eps)


def merge(mean, dev, cells, others):
    means, devs, counts = others[:, 0:1, :], others[:, 1:2, :], others[:, 2:3, :]
    every = cells + jnp.sum(counts, axis=0)
    whole = (mean * cells + jnp.sum(means * counts, axis=0)) / every
    off = means - whole
    own = mean - whole
    spread = own * own * cells + jnp.sum(off * off * counts, axis=0)
    return whole, dev + jnp.sum(devs, axis=0) + spread, every


LEFT, MAIN, RIGHT, WIDE = 8, 16, 144, 160


def prepare_b(cb_v, wba, wbb):
    for dy in range(3):
        for dx in range(2):
            span = slice(dx * CH, (dx + 1) * CH)
            high, low = split(cb_v[dy, dx])
            wba[dy * 256 : dy * 256 + 128, span] = high
            wba[dy * 256 + 128 : dy * 256 + 256, span] = high
            wba[768 + dy * 128 : 896 + dy * 128, span] = low
        high, low = split(cb_v[dy, 2])
        for part, value in enumerate((high, high, low)):
            if dy < 2:
                wbb[part * 256 + dy * 128 : part * 256 + dy * 128 + 128, 0:CH] = value
            else:
                wbb[part * 256 : part * 256 + 128, CH : 2 * CH] = jnp.zeros((CH, CH), BF16)
                wbb[part * 256 + 128 : part * 256 + 256, CH : 2 * CH] = value


def activate(value, mean, scale, shift):
    half = ((value - mean) * scale + shift) * 0.5
    return half + half * jnp.tanh(half)


def second_conv(ha, hl, act, gs, hb, wba, wbb, mean, scale, shift, not_first, not_last):
    for i in range(10):
        value = activate(ha[i, MAIN:RIGHT, :], mean, scale, shift)
        if i == 0:
            value = value * not_first
        if i == 9:
            value = value * not_last
        act[i, :, 0:128], act[i, :, 128:256] = split(value)
    known = iota((16, 1), 0)
    known = jnp.where(known == 0, not_first, jnp.where(known == 9, not_last, 1.0))
    for i in range(2):
        hl[i, 0:16, :] = activate(hl[i, 0:16, :], mean, scale, shift) * known

    def side(i, dy):
        return split(hl[i, dy : dy + 16, :])

    def rows(first, size, part):
        return act[first : first + size, :, part * 128 : part * 128 + 128].reshape(size * 128, 128)

    pieces = [act[dy : dy + 8].reshape(1024, 256) for dy in range(3)] + [rows(dy, 8, 0) for dy in range(3)]
    at_side = [side(0, dy) for dy in range(3)]
    at_side = [part for pair in at_side for part in pair] + [pair[0] for pair in at_side]
    field = jnp.concatenate([jnp.concatenate(pieces, axis=1), jnp.concatenate(at_side, axis=1)], axis=0)
    early = dot(field, wba[...])

    pieces = [rows(0, 9, 0), rows(1, 9, 0), rows(0, 9, 1), rows(1, 9, 1), rows(0, 9, 0), rows(1, 9, 0)]
    (high0, low0), (high1, low1) = side(1, 0), side(1, 1)
    at_side = [high0, high1, low0, low1, high0, high1]
    field = jnp.concatenate([jnp.concatenate(pieces, axis=1), jnp.concatenate(at_side, axis=1)], axis=0)
    late = dot(field, wbb[...])

    for i in range(8):
        gs[0, i, MAIN:RIGHT, :] = early[i * 128 : (i + 1) * 128, 0:128]
        gs[0, i, MAIN - 1 : MAIN, :] = early[1024 + i : 1025 + i, 0:128]
        gs[2, i, MAIN:RIGHT, :] = late[i * 128 : (i + 1) * 128, 0:128] + late[(i + 1) * 128 : (i + 2) * 128, 128:256]
        gs[2, i, RIGHT : RIGHT + 1, :] = late[1152 + i : 1153 + i, 0:128] + late[1153 + i : 1154 + i, 128:256]
        hb[i] = gs[0, i, MAIN - 1 : RIGHT - 1, :] + early[i * 128 : (i + 1) * 128, 128:256] + gs[2, i, MAIN + 1 : RIGHT + 1, :]


def kernel(
    src_hbm, cnt_ref, coarse_ref, remap_ref, ca_ref, cb_ref, gain_a_ref, shift_a_ref, gain_b_ref, shift_b_ref,
    hb_ref, fin_ref,
    src_ref, coarse_v, remap_v, ca_v, cb_v, vec_v,
    tt, row_out, col_out, corner_out, mate_out,
    row_in, col_in, corner_in, mate_in,
    copies, choices, side, wa32, wa, wba, wbb,
    xs, gs, ha, hl, act, hb,
    stat, buf_x, buf_z,
    in_sem, out_sem, send_sem, recv_sem,
):
    place = coords()
    row, lon = place[0], place[1]
    z_mates = along_z(place)
    xy_mates = across(place)
    lon_mates = coarse_mates(place)
    lon_left, lon_right = lax.rem(lon + 31, 32), lax.rem(lon + 1, 32)
    odd = lax.rem(row, 2)
    is_odd = odd == 1
    early = lax.rem(lax.div(row, 2), 2) == 0
    near_row = row + 1 - 2 * odd
    far_row = lax.rem(row + 2 * odd + 15, 16)
    halo = [
        (far_row, lon), (far_row, lon_right), (far_row, lon_left), (near_row, lon),
        (near_row, lon_right), (near_row, lon_left), (row, lon_right), (row, lon_left),
    ]
    barrier = pltpu.get_barrier_semaphore()
    partners = halo + lon_mates + z_mates + xy_mates
    for mate in partners:
        pl.semaphore_signal(barrier, inc=1, device_id=mate, device_id_type=MESH)

    loads = [
        pltpu.make_async_copy(coarse_ref, coarse_v, in_sem.at[0]),
        pltpu.make_async_copy(remap_ref, remap_v, in_sem.at[1]),
        pltpu.make_async_copy(ca_ref, ca_v, in_sem.at[2]),
        pltpu.make_async_copy(cb_ref, cb_v, in_sem.at[3]),
    ]
    for i, ref in enumerate((gain_a_ref, shift_a_ref, gain_b_ref, shift_b_ref)):
        loads.append(pltpu.make_async_copy(ref, vec_v.at[i], in_sem.at[4 + i]))
    sources = pltpu.make_async_copy(src_hbm, src_ref, in_sem.at[8])
    for load in [sources] + loads:
        load.start()

    sources.wait()
    lane = iota((1, 128), 1)
    own_choice = jnp.zeros((1, 128), F32)
    for k in range(SLOTS):
        local = lax.rem(src_ref[0, k] - (lon - 1) * BLK_DEV + 2 * NBLK, NBLK)
        local = jnp.where(k < cnt_ref[0], local, -64)
        own_choice = jnp.where((lane >> 5) == k, local.astype(F32), own_choice)
    choice_tile = jnp.broadcast_to(own_choice, (16, 128)).astype(BF16)

    for q in range(BLK_DEV):
        want = q * BCELLS + (lane & (BCELLS - 1))
        copies[:, q * 128 : (q + 1) * 128] = jnp.where(iota((128, 128), 0) == want, 1.0, 0.0).astype(BF16)

    loads[0].wait()
    held = coarse_v[...].astype(F32)
    tile = jnp.zeros((VARS, 128), F32)
    for b in range(BLK_DEV):
        put = jnp.where(iota((BCELLS, 128), 0) + b * BCELLS == iota((BCELLS, 128), 1), 1.0, 0.0)
        tile = tile + dot(held[:, b, :].astype(BF16), put.astype(BF16))
    pad = jnp.concatenate([tile, jnp.zeros((16 - VARS, 128), F32)], axis=0)
    tt[2] = pad.astype(BF16)

    loads[1].wait()
    at = iota((352, 1), 0)
    inner = at & 15
    cell = jnp.where(at < 128, at + odd * (7 * COLS_DEV), at + odd * (5 * COLS_DEV))
    column = (inner & 7) * COLS_DEV + (inner >> 3)
    cell = jnp.where((at >= 256) & (at < 272), column + 126, cell)
    cell = jnp.where((at >= 272) & (at < 288), column, cell)
    for i, (row0, col0) in enumerate(((6 * odd, 126), (6 * odd, 0), (6 - 6 * odd, 126), (6 - 6 * odd, 0))):
        here = jnp.where(inner < 4, (row0 + (inner >> 1)) * COLS_DEV + col0 + (inner & 1), -1)
        cell = jnp.where((at >= 288 + 16 * i) & (at < 304 + 16 * i), here, cell)
    pick = jnp.where(iota((352, 1024), 1) == cell, 1.0, 0.0).astype(BF16)
    weights = dot(pick, remap_v[...], ((1,), (1,))).astype(BF16)
    row_out[0:256, :] = weights[0:256]
    row_out[256:272, :] = choice_tile
    for i in range(2):
        col_out[i, 0:16, :] = weights[256 + 16 * i : 272 + 16 * i]
        col_out[i, 16:32, :] = choice_tile
    for i in range(4):
        cells = weights[288 + 16 * i : 304 + 16 * i].astype(F32)
        corner_out[i] = jnp.where(iota((16, 128), 0) < 8, cells, own_choice).astype(BF16)
    side[...] = jnp.zeros_like(side)
    hl[...] = jnp.zeros_like(hl)
    xs[...] = jnp.zeros_like(xs)

    loads[2].wait()
    wa32[...] = jnp.zeros_like(wa32)
    for dy in range(3):
        for part in range(3):
            first = (dy * 3 + part) * VARS
            for dx in range(3):
                wa32[first : first + VARS, dx * CH : (dx + 1) * CH] = ca_v[dy, dx]
    line = iota((128, 3 * CH), 0)
    twelfth = (line * 43) >> 9
    part_of = twelfth - 3 * ((twelfth * 11) >> 5)
    whole = wa32[...]
    high, low = split(whole)
    wa[...] = jnp.where(part_of == 2, low.astype(F32), high.astype(F32)).astype(BF16)

    twelfth_l = (lane * 43) >> 9
    var_l = jnp.where(lane < 9 * VARS, lane - 12 * twelfth_l, 4096)
    part_l = twelfth_l - 3 * ((twelfth_l * 11) >> 5)
    want = jnp.where(part_l == 1, var_l + 16, var_l)
    spread_msg = jnp.where(iota((32, 128), 0) == want, 1.0, 0.0).astype(BF16)
    spread_var = jnp.where(iota((16, 128), 0) == var_l, 1.0, 0.0).astype(BF16)
    not_first = jnp.where(row > 0, 1.0, 0.0).astype(F32)
    not_last = jnp.where(row < 15, 1.0, 0.0).astype(F32)

    pl.semaphore_wait(barrier, len(partners))

    def send(src, dst, mate, out, into):
        copy = pltpu.make_async_remote_copy(
            src_ref=src, dst_ref=dst, send_sem=send_sem.at[out], recv_sem=recv_sem.at[into],
            device_id=mate, device_id_type=MESH,
        )
        copy.start()

    send(row_out, row_in, halo[0], 0, 0)
    for i in range(2):
        send(corner_out.at[i], corner_in.at[i], halo[1 + i], 1, 1)
    for i in range(2):
        send(col_out.at[i], col_in.at[i], halo[6 + i], 8, 2)
    for i in range(2):
        send(corner_out.at[2 + i], corner_in.at[2 + i], halo[4 + i], 9, 12)
    along_lon = [
        pltpu.make_async_remote_copy(
            src_ref=tt.at[2], dst_ref=tt.at[slot], send_sem=send_sem.at[7], recv_sem=recv_sem.at[8 + i],
            device_id=mate, device_id_type=MESH,
        )
        for i, (slot, mate) in enumerate(zip((0, 1, 3, 4), lon_mates))
    ]
    for copy in along_lon:
        copy.start()

    for copy in along_lon:
        copy.wait_recv()
    choices[...] = dot(tt[...].reshape(80, 128), copies[...])

    def chosen(choice, first_tile):
        total = jnp.zeros((16, 128), F32)
        for j in range(3 * BLK_DEV):
            t, q = first_tile + j // BLK_DEV, j % BLK_DEV
            total = jnp.where(choice == j, choices[t * 16 : t * 16 + 16, q * 128 : (q + 1) * 128], total)
        return total

    blocks = chosen(own_choice, 1).astype(BF16)

    four = jnp.concatenate([remap_v[:, 0:256], remap_v[:, 768:1024]], axis=1)
    four = dot(blocks, four)
    mate_out[0] = jnp.where(is_odd, four[:, 0:128], four[:, 384:512])
    mate_out[1] = jnp.where(is_odd, four[:, 128:256], four[:, 256:384])
    send(mate_out, mate_in, halo[3], 2, 3)

    spread_blocks = dot(blocks, spread_var, ((0,), (0,))).astype(BF16)
    fine = dot(remap_v[...], spread_blocks, ((0,), (0,)))
    high, low = split(fine)
    packed = jnp.where(part_l == 1, low.astype(F32), high.astype(F32)).astype(BF16)
    xs[2:10] = packed.reshape(ROWS_DEV, COLS_DEV, 128)

    third = jnp.broadcast_to(lane, (128, 128))

    def patches(before, here, after, lanes):
        before = jnp.where(lanes < 3 * VARS, before.astype(F32), 0.0)
        here = jnp.where((lanes >= 3 * VARS) & (lanes < 6 * VARS), here.astype(F32), 0.0)
        after = jnp.where(lanes >= 6 * VARS, after.astype(F32), 0.0)
        return (before + here + after).astype(BF16)

    def taps(out_rows):
        field = [patches(xs[i], xs[i + 1], xs[i + 2], third) for i in out_rows]
        result = dot(jnp.concatenate(field, axis=0), wa[...])
        for n, i in enumerate(out_rows):
            for dx in range(3):
                gs[dx, i, MAIN:RIGHT, :] = result[n * 128 : (n + 1) * 128, dx * CH : (dx + 1) * CH]

    def joined(i, first, size):
        return gs[0, i, first - 1 : first - 1 + size, :] + gs[1, i, first : first + size, :] + gs[2, i, first + 1 : first + 1 + size, :]

    taps(list(range(2, 8)))

    def placed(fine):
        high, low = split(fine)
        return dot(jnp.concatenate([high, low], axis=0), spread_msg, ((0,), (0,))).astype(BF16)

    pltpu.make_async_copy(mate_in, mate_in, recv_sem.at[3]).wait()
    xs[10 - 9 * odd] = placed(mate_in[0])
    xs[11 - 11 * odd] = placed(mate_in[1])

    far_known = jnp.where(is_odd, not_last, not_first)
    has_far = far_known > 0.5

    def fine_of(cells, choice, first_tile, known):
        held = chosen(choice.astype(F32), first_tile) * known
        return dot(cells, held.astype(BF16), ((1,), (1,)))

    def spread_cells(parts):
        high, low = split(jnp.concatenate(parts, axis=0))
        return dot(jnp.concatenate([high, low], axis=1), spread_msg)

    def put_corner(cells, first_row, place):
        for n in range(4):
            side[first_row + (n >> 1), place + (n & 1) : place + (n & 1) + 1, :] = cells[n : n + 1]

    def far_edges():
        pltpu.make_async_copy(corner_in.at[pl.ds(0, 2)], corner_in.at[pl.ds(0, 2)], recv_sem.at[1]).wait()
        pltpu.make_async_copy(row_in, row_in, recv_sem.at[0]).wait()
        cells = spread_cells([
            fine_of(row_in[0:256, :], row_in[256:257, :], 1, far_known),
            fine_of(corner_in[0], corner_in[0, 8:9, :], 0, far_known),
            fine_of(corner_in[1], corner_in[1, 8:9, :], 2, far_known),
        ])
        xs[1 + 9 * odd] = cells[0:128].astype(BF16)
        xs[11 * odd] = cells[128:256].astype(BF16)
        put_corner(cells[256:272], 10 * odd, 6)
        put_corner(cells[272:288], 10 * odd, 0)

    pltpu.make_async_copy(col_in, col_in, recv_sem.at[2]).wait()
    pltpu.make_async_copy(corner_in.at[pl.ds(2, 2)], corner_in.at[pl.ds(2, 2)], recv_sem.at[12]).wait()
    cells = spread_cells([
        fine_of(col_in[0, 0:16, :], col_in[0, 16:17, :], 0, 1.0),
        fine_of(col_in[1, 0:16, :], col_in[1, 16:17, :], 2, 1.0),
        fine_of(corner_in[2], corner_in[2, 8:9, :], 0, 1.0),
        fine_of(corner_in[3], corner_in[3, 8:9, :], 2, 1.0),
    ])
    for i, place_at in enumerate((6, 0)):
        for n in range(16):
            at_col = place_at + (n >> 3)
            side[(n & 7) + 2, at_col : at_col + 1, :] = cells[16 * i + n : 16 * i + n + 1]
    put_corner(cells[32:48], 10 - 10 * odd, 6)
    put_corner(cells[48:64], 10 - 10 * odd, 0)
    near_border, far_border, far_beyond = 8 - 7 * odd, 1 + 7 * odd, 9 * odd
    taps([near_border])

    def far_rows():
        taps([far_border, far_beyond])
        side_lane = jnp.broadcast_to(lane.reshape(1, 1, 128), (10, 8, 128))
        side_patches = patches(side[0:10], side[1:11], side[2:12], side_lane).reshape(80, 128)
        side_taps = dot(side_patches, wa[...]).reshape(10, 8, 3 * CH)
        for dx in range(3):
            piece = side_taps[:, :, dx * CH : (dx + 1) * CH]
            gs[dx, :, LEFT:MAIN, :] = piece
            gs[dx, :, RIGHT : RIGHT + 8, :] = piece
        for i in (far_border, far_beyond):
            ha[i, MAIN:RIGHT, :] = joined(i, MAIN, 128)

    pl.when(early)(far_edges)
    far_rows()
    for i in range(2, 8):
        ha[i, MAIN:RIGHT, :] = joined(i, MAIN, 128)
    ha[near_border, MAIN:RIGHT, :] = joined(near_border, MAIN, 128)

    def all_reduce(turn, mean, dev, cells, beside):
        for stage, (mates, buf) in enumerate(((z_mates, buf_z), (xy_mates, buf_x))):
            sem = 4 + turn * 2 + stage
            stat[turn, stage, 0:1, :] = mean
            stat[turn, stage, 1:2, :] = dev
            stat[turn, stage, 2:3, :] = cells
            for j, mate in enumerate(mates):
                pltpu.make_async_remote_copy(
                    src_ref=stat.at[turn, stage], dst_ref=buf.at[turn, j], send_sem=send_sem.at[sem - 1], recv_sem=recv_sem.at[sem],
                    device_id=mate, device_id_type=MESH,
                ).start()
            if stage == 0:
                beside()
            pltpu.make_async_copy(buf.at[turn], buf.at[turn], recv_sem.at[sem]).wait()
            mean, dev, cells = merge(mean, dev, cells, buf[turn])
        return to_groups(mean, dev, cells)

    def around_a():
        for load in loads[3:]:
            load.wait()
        prepare_b(cb_v, wba, wbb)
        pl.when(jnp.logical_not(early))(far_edges)
        far_rows()
        near_beyond = 9 - 9 * odd
        taps([near_beyond])
        ha[near_beyond, MAIN:RIGHT, :] = joined(near_beyond, MAIN, 128)
        for i in range(10):
            hl[0, i : i + 1, :] = joined(i, MAIN - 1, 1)
            hl[1, i : i + 1, :] = joined(i, RIGHT, 1)

    mean, dev, cells = local_stats(
        [ha[i, MAIN:RIGHT, :] for i in range(2, 8)] + [ha[near_border, MAIN:RIGHT, :]],
        [
            (ha[far_border, MAIN:RIGHT, :], jnp.logical_or(early, jnp.logical_not(has_far))),
            (ha[far_beyond, MAIN:RIGHT, :], jnp.logical_and(early, has_far)),
        ],
    )
    mean, inverse = all_reduce(0, mean, dev, cells, around_a)

    second_conv(ha, hl, act, gs, hb, wba, wbb, mean, inverse * vec_v[0], vec_v[1], not_first, not_last)
    store = pltpu.make_async_copy(hb, hb_ref, out_sem)
    store.start()
    mean, dev, cells = local_stats([hb[i] for i in range(8)])
    mean, inverse = all_reduce(1, mean, dev, cells, lambda: None)
    fin_ref[0:1, :] = mean
    fin_ref[1:2, :] = inverse * vec_v[2]
    fin_ref[2:3, :] = vec_v[3]
    store.wait()

    pltpu.make_async_copy(row_in, row_in, send_sem.at[0]).wait()
    pltpu.make_async_copy(corner_in.at[pl.ds(0, 2)], corner_in.at[pl.ds(0, 2)], send_sem.at[1]).wait()
    pltpu.make_async_copy(corner_in.at[pl.ds(2, 2)], corner_in.at[pl.ds(2, 2)], send_sem.at[9]).wait()
    pltpu.make_async_copy(col_in, col_in, send_sem.at[8]).wait()
    pltpu.make_async_copy(mate_in, mate_in, send_sem.at[2]).wait()
    pltpu.make_async_copy(tt.at[pl.ds(0, 4)], tt.at[pl.ds(0, 4)], send_sem.at[7]).wait()
    for turn in range(2):
        pltpu.make_async_copy(buf_z.at[turn], buf_z.at[turn], send_sem.at[3 + 2 * turn]).wait()
        pltpu.make_async_copy(buf_x.at[turn], buf_x.at[turn], send_sem.at[4 + 2 * turn]).wait()


def per_device(
    coarse, src_blocks, slot_counts, remap_tiles, conv_a, conv_b, gain_a, shift_a, gain_b, shift_b
):
    anywhere = pl.BlockSpec(memory_space=pl.ANY)
    vectors = [v.reshape(1, CH) for v in (gain_a, shift_a, gain_b, shift_b)]
    hidden, final = pl.pallas_call(
        kernel,
        name="stem",
        out_shape=(
            pltpu.VMEM((ROWS_DEV, COLS_DEV, CH), F32),
            pltpu.VMEM((3, CH), F32),
        ),
        in_specs=[anywhere, pl.BlockSpec(memory_space=pltpu.SMEM)] + [anywhere] * 8,
        out_specs=(anywhere, pl.BlockSpec(memory_space=pltpu.VMEM)),
        scratch_shapes=[
            pltpu.SMEM((1, SLOTS), jnp.int32),
            pltpu.VMEM((VARS, BLK_DEV, BCELLS), BF16),
            pltpu.VMEM((128, 1024), BF16),
            pltpu.VMEM((3, 3, VARS, CH), F32),
            pltpu.VMEM((3, 3, CH, CH), F32),
            pltpu.VMEM((4, 1, CH), F32),
            pltpu.VMEM((5, 16, 128), BF16),
            pltpu.VMEM((272, 128), BF16),
            pltpu.VMEM((2, 32, 128), BF16),
            pltpu.VMEM((4, 16, 128), BF16),
            pltpu.VMEM((2, 16, 128), F32),
            pltpu.VMEM((272, 128), BF16),
            pltpu.VMEM((2, 32, 128), BF16),
            pltpu.VMEM((4, 16, 128), BF16),
            pltpu.VMEM((2, 16, 128), F32),
            pltpu.VMEM((128, BLK_DEV * 128), BF16),
            pltpu.VMEM((80, BLK_DEV * 128), F32),
            pltpu.VMEM((12, 8, 128), F32),
            pltpu.VMEM((128, 3 * CH), F32),
            pltpu.VMEM((128, 3 * CH), BF16),
            pltpu.VMEM((9 * CH, 2 * CH), BF16),
            pltpu.VMEM((6 * CH, 2 * CH), BF16),
            pltpu.VMEM((12, COLS_DEV, 128), BF16),
            pltpu.VMEM((3, 10, WIDE, CH), F32),
            pltpu.VMEM((10, WIDE, CH), F32),
            pltpu.VMEM((2, 24, CH), F32),
            pltpu.VMEM((10, COLS_DEV, 2 * CH), BF16),
            pltpu.VMEM((ROWS_DEV, COLS_DEV, CH), F32),
            pltpu.VMEM((2, 2, 3, CH), F32),
            pltpu.VMEM((2, 15, 3, CH), F32),
            pltpu.VMEM((2, 31, 3, CH), F32),
            pltpu.SemaphoreType.DMA((9,)),
            pltpu.SemaphoreType.DMA,
            pltpu.SemaphoreType.DMA((10,)),
            pltpu.SemaphoreType.DMA((13,)),
        ],
        compiler_params=pltpu.CompilerParams(
            collective_id=0, has_side_effects=True, vmem_limit_bytes=60 * 1024 * 1024
        ),
    )(
        src_blocks, slot_counts, jnp.transpose(coarse, (1, 0, 2)), remap_tiles.reshape(SLOTS * BCELLS, 1024),
        conv_a, conv_b, *vectors,
    )
    normed = (hidden - final[0]) * final[1] + final[2]
    return jax.nn.silu(normed).astype(BF16)


def solution(mesh):
    return jax.shard_map(
        per_device,
        mesh=mesh,
        in_specs=(
            P("lon", None, None),
            P(("row", "lon"), None),
            P(("row", "lon")),
            P(("row", "lon"), None, None, None),
            P(),
            P(),
            P(),
            P(),
            P(),
            P(),
        ),
        out_specs=P("row", "lon", None),
        check_vma=False,
    )
```

```python
import jax
import jax.numpy as jnp
from jax import lax
from jax.experimental import pallas as pl
from jax.experimental.pallas import tpu as pltpu
from jax.sharding import PartitionSpec as P

ROWS_DEV = 8
COLS_DEV = 128
VARS = 12
CH = 128
GROUPS = 32
SLOTS = 4
BCELLS = 32
BLK_DEV = 4
NBLK = 128
PER_GROUP = CH // GROUPS
MESH = pl.DeviceIdType.MESH
F32 = jnp.float32
BF16 = jnp.bfloat16

eps = 1e-05


def coords():
    row = lax.axis_index("row")
    lon = lax.axis_index("lon")
    core = lax.rem(row, 2)
    z_hi = lax.rem(lax.div(row, 2), 2)
    x = lax.div(row, 4)
    y = lax.div(lon, 8)
    z = z_hi * 8 + lax.rem(lon, 8)
    return row, lon, x, y, z, core


def device_at(x, y, z, core):
    return (x * 4 + lax.div(z, 8) * 2 + core, y * 8 + lax.rem(z, 8))


def moved(value, step, count):
    return lax.rem(value + step, count) if step else value


def along_z(place):
    _, _, x, y, z, core = place
    steps = [(d, c) for d in range(16) for c in range(2) if d or c]
    steps.sort(key=lambda s: -min(s[0], 16 - s[0]))
    return [device_at(x, y, moved(z, d, 16), moved(core, c, 2)) for d, c in steps]


def across(place):
    _, _, x, y, z, core = place
    steps = [(a, b) for a in range(4) for b in range(4) if a or b]
    steps.sort(key=lambda s: -(min(s[0], 4 - s[0]) + min(s[1], 4 - s[1])))
    return [device_at(moved(x, a, 4), moved(y, b, 4), z, core) for a, b in steps]


def coarse_mates(place):
    _, _, x, y, z, core = place
    z_lo = lax.rem(z, 8)
    mates = []
    for step in (2, 1, -1, -2):
        turn = lax.rem(y + 3 + lax.div(z_lo + 8 + step, 8), 4)
        mates.append(device_at(x, turn, lax.rem(z + 16 + step, 16), core))
    return mates


def iota(shape, dim):
    return lax.broadcasted_iota(jnp.int32, shape, dim)


def split(value):
    high = value.astype(BF16)
    low = (value - high.astype(F32)).astype(BF16)
    return high, low


def dot(a, b, dims=((1,), (0,))):
    return lax.dot_general(a, b, (dims, ((), ())), preferred_element_type=F32)


def over_group(row):
    place = iota(row.shape, 1) & (PER_GROUP - 1)
    total = row
    for step in range(1, PER_GROUP):
        after = pltpu.roll(row, CH - step, 1)
        before = pltpu.roll(row, step, 1)
        total = total + jnp.where(place < PER_GROUP - step, after, 0.0) + jnp.where(place >= step, before, 0.0)
    return total


def local_stats(rows):
    cells = len(rows) * rows[0].shape[0]
    about = jnp.sum(rows[0], axis=0, keepdims=True) * (1.0 / rows[0].shape[0])
    first, second = 0.0, 0.0
    for r in rows:
        off = r - about
        first = first + off
        second = second + off * off
    first = jnp.sum(first, axis=0, keepdims=True)
    mean_off = first * (1.0 / cells)
    dev = jnp.sum(second, axis=0, keepdims=True) - first * mean_off
    return about + mean_off, dev


def to_groups(mean, dev, cells):
    whole = over_group(mean) * (1.0 / PER_GROUP)
    apart = mean - whole
    spread = over_group(dev + cells * (apart * apart)) * (1.0 / (cells * PER_GROUP))
    return whole, lax.rsqrt(spread + eps)


def merge(mean, dev, others, cells):
    count = others.shape[0] + 1
    means = others[:, 0:1, :]
    whole = (mean + jnp.sum(means, axis=0)) * (1.0 / count)
    off = means - whole
    own = mean - whole
    spread = own * own + jnp.sum(off * off, axis=0)
    return whole, dev + jnp.sum(others[:, 1:2, :], axis=0) + cells * spread


LEFT, MAIN, RIGHT, WIDE = 8, 16, 144, 160


def prepare_b(cb_v, wba, wbb):
    for dy in range(3):
        for dx in range(2):
            span = slice(dx * CH, (dx + 1) * CH)
            high, low = split(cb_v[dy, dx])
            wba[dy * 256 : dy * 256 + 128, span] = high
            wba[dy * 256 + 128 : dy * 256 + 256, span] = high
            wba[768 + dy * 128 : 896 + dy * 128, span] = low
        high, low = split(cb_v[dy, 2])
        for part, value in enumerate((high, high, low)):
            if dy < 2:
                wbb[part * 256 + dy * 128 : part * 256 + dy * 128 + 128, 0:CH] = value
            else:
                wbb[part * 256 : part * 256 + 128, CH : 2 * CH] = jnp.zeros((CH, CH), BF16)
                wbb[part * 256 + 128 : part * 256 + 256, CH : 2 * CH] = value


def activate(value, mean, scale, shift):
    half = ((value - mean) * scale + shift) * 0.5
    return half + half * jnp.tanh(half)


def second_conv(ha, hl, act, gs, hb, wba, wbb, mean, scale, shift, not_first, not_last):
    for i in range(10):
        value = activate(ha[i, MAIN:RIGHT, :], mean, scale, shift)
        if i == 0:
            value = value * not_first
        if i == 9:
            value = value * not_last
        act[i, :, 0:128], act[i, :, 128:256] = split(value)
    known = iota((16, 1), 0)
    known = jnp.where(known == 0, not_first, jnp.where(known == 9, not_last, 1.0))
    for i in range(2):
        hl[i, 0:16, :] = activate(hl[i, 0:16, :], mean, scale, shift) * known

    def side(i, dy):
        return split(hl[i, dy : dy + 16, :])

    def rows(first, size, part):
        return act[first : first + size, :, part * 128 : part * 128 + 128].reshape(size * 128, 128)

    pieces = [act[dy : dy + 8].reshape(1024, 256) for dy in range(3)] + [rows(dy, 8, 0) for dy in range(3)]
    at_side = [side(0, dy) for dy in range(3)]
    at_side = [part for pair in at_side for part in pair] + [pair[0] for pair in at_side]
    field = jnp.concatenate([jnp.concatenate(pieces, axis=1), jnp.concatenate(at_side, axis=1)], axis=0)
    early = dot(field, wba[...])

    pieces = [rows(0, 9, 0), rows(1, 9, 0), rows(0, 9, 1), rows(1, 9, 1), rows(0, 9, 0), rows(1, 9, 0)]
    (high0, low0), (high1, low1) = side(1, 0), side(1, 1)
    at_side = [high0, high1, low0, low1, high0, high1]
    field = jnp.concatenate([jnp.concatenate(pieces, axis=1), jnp.concatenate(at_side, axis=1)], axis=0)
    late = dot(field, wbb[...])

    for i in range(8):
        gs[0, i, MAIN:RIGHT, :] = early[i * 128 : (i + 1) * 128, 0:128]
        gs[0, i, MAIN - 1 : MAIN, :] = early[1024 + i : 1025 + i, 0:128]
        gs[2, i, MAIN:RIGHT, :] = late[i * 128 : (i + 1) * 128, 0:128] + late[(i + 1) * 128 : (i + 2) * 128, 128:256]
        gs[2, i, RIGHT : RIGHT + 1, :] = late[1152 + i : 1153 + i, 0:128] + late[1153 + i : 1154 + i, 128:256]
        hb[i] = gs[0, i, MAIN - 1 : RIGHT - 1, :] + early[i * 128 : (i + 1) * 128, 128:256] + gs[2, i, MAIN + 1 : RIGHT + 1, :]


def kernel(
    src_hbm, cnt_ref, coarse_ref, remap_ref, ca_ref, cb_ref, gain_a_ref, shift_a_ref, gain_b_ref, shift_b_ref,
    hb_ref, fin_ref,
    src_ref, coarse_v, remap_v, ca_v, cb_v, vec_v,
    tt, row_out, col_out, corner_out, mate_out, far_out,
    row_in, col_in, corner_in, mate_in, far_in,
    copies, choices, side, wa32, wa, wba, wbb,
    xs, gs, ha, hl, act, hb,
    stat, buf_x, buf_z,
    in_sem, out_sem, send_sem, recv_sem,
):
    place = coords()
    row, lon = place[0], place[1]
    z_mates = along_z(place)
    xy_mates = across(place)
    lon_mates = coarse_mates(place)
    lon_left, lon_right = lax.rem(lon + 31, 32), lax.rem(lon + 1, 32)
    odd = lax.rem(row, 2)
    is_odd = odd == 1
    early = lax.rem(lax.div(row, 2), 2) == 0
    near_row = row + 1 - 2 * odd
    far_row = lax.rem(row + 2 * odd + 15, 16)
    halo = [
        (far_row, lon), (far_row, lon_right), (far_row, lon_left), (near_row, lon),
        (near_row, lon_right), (near_row, lon_left), (row, lon_right), (row, lon_left),
    ]
    barrier = pltpu.get_barrier_semaphore()
    partners = halo + lon_mates + z_mates + xy_mates
    for mate in partners:
        pl.semaphore_signal(barrier, inc=1, device_id=mate, device_id_type=MESH)

    loads = [
        pltpu.make_async_copy(coarse_ref, coarse_v, in_sem.at[0]),
        pltpu.make_async_copy(remap_ref, remap_v, in_sem.at[1]),
        pltpu.make_async_copy(ca_ref, ca_v, in_sem.at[2]),
        pltpu.make_async_copy(cb_ref, cb_v, in_sem.at[3]),
    ]
    for i, ref in enumerate((gain_a_ref, shift_a_ref, gain_b_ref, shift_b_ref)):
        loads.append(pltpu.make_async_copy(ref, vec_v.at[i], in_sem.at[4 + i]))
    sources = pltpu.make_async_copy(src_hbm, src_ref, in_sem.at[8])
    for load in [sources] + loads:
        load.start()

    sources.wait()
    lane = iota((1, 128), 1)
    own_choice = jnp.zeros((1, 128), F32)
    for k in range(SLOTS):
        local = lax.rem(src_ref[0, k] - (lon - 1) * BLK_DEV + 2 * NBLK, NBLK)
        local = jnp.where(k < cnt_ref[0], local, -64)
        own_choice = jnp.where((lane >> 5) == k, local.astype(F32), own_choice)
    choice_tile = jnp.broadcast_to(own_choice, (16, 128)).astype(BF16)

    for q in range(BLK_DEV):
        want = q * BCELLS + (lane & (BCELLS - 1))
        copies[:, q * 128 : (q + 1) * 128] = jnp.where(iota((128, 128), 0) == want, 1.0, 0.0).astype(BF16)

    loads[0].wait()
    held = coarse_v[...].astype(F32)
    tile = jnp.zeros((VARS, 128), F32)
    for b in range(BLK_DEV):
        put = jnp.where(iota((BCELLS, 128), 0) + b * BCELLS == iota((BCELLS, 128), 1), 1.0, 0.0)
        tile = tile + dot(held[:, b, :].astype(BF16), put.astype(BF16))
    pad = jnp.concatenate([tile, jnp.zeros((16 - VARS, 128), F32)], axis=0)
    tt[2] = pad.astype(BF16)

    loads[1].wait()
    at = iota((224, 1), 0)
    inner = at & 15
    cell = at + odd * (7 * COLS_DEV)
    column = (inner & 7) * COLS_DEV + (inner >> 3)
    cell = jnp.where((at >= 128) & (at < 144), column + 126, cell)
    cell = jnp.where((at >= 144) & (at < 160), column, cell)
    for i, (row0, col0) in enumerate(((6 * odd, 126), (6 * odd, 0), (6 - 6 * odd, 126), (6 - 6 * odd, 0))):
        here = jnp.where(inner < 4, (row0 + (inner >> 1)) * COLS_DEV + col0 + (inner & 1), -1)
        cell = jnp.where((at >= 160 + 16 * i) & (at < 176 + 16 * i), here, cell)
    pick = jnp.where(iota((224, 1024), 1) == cell, 1.0, 0.0).astype(BF16)
    weights = dot(pick, remap_v[...], ((1,), (1,))).astype(BF16)
    row_out[0:128, :] = weights[0:128]
    row_out[128:144, :] = choice_tile
    for i in range(2):
        col_out[i, 0:16, :] = weights[128 + 16 * i : 144 + 16 * i]
        col_out[i, 16:32, :] = choice_tile
    for i in range(4):
        cells = weights[160 + 16 * i : 176 + 16 * i].astype(F32)
        corner_out[i] = jnp.where(iota((16, 128), 0) < 8, cells, own_choice).astype(BF16)
    side[...] = jnp.zeros_like(side)
    hl[...] = jnp.zeros_like(hl)
    xs[...] = jnp.zeros_like(xs)

    loads[2].wait()
    wa32[...] = jnp.zeros_like(wa32)
    for dy in range(3):
        for part in range(3):
            first = (dy * 3 + part) * VARS
            for dx in range(3):
                wa32[first : first + VARS, dx * CH : (dx + 1) * CH] = ca_v[dy, dx]
    line = iota((128, 3 * CH), 0)
    twelfth = (line * 43) >> 9
    part_of = twelfth - 3 * ((twelfth * 11) >> 5)
    whole = wa32[...]
    high, low = split(whole)
    wa[...] = jnp.where(part_of == 2, low.astype(F32), high.astype(F32)).astype(BF16)

    twelfth_l = (lane * 43) >> 9
    var_l = jnp.where(lane < 9 * VARS, lane - 12 * twelfth_l, 4096)
    part_l = twelfth_l - 3 * ((twelfth_l * 11) >> 5)
    want = jnp.where(part_l == 1, var_l + 16, var_l)
    spread_msg = jnp.where(iota((32, 128), 0) == want, 1.0, 0.0).astype(BF16)
    spread_var = jnp.where(iota((16, 128), 0) == var_l, 1.0, 0.0).astype(BF16)
    not_first = jnp.where(row > 0, 1.0, 0.0).astype(F32)
    not_last = jnp.where(row < 15, 1.0, 0.0).astype(F32)

    pl.semaphore_wait(barrier, len(partners))

    def send(src, dst, mate, out, into):
        copy = pltpu.make_async_remote_copy(
            src_ref=src, dst_ref=dst, send_sem=send_sem.at[out], recv_sem=recv_sem.at[into],
            device_id=mate, device_id_type=MESH,
        )
        copy.start()

    @pl.when(early)
    def _():
        send(row_out, row_in, halo[0], 0, 0)

    for i in range(2):
        send(corner_out.at[i], corner_in.at[i], halo[1 + i], 1, 1)
    for i in range(2):
        send(col_out.at[i], col_in.at[i], halo[6 + i], 8, 2)
    for i in range(2):
        send(corner_out.at[2 + i], corner_in.at[2 + i], halo[4 + i], 9, 12)
    along_lon = [
        pltpu.make_async_remote_copy(
            src_ref=tt.at[2], dst_ref=tt.at[slot], send_sem=send_sem.at[7], recv_sem=recv_sem.at[8 + i],
            device_id=mate, device_id_type=MESH,
        )
        for i, (slot, mate) in enumerate(zip((0, 1, 3, 4), lon_mates))
    ]
    for copy in along_lon:
        copy.start()

    for copy in along_lon:
        copy.wait_recv()
    choices[...] = dot(tt[...].reshape(80, 128), copies[...])

    def chosen(choice, first_tile):
        total = jnp.zeros((16, 128), F32)
        for j in range(3 * BLK_DEV):
            t, q = first_tile + j // BLK_DEV, j % BLK_DEV
            total = jnp.where(choice == j, choices[t * 16 : t * 16 + 16, q * 128 : (q + 1) * 128], total)
        return total

    blocks = chosen(own_choice, 1).astype(BF16)

    four = jnp.concatenate([remap_v[:, 0:256], remap_v[:, 768:1024]], axis=1)
    four = dot(blocks, four)
    mate_out[0] = jnp.where(is_odd, four[:, 0:128], four[:, 384:512])
    mate_out[1] = jnp.where(is_odd, four[:, 128:256], four[:, 256:384])
    far_out[0] = jnp.where(is_odd, four[:, 384:512], four[:, 0:128])
    far_out[1] = jnp.where(is_odd, four[:, 256:384], four[:, 128:256])
    send(far_out, far_in, halo[0], 10, 13)
    send(mate_out, mate_in, halo[3], 2, 3)

    spread_blocks = dot(blocks, spread_var, ((0,), (0,))).astype(BF16)
    fine = dot(remap_v[...], spread_blocks, ((0,), (0,)))
    high, low = split(fine)
    packed = jnp.where(part_l == 1, low.astype(F32), high.astype(F32)).astype(BF16)
    xs[2:10] = packed.reshape(ROWS_DEV, COLS_DEV, 128)

    third = jnp.broadcast_to(lane, (128, 128))

    def patches(before, here, after, lanes):
        before = jnp.where(lanes < 3 * VARS, before.astype(F32), 0.0)
        here = jnp.where((lanes >= 3 * VARS) & (lanes < 6 * VARS), here.astype(F32), 0.0)
        after = jnp.where(lanes >= 6 * VARS, after.astype(F32), 0.0)
        return (before + here + after).astype(BF16)

    def taps(out_rows):
        field = [patches(xs[i], xs[i + 1], xs[i + 2], third) for i in out_rows]
        result = dot(jnp.concatenate(field, axis=0), wa[...])
        for n, i in enumerate(out_rows):
            for dx in range(3):
                gs[dx, i, MAIN:RIGHT, :] = result[n * 128 : (n + 1) * 128, dx * CH : (dx + 1) * CH]

    def joined(i, first, size):
        return gs[0, i, first - 1 : first - 1 + size, :] + gs[1, i, first : first + size, :] + gs[2, i, first + 1 : first + 1 + size, :]

    taps(list(range(2, 8)))

    def placed(fine):
        high, low = split(fine)
        return dot(jnp.concatenate([high, low], axis=0), spread_msg, ((0,), (0,))).astype(BF16)

    pltpu.make_async_copy(mate_in, mate_in, recv_sem.at[3]).wait()
    xs[10 - 9 * odd] = placed(mate_in[0])
    xs[11 - 11 * odd] = placed(mate_in[1])

    far_known = jnp.where(is_odd, not_last, not_first)

    def fine_of(cells, choice, first_tile, known):
        held = chosen(choice.astype(F32), first_tile) * known
        return dot(cells, held.astype(BF16), ((1,), (1,)))

    def spread_cells(parts):
        high, low = split(jnp.concatenate(parts, axis=0))
        return dot(jnp.concatenate([high, low], axis=1), spread_msg)

    def put_corner(cells, first_row, place):
        for n in range(4):
            side[first_row + (n >> 1), place + (n & 1) : place + (n & 1) + 1, :] = cells[n : n + 1]

    pltpu.make_async_copy(col_in, col_in, recv_sem.at[2]).wait()
    pltpu.make_async_copy(corner_in.at[pl.ds(2, 2)], corner_in.at[pl.ds(2, 2)], recv_sem.at[12]).wait()
    cells = spread_cells([
        fine_of(col_in[0, 0:16, :], col_in[0, 16:17, :], 0, 1.0),
        fine_of(col_in[1, 0:16, :], col_in[1, 16:17, :], 2, 1.0),
        fine_of(corner_in[2], corner_in[2, 8:9, :], 0, 1.0),
        fine_of(corner_in[3], corner_in[3, 8:9, :], 2, 1.0),
    ])
    for i, place_at in enumerate((6, 0)):
        for n in range(16):
            at_col = place_at + (n >> 3)
            side[(n & 7) + 2, at_col : at_col + 1, :] = cells[16 * i + n : 16 * i + n + 1]
    put_corner(cells[32:48], 10 - 10 * odd, 6)
    put_corner(cells[48:64], 10 - 10 * odd, 0)
    near_border, far_border, near_beyond, far_beyond = 8 - 7 * odd, 1 + 7 * odd, 9 - 9 * odd, 9 * odd
    taps([near_border])

    pltpu.make_async_copy(corner_in.at[pl.ds(0, 2)], corner_in.at[pl.ds(0, 2)], recv_sem.at[1]).wait()
    cells = spread_cells([
        fine_of(corner_in[0], corner_in[0, 8:9, :], 0, far_known),
        fine_of(corner_in[1], corner_in[1, 8:9, :], 2, far_known),
    ])
    put_corner(cells[0:16], 10 * odd, 6)
    put_corner(cells[16:32], 10 * odd, 0)
    side_lane = jnp.broadcast_to(lane.reshape(1, 1, 128), (10, 8, 128))
    side_patches = patches(side[0:10], side[1:11], side[2:12], side_lane).reshape(80, 128)
    side_taps = dot(side_patches, wa[...]).reshape(10, 8, 3 * CH)
    for dx in range(3):
        piece = side_taps[:, :, dx * CH : (dx + 1) * CH]
        gs[dx, :, LEFT:MAIN, :] = piece
        gs[dx, :, RIGHT : RIGHT + 8, :] = piece
    for i in [near_border] + list(range(2, 8)):
        ha[i, MAIN:RIGHT, :] = joined(i, MAIN, 128)

    @pl.when(early)
    def _():
        pltpu.make_async_copy(far_in, far_in, recv_sem.at[13]).wait()
        xs[1 + 9 * odd] = placed(far_in[0] * far_known)

    @pl.when(jnp.logical_not(early))
    def _():
        pltpu.make_async_copy(row_in, row_in, recv_sem.at[0]).wait()
        xs[1 + 9 * odd] = spread_cells([fine_of(row_in[0:128, :], row_in[128:129, :], 1, far_known)]).astype(BF16)

    taps([far_border])
    ha[far_border, MAIN:RIGHT, :] = joined(far_border, MAIN, 128)

    def all_reduce(turn, mean, dev, beside):
        cells = ROWS_DEV * COLS_DEV
        for stage, (mates, buf) in enumerate(((z_mates, buf_z), (xy_mates, buf_x))):
            sem = 4 + turn * 2 + stage
            stat[turn, stage, 0:1, :] = mean
            stat[turn, stage, 1:2, :] = dev
            for j, mate in enumerate(mates):
                pltpu.make_async_remote_copy(
                    src_ref=stat.at[turn, stage], dst_ref=buf.at[turn, j], send_sem=send_sem.at[sem - 1], recv_sem=recv_sem.at[sem],
                    device_id=mate, device_id_type=MESH,
                ).start()
            if stage == 0:
                beside()
            pltpu.make_async_copy(buf.at[turn], buf.at[turn], recv_sem.at[sem]).wait()
            mean, dev = merge(mean, dev, buf[turn], cells)
            cells = cells * (len(mates) + 1)
        return to_groups(mean, dev, cells)

    def around_a():
        for load in loads[3:]:
            load.wait()
        prepare_b(cb_v, wba, wbb)

        @pl.when(jnp.logical_not(early))
        def _():
            pltpu.make_async_copy(far_in, far_in, recv_sem.at[13]).wait()

        xs[11 * odd] = placed(far_in[1] * far_known)
        taps([near_beyond, far_beyond])
        for i in (near_beyond, far_beyond):
            ha[i, MAIN:RIGHT, :] = joined(i, MAIN, 128)
        for i in range(10):
            hl[0, i : i + 1, :] = joined(i, MAIN - 1, 1)
            hl[1, i : i + 1, :] = joined(i, RIGHT, 1)

    mean, dev = local_stats([ha[i, MAIN:RIGHT, :] for i in [2, 3, 4, 5, 6, 7, near_border, far_border]])
    mean, inverse = all_reduce(0, mean, dev, around_a)

    second_conv(ha, hl, act, gs, hb, wba, wbb, mean, inverse * vec_v[0], vec_v[1], not_first, not_last)
    store = pltpu.make_async_copy(hb, hb_ref, out_sem)
    store.start()
    mean, dev = local_stats([hb[i] for i in range(8)])
    mean, inverse = all_reduce(1, mean, dev, lambda: None)
    fin_ref[0:1, :] = mean
    fin_ref[1:2, :] = inverse * vec_v[2]
    fin_ref[2:3, :] = vec_v[3]
    store.wait()

    @pl.when(early)
    def _():
        pltpu.make_async_copy(row_in, row_in, send_sem.at[0]).wait()

    pltpu.make_async_copy(far_in, far_in, send_sem.at[10]).wait()
    pltpu.make_async_copy(corner_in.at[pl.ds(0, 2)], corner_in.at[pl.ds(0, 2)], send_sem.at[1]).wait()
    pltpu.make_async_copy(corner_in.at[pl.ds(2, 2)], corner_in.at[pl.ds(2, 2)], send_sem.at[9]).wait()
    pltpu.make_async_copy(col_in, col_in, send_sem.at[8]).wait()
    pltpu.make_async_copy(mate_in, mate_in, send_sem.at[2]).wait()
    pltpu.make_async_copy(tt.at[pl.ds(0, 4)], tt.at[pl.ds(0, 4)], send_sem.at[7]).wait()
    for turn in range(2):
        pltpu.make_async_copy(buf_z.at[turn], buf_z.at[turn], send_sem.at[3 + 2 * turn]).wait()
        pltpu.make_async_copy(buf_x.at[turn], buf_x.at[turn], send_sem.at[4 + 2 * turn]).wait()


def per_device(
    coarse, src_blocks, slot_counts, remap_tiles, conv_a, conv_b, gain_a, shift_a, gain_b, shift_b
):
    anywhere = pl.BlockSpec(memory_space=pl.ANY)
    vectors = [v.reshape(1, CH) for v in (gain_a, shift_a, gain_b, shift_b)]
    hidden, final = pl.pallas_call(
        kernel,
        name="stem",
        out_shape=(
            pltpu.VMEM((ROWS_DEV, COLS_DEV, CH), F32),
            pltpu.VMEM((3, CH), F32),
        ),
        in_specs=[anywhere, pl.BlockSpec(memory_space=pltpu.SMEM)] + [anywhere] * 8,
        out_specs=(anywhere, pl.BlockSpec(memory_space=pltpu.VMEM)),
        scratch_shapes=[
            pltpu.SMEM((1, SLOTS), jnp.int32),
            pltpu.VMEM((VARS, BLK_DEV, BCELLS), BF16),
            pltpu.VMEM((128, 1024), BF16),
            pltpu.VMEM((3, 3, VARS, CH), F32),
            pltpu.VMEM((3, 3, CH, CH), F32),
            pltpu.VMEM((4, 1, CH), F32),
            pltpu.VMEM((5, 16, 128), BF16),
            pltpu.VMEM((144, 128), BF16),
            pltpu.VMEM((2, 32, 128), BF16),
            pltpu.VMEM((4, 16, 128), BF16),
            pltpu.VMEM((2, 16, 128), F32),
            pltpu.VMEM((2, 16, 128), F32),
            pltpu.VMEM((144, 128), BF16),
            pltpu.VMEM((2, 32, 128), BF16),
            pltpu.VMEM((4, 16, 128), BF16),
            pltpu.VMEM((2, 16, 128), F32),
            pltpu.VMEM((2, 16, 128), F32),
            pltpu.VMEM((128, BLK_DEV * 128), BF16),
            pltpu.VMEM((80, BLK_DEV * 128), F32),
            pltpu.VMEM((12, 8, 128), F32),
            pltpu.VMEM((128, 3 * CH), F32),
            pltpu.VMEM((128, 3 * CH), BF16),
            pltpu.VMEM((9 * CH, 2 * CH), BF16),
            pltpu.VMEM((6 * CH, 2 * CH), BF16),
            pltpu.VMEM((12, COLS_DEV, 128), BF16),
            pltpu.VMEM((3, 10, WIDE, CH), F32),
            pltpu.VMEM((10, WIDE, CH), F32),
            pltpu.VMEM((2, 24, CH), F32),
            pltpu.VMEM((10, COLS_DEV, 2 * CH), BF16),
            pltpu.VMEM((ROWS_DEV, COLS_DEV, CH), F32),
            pltpu.VMEM((2, 2, 2, CH), F32),
            pltpu.VMEM((2, 15, 2, CH), F32),
            pltpu.VMEM((2, 31, 2, CH), F32),
            pltpu.SemaphoreType.DMA((9,)),
            pltpu.SemaphoreType.DMA,
            pltpu.SemaphoreType.DMA((11,)),
            pltpu.SemaphoreType.DMA((14,)),
        ],
        compiler_params=pltpu.CompilerParams(
            collective_id=0, has_side_effects=True, vmem_limit_bytes=60 * 1024 * 1024
        ),
    )(
        src_blocks, slot_counts, jnp.transpose(coarse, (1, 0, 2)), remap_tiles.reshape(SLOTS * BCELLS, 1024),
        conv_a, conv_b, *vectors,
    )
    normed = (hidden - final[0]) * final[1] + final[2]
    return jax.nn.silu(normed).astype(BF16)


def solution(mesh):
    return jax.shard_map(
        per_device,
        mesh=mesh,
        in_specs=(
            P("lon", None, None),
            P(("row", "lon"), None),
            P(("row", "lon")),
            P(("row", "lon"), None, None, None),
            P(),
            P(),
            P(),
            P(),
            P(),
            P(),
        ),
        out_specs=P("row", "lon", None),
        check_vma=False,
    )
```

```python
import jax
import jax.numpy as jnp
from jax import lax
from jax.experimental import pallas as pl
from jax.experimental.pallas import tpu as pltpu
from jax.sharding import PartitionSpec as P

ROWS_DEV = 8
COLS_DEV = 128
VARS = 12
CH = 128
GROUPS = 32
SLOTS = 4
BCELLS = 32
BLK_DEV = 4
NBLK = 128
PER_GROUP = CH // GROUPS
MESH = pl.DeviceIdType.MESH
F32 = jnp.float32
BF16 = jnp.bfloat16

eps = 1e-05


def coords():
    row = lax.axis_index("row")
    lon = lax.axis_index("lon")
    core = lax.rem(row, 2)
    z_hi = lax.rem(lax.div(row, 2), 2)
    x = lax.div(row, 4)
    y = lax.div(lon, 8)
    z = z_hi * 8 + lax.rem(lon, 8)
    return row, lon, x, y, z, core


def device_at(x, y, z, core):
    return (x * 4 + lax.div(z, 8) * 2 + core, y * 8 + lax.rem(z, 8))


def moved(value, step, count):
    return lax.rem(value + step, count) if step else value


def along_z(place):
    _, _, x, y, z, core = place
    steps = [(d, c) for d in range(16) for c in range(2) if d or c]
    steps.sort(key=lambda s: -min(s[0], 16 - s[0]))
    return [device_at(x, y, moved(z, d, 16), moved(core, c, 2)) for d, c in steps]


def across(place):
    _, _, x, y, z, core = place
    steps = [(a, b) for a in range(4) for b in range(4) if a or b]
    steps.sort(key=lambda s: -(min(s[0], 4 - s[0]) + min(s[1], 4 - s[1])))
    return [device_at(moved(x, a, 4), moved(y, b, 4), z, core) for a, b in steps]


def coarse_mates(place):
    _, _, x, y, z, core = place
    z_lo = lax.rem(z, 8)
    mates = []
    for step in (2, 1, -1, -2):
        turn = lax.rem(y + 3 + lax.div(z_lo + 8 + step, 8), 4)
        mates.append(device_at(x, turn, lax.rem(z + 16 + step, 16), core))
    return mates


def iota(shape, dim):
    return lax.broadcasted_iota(jnp.int32, shape, dim)


def split(value):
    high = value.astype(BF16)
    low = (value - high.astype(F32)).astype(BF16)
    return high, low


def dot(a, b, dims=((1,), (0,))):
    return lax.dot_general(a, b, (dims, ((), ())), preferred_element_type=F32)


def over_group(row):
    place = iota(row.shape, 1) & (PER_GROUP - 1)
    total = row
    for step in range(1, PER_GROUP):
        after = pltpu.roll(row, CH - step, 1)
        before = pltpu.roll(row, step, 1)
        total = total + jnp.where(place < PER_GROUP - step, after, 0.0) + jnp.where(place >= step, before, 0.0)
    return total


def add_rows(rows, about, first=0.0, second=0.0):
    for r in rows:
        off = r - about
        first = first + off
        second = second + off * off
    return first, second


def row_mean(r):
    return jnp.sum(r, axis=0, keepdims=True) * (1.0 / r.shape[0])


def channel_stats(about, first, second):
    cells = ROWS_DEV * COLS_DEV
    first = jnp.sum(first, axis=0, keepdims=True)
    mean_off = first * (1.0 / cells)
    return about + mean_off, jnp.sum(second, axis=0, keepdims=True) - first * mean_off


def to_groups(mean, dev, cells):
    whole = over_group(mean) * (1.0 / PER_GROUP)
    apart = mean - whole
    spread = over_group(dev + cells * (apart * apart)) * (1.0 / (cells * PER_GROUP))
    return whole, lax.rsqrt(spread + eps)


def merge(mean, dev, others, cells):
    count = others.shape[0] + 1
    means = others[:, 0:1, :]
    whole = (mean + jnp.sum(means, axis=0)) * (1.0 / count)
    off = means - whole
    own = mean - whole
    spread = own * own + jnp.sum(off * off, axis=0)
    return whole, dev + jnp.sum(others[:, 1:2, :], axis=0) + cells * spread


LEFT, MAIN, RIGHT, WIDE = 8, 16, 144, 160


def prepare_b(cb_v, wba, wbb):
    for dy in range(3):
        for dx in range(2):
            span = slice(dx * CH, (dx + 1) * CH)
            high, low = split(cb_v[dy, dx])
            wba[dy * 256 : dy * 256 + 128, span] = high
            wba[dy * 256 + 128 : dy * 256 + 256, span] = high
            wba[768 + dy * 128 : 896 + dy * 128, span] = low
        high, low = split(cb_v[dy, 2])
        for part, value in enumerate((high, high, low)):
            if dy < 2:
                wbb[part * 256 + dy * 128 : part * 256 + dy * 128 + 128, 0:CH] = value
            else:
                wbb[part * 256 : part * 256 + 128, CH : 2 * CH] = jnp.zeros((CH, CH), BF16)
                wbb[part * 256 + 128 : part * 256 + 256, CH : 2 * CH] = value


def activate(value, mean, scale, shift):
    half = ((value - mean) * scale + shift) * 0.5
    return half + half * jnp.tanh(half)


def second_conv(ha, hl, act, gs, hb, wba, wbb, mean, scale, shift, not_first, not_last):
    for i in range(10):
        value = activate(ha[i, MAIN:RIGHT, :], mean, scale, shift)
        if i == 0:
            value = value * not_first
        if i == 9:
            value = value * not_last
        act[i, :, 0:128], act[i, :, 128:256] = split(value)
    known = iota((16, 1), 0)
    known = jnp.where(known == 0, not_first, jnp.where(known == 9, not_last, 1.0))
    for i in range(2):
        hl[i, 0:16, :] = activate(hl[i, 0:16, :], mean, scale, shift) * known

    def side(i, dy):
        return split(hl[i, dy : dy + 16, :])

    def rows(first, size, part):
        return act[first : first + size, :, part * 128 : part * 128 + 128].reshape(size * 128, 128)

    pieces = [act[dy : dy + 8].reshape(1024, 256) for dy in range(3)] + [rows(dy, 8, 0) for dy in range(3)]
    at_side = [side(0, dy) for dy in range(3)]
    at_side = [part for pair in at_side for part in pair] + [pair[0] for pair in at_side]
    field = jnp.concatenate([jnp.concatenate(pieces, axis=1), jnp.concatenate(at_side, axis=1)], axis=0)
    early = dot(field, wba[...])

    pieces = [rows(0, 9, 0), rows(1, 9, 0), rows(0, 9, 1), rows(1, 9, 1), rows(0, 9, 0), rows(1, 9, 0)]
    (high0, low0), (high1, low1) = side(1, 0), side(1, 1)
    at_side = [high0, high1, low0, low1, high0, high1]
    field = jnp.concatenate([jnp.concatenate(pieces, axis=1), jnp.concatenate(at_side, axis=1)], axis=0)
    late = dot(field, wbb[...])

    for i in range(8):
        gs[0, i, MAIN:RIGHT, :] = early[i * 128 : (i + 1) * 128, 0:128]
        gs[0, i, MAIN - 1 : MAIN, :] = early[1024 + i : 1025 + i, 0:128]
        gs[2, i, MAIN:RIGHT, :] = late[i * 128 : (i + 1) * 128, 0:128] + late[(i + 1) * 128 : (i + 2) * 128, 128:256]
        gs[2, i, RIGHT : RIGHT + 1, :] = late[1152 + i : 1153 + i, 0:128] + late[1153 + i : 1154 + i, 128:256]
        hb[i] = gs[0, i, MAIN - 1 : RIGHT - 1, :] + early[i * 128 : (i + 1) * 128, 128:256] + gs[2, i, MAIN + 1 : RIGHT + 1, :]


def kernel(
    src_hbm, cnt_ref, coarse_ref, remap_ref, ca_ref, cb_ref, gain_a_ref, shift_a_ref, gain_b_ref, shift_b_ref,
    hb_ref, fin_ref,
    src_ref, coarse_v, remap_v, ca_v, cb_v, vec_v,
    tt, row_out, col_out, corner_out, mate_out, next_out, choice_out,
    row_in, col_in, corner_in, mate_in, next_in, choice_in,
    copies, choices, side, wa32, wa, wba, wbb,
    xs, gs, ha, hl, act, hb,
    stat, buf_x, buf_z,
    in_sem, out_sem, send_sem, recv_sem,
):
    place = coords()
    row, lon = place[0], place[1]
    z_mates = along_z(place)
    xy_mates = across(place)
    lon_mates = coarse_mates(place)
    lon_left, lon_right = lax.rem(lon + 31, 32), lax.rem(lon + 1, 32)
    odd = lax.rem(row, 2)
    is_odd = odd == 1
    near_row = row + 1 - 2 * odd
    far_row = lax.rem(row + 2 * odd + 15, 16)
    halo = [
        (far_row, lon), (far_row, lon_right), (far_row, lon_left), (near_row, lon),
        (near_row, lon_right), (near_row, lon_left), (row, lon_right), (row, lon_left),
    ]
    barrier = pltpu.get_barrier_semaphore()
    partners = halo + lon_mates + z_mates + xy_mates
    for mate in partners:
        pl.semaphore_signal(barrier, inc=1, device_id=mate, device_id_type=MESH)

    loads = [
        pltpu.make_async_copy(coarse_ref, coarse_v, in_sem.at[0]),
        pltpu.make_async_copy(remap_ref, remap_v, in_sem.at[1]),
        pltpu.make_async_copy(ca_ref, ca_v, in_sem.at[2]),
        pltpu.make_async_copy(cb_ref, cb_v, in_sem.at[3]),
    ]
    for i, ref in enumerate((gain_a_ref, shift_a_ref, gain_b_ref, shift_b_ref)):
        loads.append(pltpu.make_async_copy(ref, vec_v.at[i], in_sem.at[4 + i]))
    sources = pltpu.make_async_copy(src_hbm, src_ref, in_sem.at[8])
    for load in [sources] + loads:
        load.start()

    sources.wait()
    lane = iota((1, 128), 1)
    own_choice = jnp.zeros((1, 128), F32)
    for k in range(SLOTS):
        local = lax.rem(src_ref[0, k] - (lon - 1) * BLK_DEV + 2 * NBLK, NBLK)
        local = jnp.where(k < cnt_ref[0], local, -64)
        own_choice = jnp.where((lane >> 5) == k, local.astype(F32), own_choice)
    choice_tile = jnp.broadcast_to(own_choice, (16, 128)).astype(BF16)

    for q in range(BLK_DEV):
        want = q * BCELLS + (lane & (BCELLS - 1))
        copies[:, q * 128 : (q + 1) * 128] = jnp.where(iota((128, 128), 0) == want, 1.0, 0.0).astype(BF16)

    loads[0].wait()
    held = coarse_v[...].astype(F32)
    tile = jnp.zeros((VARS, 128), F32)
    for b in range(BLK_DEV):
        put = jnp.where(iota((BCELLS, 128), 0) + b * BCELLS == iota((BCELLS, 128), 1), 1.0, 0.0)
        tile = tile + dot(held[:, b, :].astype(BF16), put.astype(BF16))
    pad = jnp.concatenate([tile, jnp.zeros((16 - VARS, 128), F32)], axis=0)
    tt[2] = pad.astype(BF16)

    loads[1].wait()
    at = iota((224, 1), 0)
    inner = at & 15
    cell = at + odd * (7 * COLS_DEV)
    column = (inner & 7) * COLS_DEV + (inner >> 3)
    cell = jnp.where((at >= 128) & (at < 144), column + 126, cell)
    cell = jnp.where((at >= 144) & (at < 160), column, cell)
    for i, (row0, col0) in enumerate(((6 * odd, 126), (6 * odd, 0), (6 - 6 * odd, 126), (6 - 6 * odd, 0))):
        here = jnp.where(inner < 4, (row0 + (inner >> 1)) * COLS_DEV + col0 + (inner & 1), -1)
        cell = jnp.where((at >= 160 + 16 * i) & (at < 176 + 16 * i), here, cell)
    pick = jnp.where(iota((224, 1024), 1) == cell, 1.0, 0.0).astype(BF16)
    weights = dot(pick, remap_v[...], ((1,), (1,))).astype(BF16)
    row_out[...] = weights[0:128]
    choice_out[...] = own_choice
    for i in range(2):
        col_out[i, 0:16, :] = weights[128 + 16 * i : 144 + 16 * i]
        col_out[i, 16:32, :] = choice_tile
    for i in range(4):
        cells = weights[160 + 16 * i : 176 + 16 * i].astype(F32)
        corner_out[i] = jnp.where(iota((8, 128), 0) < 4, cells[0:8], own_choice)
    side[...] = jnp.zeros_like(side)
    hl[...] = jnp.zeros_like(hl)
    xs[...] = jnp.zeros_like(xs)

    loads[2].wait()
    wa32[...] = jnp.zeros_like(wa32)
    for dy in range(3):
        for part in range(3):
            first = (dy * 3 + part) * VARS
            for dx in range(3):
                wa32[first : first + VARS, dx * CH : (dx + 1) * CH] = ca_v[dy, dx]
    line = iota((128, 3 * CH), 0)
    twelfth = (line * 43) >> 9
    part_of = twelfth - 3 * ((twelfth * 11) >> 5)
    whole = wa32[...]
    high, low = split(whole)
    wa[...] = jnp.where(part_of == 2, low.astype(F32), high.astype(F32)).astype(BF16)

    twelfth_l = (lane * 43) >> 9
    var_l = jnp.where(lane < 9 * VARS, lane - 12 * twelfth_l, 4096)
    part_l = twelfth_l - 3 * ((twelfth_l * 11) >> 5)
    want = jnp.where(part_l == 1, var_l + 16, var_l)
    spread_msg = jnp.where(iota((32, 128), 0) == want, 1.0, 0.0).astype(BF16)
    spread_var = jnp.where(iota((16, 128), 0) == var_l, 1.0, 0.0).astype(BF16)
    not_first = jnp.where(row > 0, 1.0, 0.0).astype(F32)
    not_last = jnp.where(row < 15, 1.0, 0.0).astype(F32)

    pl.semaphore_wait(barrier, len(partners))

    def send(src, dst, mate, out, into):
        copy = pltpu.make_async_remote_copy(
            src_ref=src, dst_ref=dst, send_sem=send_sem.at[out], recv_sem=recv_sem.at[into],
            device_id=mate, device_id_type=MESH,
        )
        copy.start()

    send(row_out, row_in, halo[0], 0, 0)
    send(choice_out, choice_in, halo[0], 11, 14)
    for i in range(2):
        send(corner_out.at[i, pl.ds(0, 5)], corner_in.at[i, pl.ds(0, 5)], halo[1 + i], 1, 1)
    for i in range(2):
        send(col_out.at[i], col_in.at[i], halo[6 + i], 8, 2)
    for i in range(2, 4):
        send(corner_out.at[i, pl.ds(0, 5)], corner_in.at[i, pl.ds(0, 5)], halo[2 + i], 9, 12)
    along_lon = [
        pltpu.make_async_remote_copy(
            src_ref=tt.at[2], dst_ref=tt.at[slot], send_sem=send_sem.at[7], recv_sem=recv_sem.at[8 + i],
            device_id=mate, device_id_type=MESH,
        )
        for i, (slot, mate) in enumerate(zip((0, 1, 3, 4), lon_mates))
    ]
    for copy in along_lon:
        copy.start()

    for copy in along_lon:
        copy.wait_recv()
    choices[...] = dot(tt[...].reshape(80, 128), copies[...])

    def chosen(choice, first_tile):
        total = jnp.zeros((16, 128), F32)
        for j in range(3 * BLK_DEV):
            t, q = first_tile + j // BLK_DEV, j % BLK_DEV
            total = jnp.where(choice == j, choices[t * 16 : t * 16 + 16, q * 128 : (q + 1) * 128], total)
        return total

    blocks = chosen(own_choice, 1).astype(BF16)

    four = jnp.concatenate([remap_v[:, 0:256], remap_v[:, 768:1024]], axis=1)
    four = dot(blocks, four)
    mate_out[0] = jnp.where(is_odd, four[:, 0:128], four[:, 384:512])
    mate_out[1] = jnp.where(is_odd, four[:, 128:256], four[:, 256:384])
    next_out[...] = jnp.where(is_odd, four[:, 256:384], four[:, 128:256])
    send(next_out, next_in, halo[0], 10, 13)
    send(mate_out, mate_in, halo[3], 2, 3)

    spread_blocks = dot(blocks, spread_var, ((0,), (0,))).astype(BF16)
    fine = dot(remap_v[...], spread_blocks, ((0,), (0,)))
    high, low = split(fine)
    packed = jnp.where(part_l == 1, low.astype(F32), high.astype(F32)).astype(BF16)
    xs[2:10] = packed.reshape(ROWS_DEV, COLS_DEV, 128)

    third = jnp.broadcast_to(lane, (128, 128))

    def patches(before, here, after, lanes):
        before = jnp.where(lanes < 3 * VARS, before.astype(F32), 0.0)
        here = jnp.where((lanes >= 3 * VARS) & (lanes < 6 * VARS), here.astype(F32), 0.0)
        after = jnp.where(lanes >= 6 * VARS, after.astype(F32), 0.0)
        return (before + here + after).astype(BF16)

    def taps(out_rows):
        field = [patches(xs[i], xs[i + 1], xs[i + 2], third) for i in out_rows]
        result = dot(jnp.concatenate(field, axis=0), wa[...])
        for n, i in enumerate(out_rows):
            for dx in range(3):
                gs[dx, i, MAIN:RIGHT, :] = result[n * 128 : (n + 1) * 128, dx * CH : (dx + 1) * CH]

    def joined(i, first, size):
        return gs[0, i, first - 1 : first - 1 + size, :] + gs[1, i, first : first + size, :] + gs[2, i, first + 1 : first + 1 + size, :]

    taps(list(range(2, 8)))

    def placed(fine):
        high, low = split(fine)
        return dot(jnp.concatenate([high, low], axis=0), spread_msg, ((0,), (0,))).astype(BF16)

    pltpu.make_async_copy(mate_in, mate_in, recv_sem.at[3]).wait()
    xs[10 - 9 * odd] = placed(mate_in[0])
    xs[11 - 11 * odd] = placed(mate_in[1])

    far_known = jnp.where(is_odd, not_last, not_first)

    def fine_of(cells, choice, first_tile, known):
        held = chosen(choice.astype(F32), first_tile) * known
        return dot(cells.astype(BF16), held.astype(BF16), ((1,), (1,)))

    def spread_cells(parts):
        high, low = split(jnp.concatenate(parts, axis=0))
        return dot(jnp.concatenate([high, low], axis=1), spread_msg)

    def put_corner(cells, first_row, place):
        for n in range(4):
            side[first_row + (n >> 1), place + (n & 1) : place + (n & 1) + 1, :] = cells[n : n + 1]

    def corners(first):
        some = corner_in.at[pl.ds(first, 2), pl.ds(0, 5)]
        return pltpu.make_async_copy(some, some, recv_sem.at[1 if first == 0 else 12])

    pltpu.make_async_copy(col_in, col_in, recv_sem.at[2]).wait()
    corners(2).wait()
    cells = spread_cells([
        fine_of(col_in[0, 0:16, :], col_in[0, 16:17, :], 0, 1.0),
        fine_of(col_in[1, 0:16, :], col_in[1, 16:17, :], 2, 1.0),
        fine_of(corner_in[2], corner_in[2, 4:5, :], 0, 1.0),
        fine_of(corner_in[3], corner_in[3, 4:5, :], 2, 1.0),
    ])
    for i, place_at in enumerate((6, 0)):
        for n in range(16):
            at_col = place_at + (n >> 3)
            side[(n & 7) + 2, at_col : at_col + 1, :] = cells[16 * i + n : 16 * i + n + 1]
    put_corner(cells[32:40], 10 - 10 * odd, 6)
    put_corner(cells[40:48], 10 - 10 * odd, 0)
    near_border, far_border, near_beyond, far_beyond = 8 - 7 * odd, 1 + 7 * odd, 9 - 9 * odd, 9 * odd
    taps([near_border])

    def side_taps():
        side_lane = jnp.broadcast_to(lane.reshape(1, 1, 128), (10, 8, 128))
        side_patches = patches(side[0:10], side[1:11], side[2:12], side_lane).reshape(80, 128)
        result = dot(side_patches, wa[...]).reshape(10, 8, 3 * CH)
        for dx in range(3):
            piece = result[:, :, dx * CH : (dx + 1) * CH]
            gs[dx, :, LEFT:MAIN, :] = piece
            gs[dx, :, RIGHT : RIGHT + 8, :] = piece

    side_taps()
    inner_rows = [2, 3, 4, 5, 6, 7, near_border]
    for i in inner_rows:
        ha[i, MAIN:RIGHT, :] = joined(i, MAIN, 128)
    about = row_mean(ha[2, MAIN:RIGHT, :])
    first, second = add_rows([ha[i, MAIN:RIGHT, :] for i in inner_rows], about)

    corners(0).wait()
    pltpu.make_async_copy(choice_in, choice_in, recv_sem.at[14]).wait()
    pltpu.make_async_copy(row_in, row_in, recv_sem.at[0]).wait()
    cells = spread_cells([
        fine_of(row_in[...], choice_in[...], 1, far_known),
        fine_of(corner_in[0], corner_in[0, 4:5, :], 0, far_known),
        fine_of(corner_in[1], corner_in[1, 4:5, :], 2, far_known),
    ])
    xs[1 + 9 * odd] = cells[0:128].astype(BF16)
    put_corner(cells[128:136], 10 * odd, 6)
    put_corner(cells[136:144], 10 * odd, 0)
    side_taps()
    taps([far_border])
    border = joined(far_border, MAIN, 128)
    ha[far_border, MAIN:RIGHT, :] = border
    mean, dev = channel_stats(about, *add_rows([border], about, first, second))

    def all_reduce(turn, mean, dev, beside):
        cells = ROWS_DEV * COLS_DEV
        for stage, (mates, buf) in enumerate(((z_mates, buf_z), (xy_mates, buf_x))):
            sem = 4 + turn * 2 + stage
            stat[turn, stage, 0:1, :] = mean
            stat[turn, stage, 1:2, :] = dev
            for j, mate in enumerate(mates):
                pltpu.make_async_remote_copy(
                    src_ref=stat.at[turn, stage], dst_ref=buf.at[turn, j], send_sem=send_sem.at[sem - 1], recv_sem=recv_sem.at[sem],
                    device_id=mate, device_id_type=MESH,
                ).start()
            if stage == 0:
                beside()
            pltpu.make_async_copy(buf.at[turn], buf.at[turn], recv_sem.at[sem]).wait()
            mean, dev = merge(mean, dev, buf[turn], cells)
            cells = cells * (len(mates) + 1)
        return to_groups(mean, dev, cells)

    def around_a():
        for load in loads[3:]:
            load.wait()
        prepare_b(cb_v, wba, wbb)
        pltpu.make_async_copy(next_in, next_in, recv_sem.at[13]).wait()
        xs[11 * odd] = placed(next_in[...] * far_known)
        taps([near_beyond, far_beyond])
        for i in (near_beyond, far_beyond):
            ha[i, MAIN:RIGHT, :] = joined(i, MAIN, 128)
        for i in range(10):
            hl[0, i : i + 1, :] = joined(i, MAIN - 1, 1)
            hl[1, i : i + 1, :] = joined(i, RIGHT, 1)

    mean, inverse = all_reduce(0, mean, dev, around_a)

    second_conv(ha, hl, act, gs, hb, wba, wbb, mean, inverse * vec_v[0], vec_v[1], not_first, not_last)
    store = pltpu.make_async_copy(hb, hb_ref, out_sem)
    store.start()
    about = row_mean(hb[0])
    mean, dev = channel_stats(about, *add_rows([hb[i] for i in range(8)], about))
    mean, inverse = all_reduce(1, mean, dev, lambda: None)
    fin_ref[0:1, :] = mean
    fin_ref[1:2, :] = inverse * vec_v[2]
    fin_ref[2:3, :] = vec_v[3]
    store.wait()

    pltpu.make_async_copy(row_in, row_in, send_sem.at[0]).wait()
    pltpu.make_async_copy(choice_in, choice_in, send_sem.at[11]).wait()
    pltpu.make_async_copy(next_in, next_in, send_sem.at[10]).wait()
    for first, sem in ((0, 1), (2, 9)):
        some = corner_in.at[pl.ds(first, 2), pl.ds(0, 5)]
        pltpu.make_async_copy(some, some, send_sem.at[sem]).wait()
    pltpu.make_async_copy(col_in, col_in, send_sem.at[8]).wait()
    pltpu.make_async_copy(mate_in, mate_in, send_sem.at[2]).wait()
    pltpu.make_async_copy(tt.at[pl.ds(0, 4)], tt.at[pl.ds(0, 4)], send_sem.at[7]).wait()
    for turn in range(2):
        pltpu.make_async_copy(buf_z.at[turn], buf_z.at[turn], send_sem.at[3 + 2 * turn]).wait()
        pltpu.make_async_copy(buf_x.at[turn], buf_x.at[turn], send_sem.at[4 + 2 * turn]).wait()


def per_device(
    coarse, src_blocks, slot_counts, remap_tiles, conv_a, conv_b, gain_a, shift_a, gain_b, shift_b
):
    anywhere = pl.BlockSpec(memory_space=pl.ANY)
    vectors = [v.reshape(1, CH) for v in (gain_a, shift_a, gain_b, shift_b)]
    hidden, final = pl.pallas_call(
        kernel,
        name="stem",
        out_shape=(
            pltpu.VMEM((ROWS_DEV, COLS_DEV, CH), F32),
            pltpu.VMEM((3, CH), F32),
        ),
        in_specs=[anywhere, pl.BlockSpec(memory_space=pltpu.SMEM)] + [anywhere] * 8,
        out_specs=(anywhere, pl.BlockSpec(memory_space=pltpu.VMEM)),
        scratch_shapes=[
            pltpu.SMEM((1, SLOTS), jnp.int32),
            pltpu.VMEM((VARS, BLK_DEV, BCELLS), BF16),
            pltpu.VMEM((128, 1024), BF16),
            pltpu.VMEM((3, 3, VARS, CH), F32),
            pltpu.VMEM((3, 3, CH, CH), F32),
            pltpu.VMEM((4, 1, CH), F32),
            pltpu.VMEM((5, 16, 128), BF16),
            pltpu.VMEM((128, 128), BF16),
            pltpu.VMEM((2, 32, 128), BF16),
            pltpu.VMEM((4, 8, 128), F32),
            pltpu.VMEM((2, 16, 128), F32),
            pltpu.VMEM((16, 128), F32),
            pltpu.VMEM((1, 128), F32),
            pltpu.VMEM((128, 128), BF16),
            pltpu.VMEM((2, 32, 128), BF16),
            pltpu.VMEM((4, 8, 128), F32),
            pltpu.VMEM((2, 16, 128), F32),
            pltpu.VMEM((16, 128), F32),
            pltpu.VMEM((1, 128), F32),
            pltpu.VMEM((128, BLK_DEV * 128), BF16),
            pltpu.VMEM((80, BLK_DEV * 128), F32),
            pltpu.VMEM((12, 8, 128), F32),
            pltpu.VMEM((128, 3 * CH), F32),
            pltpu.VMEM((128, 3 * CH), BF16),
            pltpu.VMEM((9 * CH, 2 * CH), BF16),
            pltpu.VMEM((6 * CH, 2 * CH), BF16),
            pltpu.VMEM((12, COLS_DEV, 128), BF16),
            pltpu.VMEM((3, 10, WIDE, CH), F32),
            pltpu.VMEM((10, WIDE, CH), F32),
            pltpu.VMEM((2, 24, CH), F32),
            pltpu.VMEM((10, COLS_DEV, 2 * CH), BF16),
            pltpu.VMEM((ROWS_DEV, COLS_DEV, CH), F32),
            pltpu.VMEM((2, 2, 2, CH), F32),
            pltpu.VMEM((2, 15, 2, CH), F32),
            pltpu.VMEM((2, 31, 2, CH), F32),
            pltpu.SemaphoreType.DMA((9,)),
            pltpu.SemaphoreType.DMA,
            pltpu.SemaphoreType.DMA((12,)),
            pltpu.SemaphoreType.DMA((15,)),
        ],
        compiler_params=pltpu.CompilerParams(
            collective_id=0, has_side_effects=True, vmem_limit_bytes=60 * 1024 * 1024
        ),
    )(
        src_blocks, slot_counts, jnp.transpose(coarse, (1, 0, 2)), remap_tiles.reshape(SLOTS * BCELLS, 1024),
        conv_a, conv_b, *vectors,
    )
    normed = (hidden - final[0]) * final[1] + final[2]
    return jax.nn.silu(normed).astype(BF16)


def solution(mesh):
    return jax.shard_map(
        per_device,
        mesh=mesh,
        in_specs=(
            P("lon", None, None),
            P(("row", "lon"), None),
            P(("row", "lon")),
            P(("row", "lon"), None, None, None),
            P(),
            P(),
            P(),
            P(),
            P(),
            P(),
        ),
        out_specs=P("row", "lon", None),
        check_vma=False,
    )
```

```python
import jax
import jax.numpy as jnp
from jax import lax
from jax.experimental import pallas as pl
from jax.experimental.pallas import tpu as pltpu
from jax.sharding import PartitionSpec as P

ROWS_DEV = 8
COLS_DEV = 128
VARS = 12
CH = 128
GROUPS = 32
SLOTS = 4
BCELLS = 32
BLK_DEV = 4
NBLK = 128
PER_GROUP = CH // GROUPS
MESH = pl.DeviceIdType.MESH
F32 = jnp.float32
BF16 = jnp.bfloat16

eps = 1e-05


def coords():
    row = lax.axis_index("row")
    lon = lax.axis_index("lon")
    core = lax.rem(row, 2)
    z_hi = lax.rem(lax.div(row, 2), 2)
    x = lax.div(row, 4)
    y = lax.div(lon, 8)
    z = z_hi * 8 + lax.rem(lon, 8)
    return row, lon, x, y, z, core


def device_at(x, y, z, core):
    return (x * 4 + lax.div(z, 8) * 2 + core, y * 8 + lax.rem(z, 8))


def moved(value, step, count):
    return lax.rem(value + step, count) if step else value


def along_z(place):
    _, _, x, y, z, core = place
    steps = [(d, c) for d in range(16) for c in range(2) if d or c]
    steps.sort(key=lambda s: -min(s[0], 16 - s[0]))
    return [device_at(x, y, moved(z, d, 16), moved(core, c, 2)) for d, c in steps]


def across(place):
    _, _, x, y, z, core = place
    steps = [(a, b) for a in range(4) for b in range(4) if a or b]
    steps.sort(key=lambda s: -(min(s[0], 4 - s[0]) + min(s[1], 4 - s[1])))
    return [device_at(moved(x, a, 4), moved(y, b, 4), z, core) for a, b in steps]


def coarse_mates(place):
    _, _, x, y, z, core = place
    z_lo = lax.rem(z, 8)
    mates = []
    for step in (2, 1, -1, -2):
        turn = lax.rem(y + 3 + lax.div(z_lo + 8 + step, 8), 4)
        mates.append(device_at(x, turn, lax.rem(z + 16 + step, 16), core))
    return mates


def iota(shape, dim):
    return lax.broadcasted_iota(jnp.int32, shape, dim)


def split(value):
    high = value.astype(BF16)
    low = (value - high.astype(F32)).astype(BF16)
    return high, low


def dot(a, b, dims=((1,), (0,))):
    return lax.dot_general(a, b, (dims, ((), ())), preferred_element_type=F32)


def over_group(row):
    place = iota(row.shape, 1) & (PER_GROUP - 1)
    total = row
    for step in range(1, PER_GROUP):
        after = pltpu.roll(row, CH - step, 1)
        before = pltpu.roll(row, step, 1)
        total = total + jnp.where(place < PER_GROUP - step, after, 0.0) + jnp.where(place >= step, before, 0.0)
    return total


def add_rows(rows, about, first=0.0, second=0.0):
    for r in rows:
        off = r - about
        first = first + off
        second = second + off * off
    return first, second


def row_mean(r):
    return jnp.sum(r, axis=0, keepdims=True) * (1.0 / r.shape[0])


def channel_stats(about, first, second):
    cells = ROWS_DEV * COLS_DEV
    first = jnp.sum(first, axis=0, keepdims=True)
    mean_off = first * (1.0 / cells)
    return about + mean_off, jnp.sum(second, axis=0, keepdims=True) - first * mean_off


def to_groups(mean, dev, cells):
    whole = over_group(mean) * (1.0 / PER_GROUP)
    apart = mean - whole
    spread = over_group(dev + cells * (apart * apart)) * (1.0 / (cells * PER_GROUP))
    return whole, lax.rsqrt(spread + eps)


def merge(mean, dev, others, cells):
    count = others.shape[0] + 1
    means = others[:, 0:1, :]
    whole = (mean + jnp.sum(means, axis=0)) * (1.0 / count)
    off = means - whole
    own = mean - whole
    spread = own * own + jnp.sum(off * off, axis=0)
    return whole, dev + jnp.sum(others[:, 1:2, :], axis=0) + cells * spread


LEFT, MAIN, RIGHT, WIDE = 8, 16, 144, 160


def prepare_b(cb_v, wba, wbb):
    for dy in range(3):
        for dx in range(2):
            span = slice(dx * CH, (dx + 1) * CH)
            high, low = split(cb_v[dy, dx])
            wba[dy * 256 : dy * 256 + 128, span] = high
            wba[dy * 256 + 128 : dy * 256 + 256, span] = high
            wba[768 + dy * 128 : 896 + dy * 128, span] = low
        high, low = split(cb_v[dy, 2])
        for part, value in enumerate((high, high, low)):
            if dy < 2:
                wbb[part * 256 + dy * 128 : part * 256 + dy * 128 + 128, 0:CH] = value
            else:
                wbb[part * 256 : part * 256 + 128, CH : 2 * CH] = jnp.zeros((CH, CH), BF16)
                wbb[part * 256 + 128 : part * 256 + 256, CH : 2 * CH] = value


def activate(value, mean, scale, shift):
    half = ((value - mean) * scale + shift) * 0.5
    return half + half * jnp.tanh(half)


def second_conv(ha, hl, act, gs, hb, wba, wbb, mean, scale, shift, not_first, not_last):
    for i in range(10):
        value = activate(ha[i, MAIN:RIGHT, :], mean, scale, shift)
        if i == 0:
            value = value * not_first
        if i == 9:
            value = value * not_last
        act[i, :, 0:128], act[i, :, 128:256] = split(value)
    known = iota((16, 1), 0)
    known = jnp.where(known == 0, not_first, jnp.where(known == 9, not_last, 1.0))
    for i in range(2):
        hl[i, 0:16, :] = activate(hl[i, 0:16, :], mean, scale, shift) * known

    def side(i, dy):
        return split(hl[i, dy : dy + 16, :])

    def rows(first, size, part):
        return act[first : first + size, :, part * 128 : part * 128 + 128].reshape(size * 128, 128)

    pieces = [act[dy : dy + 8].reshape(1024, 256) for dy in range(3)] + [rows(dy, 8, 0) for dy in range(3)]
    at_side = [side(0, dy) for dy in range(3)]
    at_side = [part for pair in at_side for part in pair] + [pair[0] for pair in at_side]
    field = jnp.concatenate([jnp.concatenate(pieces, axis=1), jnp.concatenate(at_side, axis=1)], axis=0)
    early = dot(field, wba[...])

    pieces = [rows(0, 9, 0), rows(1, 9, 0), rows(0, 9, 1), rows(1, 9, 1), rows(0, 9, 0), rows(1, 9, 0)]
    (high0, low0), (high1, low1) = side(1, 0), side(1, 1)
    at_side = [high0, high1, low0, low1, high0, high1]
    field = jnp.concatenate([jnp.concatenate(pieces, axis=1), jnp.concatenate(at_side, axis=1)], axis=0)
    late = dot(field, wbb[...])

    for i in range(8):
        gs[0, i, MAIN:RIGHT, :] = early[i * 128 : (i + 1) * 128, 0:128]
        gs[0, i, MAIN - 1 : MAIN, :] = early[1024 + i : 1025 + i, 0:128]
        gs[2, i, MAIN:RIGHT, :] = late[i * 128 : (i + 1) * 128, 0:128] + late[(i + 1) * 128 : (i + 2) * 128, 128:256]
        gs[2, i, RIGHT : RIGHT + 1, :] = late[1152 + i : 1153 + i, 0:128] + late[1153 + i : 1154 + i, 128:256]
        hb[i] = gs[0, i, MAIN - 1 : RIGHT - 1, :] + early[i * 128 : (i + 1) * 128, 128:256] + gs[2, i, MAIN + 1 : RIGHT + 1, :]


def kernel(
    src_hbm, cnt_ref, coarse_ref, remap_ref, ca_ref, cb_ref, gain_a_ref, shift_a_ref, gain_b_ref, shift_b_ref,
    hb_ref, fin_ref,
    src_ref, coarse_v, remap_v, ca_v, cb_v, vec_v,
    tt, row_out, col_out, corner_out, mate_out, next_out, choice_out,
    row_in, col_in, corner_in, mate_in, next_in, choice_in,
    copies, choices, side, wa32, wa, wba, wbb,
    xs, gs, ha, hl, act, hb,
    stat, buf_x, buf_z,
    in_sem, out_sem, send_sem, recv_sem,
):
    place = coords()
    row, lon = place[0], place[1]
    z_mates = along_z(place)
    xy_mates = across(place)
    lon_mates = coarse_mates(place)
    lon_left, lon_right = lax.rem(lon + 31, 32), lax.rem(lon + 1, 32)
    odd = lax.rem(row, 2)
    is_odd = odd == 1
    near_row = row + 1 - 2 * odd
    far_row = lax.rem(row + 2 * odd + 15, 16)
    halo = [
        (far_row, lon), (far_row, lon_right), (far_row, lon_left), (near_row, lon),
        (near_row, lon_right), (near_row, lon_left), (row, lon_right), (row, lon_left),
    ]
    barrier = pltpu.get_barrier_semaphore()
    partners = halo + lon_mates + z_mates + xy_mates
    for mate in partners:
        pl.semaphore_signal(barrier, inc=1, device_id=mate, device_id_type=MESH)

    loads = [
        pltpu.make_async_copy(coarse_ref, coarse_v, in_sem.at[0]),
        pltpu.make_async_copy(remap_ref, remap_v, in_sem.at[1]),
        pltpu.make_async_copy(ca_ref, ca_v, in_sem.at[2]),
        pltpu.make_async_copy(cb_ref, cb_v, in_sem.at[3]),
    ]
    for i, ref in enumerate((gain_a_ref, shift_a_ref, gain_b_ref, shift_b_ref)):
        loads.append(pltpu.make_async_copy(ref, vec_v.at[i], in_sem.at[4 + i]))
    sources = pltpu.make_async_copy(src_hbm, src_ref, in_sem.at[8])
    for load in [sources] + loads:
        load.start()

    sources.wait()
    lane = iota((1, 128), 1)
    own_choice = jnp.zeros((1, 128), F32)
    for k in range(SLOTS):
        local = lax.rem(src_ref[0, k] - (lon - 1) * BLK_DEV + 2 * NBLK, NBLK)
        local = jnp.where(k < cnt_ref[0], local, -64)
        own_choice = jnp.where((lane >> 5) == k, local.astype(F32), own_choice)
    choice_tile = jnp.broadcast_to(own_choice, (16, 128)).astype(BF16)

    for q in range(BLK_DEV):
        want = q * BCELLS + (lane & (BCELLS - 1))
        copies[:, q * 128 : (q + 1) * 128] = jnp.where(iota((128, 128), 0) == want, 1.0, 0.0).astype(BF16)

    loads[0].wait()
    held = coarse_v[...].astype(F32)
    tile = jnp.zeros((VARS, 128), F32)
    for b in range(BLK_DEV):
        put = jnp.where(iota((BCELLS, 128), 0) + b * BCELLS == iota((BCELLS, 128), 1), 1.0, 0.0)
        tile = tile + dot(held[:, b, :].astype(BF16), put.astype(BF16))
    pad = jnp.concatenate([tile, jnp.zeros((16 - VARS, 128), F32)], axis=0)
    tt[2] = pad.astype(BF16)

    loads[1].wait()
    at = iota((224, 1), 0)
    inner = at & 15
    cell = at + odd * (7 * COLS_DEV)
    column = (inner & 7) * COLS_DEV + (inner >> 3)
    cell = jnp.where((at >= 128) & (at < 144), column + 126, cell)
    cell = jnp.where((at >= 144) & (at < 160), column, cell)
    for i, (row0, col0) in enumerate(((6 * odd, 126), (6 * odd, 0), (6 - 6 * odd, 126), (6 - 6 * odd, 0))):
        here = jnp.where(inner < 4, (row0 + (inner >> 1)) * COLS_DEV + col0 + (inner & 1), -1)
        cell = jnp.where((at >= 160 + 16 * i) & (at < 176 + 16 * i), here, cell)
    pick = jnp.where(iota((224, 1024), 1) == cell, 1.0, 0.0).astype(BF16)
    weights = dot(pick, remap_v[...], ((1,), (1,))).astype(BF16)
    row_out[...] = weights[0:128]
    choice_out[...] = own_choice
    for i in range(2):
        col_out[i, 0:16, :] = weights[128 + 16 * i : 144 + 16 * i]
        col_out[i, 16:32, :] = choice_tile
    for i in range(4):
        cells = weights[160 + 16 * i : 176 + 16 * i].astype(F32)
        corner_out[i] = jnp.where(iota((8, 128), 0) < 4, cells[0:8], own_choice)
    side[...] = jnp.zeros_like(side)
    hl[...] = jnp.zeros_like(hl)
    xs[...] = jnp.zeros_like(xs)

    loads[2].wait()
    wa32[...] = jnp.zeros_like(wa32)
    for dy in range(3):
        for part in range(3):
            first = (dy * 3 + part) * VARS
            for dx in range(3):
                wa32[first : first + VARS, dx * CH : (dx + 1) * CH] = ca_v[dy, dx]
    line = iota((128, 3 * CH), 0)
    twelfth = (line * 43) >> 9
    part_of = twelfth - 3 * ((twelfth * 11) >> 5)
    whole = wa32[...]
    high, low = split(whole)
    wa[...] = jnp.where(part_of == 2, low.astype(F32), high.astype(F32)).astype(BF16)

    twelfth_l = (lane * 43) >> 9
    var_l = jnp.where(lane < 9 * VARS, lane - 12 * twelfth_l, 4096)
    part_l = twelfth_l - 3 * ((twelfth_l * 11) >> 5)
    want = jnp.where(part_l == 1, var_l + 16, var_l)
    spread_msg = jnp.where(iota((32, 128), 0) == want, 1.0, 0.0).astype(BF16)
    spread_var = jnp.where(iota((16, 128), 0) == var_l, 1.0, 0.0).astype(BF16)
    not_first = jnp.where(row > 0, 1.0, 0.0).astype(F32)
    not_last = jnp.where(row < 15, 1.0, 0.0).astype(F32)

    pl.semaphore_wait(barrier, len(partners))

    def send(src, dst, mate, out, into):
        copy = pltpu.make_async_remote_copy(
            src_ref=src, dst_ref=dst, send_sem=send_sem.at[out], recv_sem=recv_sem.at[into],
            device_id=mate, device_id_type=MESH,
        )
        copy.start()

    for i in range(2):
        send(col_out.at[i], col_in.at[i], halo[6 + i], 8, 2)
    for i in range(4):
        out, into = (1, 1) if i < 2 else (9, 12)
        send(corner_out.at[i, pl.ds(0, 5)], corner_in.at[i, pl.ds(0, 5)], halo[(1, 2, 4, 5)[i]], out, into)
    send(row_out, row_in, halo[0], 0, 0)
    send(choice_out, choice_in, halo[0], 11, 14)
    along_lon = [
        pltpu.make_async_remote_copy(
            src_ref=tt.at[2], dst_ref=tt.at[slot], send_sem=send_sem.at[7], recv_sem=recv_sem.at[8 + i],
            device_id=mate, device_id_type=MESH,
        )
        for i, (slot, mate) in enumerate(zip((0, 1, 3, 4), lon_mates))
    ]
    for copy in along_lon:
        copy.start()

    for copy in along_lon:
        copy.wait_recv()
    choices[...] = dot(tt[...].reshape(80, 128), copies[...])

    def chosen(choice, first_tile):
        total = jnp.zeros((16, 128), F32)
        for j in range(3 * BLK_DEV):
            t, q = first_tile + j // BLK_DEV, j % BLK_DEV
            total = jnp.where(choice == j, choices[t * 16 : t * 16 + 16, q * 128 : (q + 1) * 128], total)
        return total

    blocks = chosen(own_choice, 1).astype(BF16)

    four = jnp.concatenate([remap_v[:, 0:256], remap_v[:, 768:1024]], axis=1)
    four = dot(blocks, four)
    mate_out[0] = jnp.where(is_odd, four[:, 0:128], four[:, 384:512])
    mate_out[1] = jnp.where(is_odd, four[:, 128:256], four[:, 256:384])
    next_out[...] = jnp.where(is_odd, four[:, 256:384], four[:, 128:256])
    send(next_out, next_in, halo[0], 10, 13)
    send(mate_out, mate_in, halo[3], 2, 3)

    spread_blocks = dot(blocks, spread_var, ((0,), (0,))).astype(BF16)
    fine = dot(remap_v[...], spread_blocks, ((0,), (0,)))
    high, low = split(fine)
    packed = jnp.where(part_l == 1, low.astype(F32), high.astype(F32)).astype(BF16)
    xs[2:10] = packed.reshape(ROWS_DEV, COLS_DEV, 128)

    third = jnp.broadcast_to(lane, (128, 128))

    def patches(before, here, after, lanes):
        before = jnp.where(lanes < 3 * VARS, before.astype(F32), 0.0)
        here = jnp.where((lanes >= 3 * VARS) & (lanes < 6 * VARS), here.astype(F32), 0.0)
        after = jnp.where(lanes >= 6 * VARS, after.astype(F32), 0.0)
        return (before + here + after).astype(BF16)

    def taps(out_rows):
        field = [patches(xs[i], xs[i + 1], xs[i + 2], third) for i in out_rows]
        result = dot(jnp.concatenate(field, axis=0), wa[...])
        for n, i in enumerate(out_rows):
            for dx in range(3):
                gs[dx, i, MAIN:RIGHT, :] = result[n * 128 : (n + 1) * 128, dx * CH : (dx + 1) * CH]

    def joined(i, first, size):
        return gs[0, i, first - 1 : first - 1 + size, :] + gs[1, i, first : first + size, :] + gs[2, i, first + 1 : first + 1 + size, :]

    taps(list(range(2, 8)))

    def placed(fine):
        high, low = split(fine)
        return dot(jnp.concatenate([high, low], axis=0), spread_msg, ((0,), (0,))).astype(BF16)

    pltpu.make_async_copy(mate_in, mate_in, recv_sem.at[3]).wait()
    xs[10 - 9 * odd] = placed(mate_in[0])
    xs[11 - 11 * odd] = placed(mate_in[1])

    far_known = jnp.where(is_odd, not_last, not_first)

    def fine_of(cells, choice, first_tile, known):
        held = chosen(choice.astype(F32), first_tile) * known
        return dot(cells.astype(BF16), held.astype(BF16), ((1,), (1,)))

    def spread_cells(parts):
        high, low = split(jnp.concatenate(parts, axis=0))
        return dot(jnp.concatenate([high, low], axis=1), spread_msg)

    def put_corner(cells, first_row, place):
        for n in range(4):
            side[first_row + (n >> 1), place + (n & 1) : place + (n & 1) + 1, :] = cells[n : n + 1]

    def corners(first):
        some = corner_in.at[pl.ds(first, 2), pl.ds(0, 5)]
        return pltpu.make_async_copy(some, some, recv_sem.at[1 if first == 0 else 12])

    pltpu.make_async_copy(col_in, col_in, recv_sem.at[2]).wait()
    corners(2).wait()
    cells = spread_cells([
        fine_of(col_in[0, 0:16, :], col_in[0, 16:17, :], 0, 1.0),
        fine_of(col_in[1, 0:16, :], col_in[1, 16:17, :], 2, 1.0),
        fine_of(corner_in[2], corner_in[2, 4:5, :], 0, 1.0),
        fine_of(corner_in[3], corner_in[3, 4:5, :], 2, 1.0),
    ])
    for i, place_at in enumerate((6, 0)):
        for n in range(16):
            at_col = place_at + (n >> 3)
            side[(n & 7) + 2, at_col : at_col + 1, :] = cells[16 * i + n : 16 * i + n + 1]
    put_corner(cells[32:40], 10 - 10 * odd, 6)
    put_corner(cells[40:48], 10 - 10 * odd, 0)
    near_border, far_border, near_beyond, far_beyond = 8 - 7 * odd, 1 + 7 * odd, 9 - 9 * odd, 9 * odd
    taps([near_border])

    def side_taps():
        side_lane = jnp.broadcast_to(lane.reshape(1, 1, 128), (10, 8, 128))
        side_patches = patches(side[0:10], side[1:11], side[2:12], side_lane).reshape(80, 128)
        result = dot(side_patches, wa[...]).reshape(10, 8, 3 * CH)
        for dx in range(3):
            piece = result[:, :, dx * CH : (dx + 1) * CH]
            gs[dx, :, LEFT:MAIN, :] = piece
            gs[dx, :, RIGHT : RIGHT + 8, :] = piece

    side_taps()
    inner_rows = [2, 3, 4, 5, 6, 7, near_border]
    for i in inner_rows:
        ha[i, MAIN:RIGHT, :] = joined(i, MAIN, 128)
    about = row_mean(ha[2, MAIN:RIGHT, :])
    first, second = add_rows([ha[i, MAIN:RIGHT, :] for i in inner_rows], about)

    corners(0).wait()
    pltpu.make_async_copy(choice_in, choice_in, recv_sem.at[14]).wait()
    pltpu.make_async_copy(row_in, row_in, recv_sem.at[0]).wait()
    cells = spread_cells([
        fine_of(row_in[...], choice_in[...], 1, far_known),
        fine_of(corner_in[0], corner_in[0, 4:5, :], 0, far_known),
        fine_of(corner_in[1], corner_in[1, 4:5, :], 2, far_known),
    ])
    xs[1 + 9 * odd] = cells[0:128].astype(BF16)
    put_corner(cells[128:136], 10 * odd, 6)
    put_corner(cells[136:144], 10 * odd, 0)
    side_taps()
    taps([far_border])
    border = joined(far_border, MAIN, 128)
    ha[far_border, MAIN:RIGHT, :] = border
    mean, dev = channel_stats(about, *add_rows([border], about, first, second))

    def all_reduce(turn, mean, dev, beside):
        cells = ROWS_DEV * COLS_DEV
        for stage, (mates, buf) in enumerate(((z_mates, buf_z), (xy_mates, buf_x))):
            sem = 4 + turn * 2 + stage
            stat[turn, stage, 0:1, :] = mean
            stat[turn, stage, 1:2, :] = dev
            for j, mate in enumerate(mates):
                pltpu.make_async_remote_copy(
                    src_ref=stat.at[turn, stage], dst_ref=buf.at[turn, j], send_sem=send_sem.at[sem - 1], recv_sem=recv_sem.at[sem],
                    device_id=mate, device_id_type=MESH,
                ).start()
            if stage == 0:
                beside()
            pltpu.make_async_copy(buf.at[turn], buf.at[turn], recv_sem.at[sem]).wait()
            mean, dev = merge(mean, dev, buf[turn], cells)
            cells = cells * (len(mates) + 1)
        return to_groups(mean, dev, cells)

    def around_a():
        for load in loads[3:]:
            load.wait()
        prepare_b(cb_v, wba, wbb)
        pltpu.make_async_copy(next_in, next_in, recv_sem.at[13]).wait()
        xs[11 * odd] = placed(next_in[...] * far_known)
        taps([near_beyond, far_beyond])
        for i in (near_beyond, far_beyond):
            ha[i, MAIN:RIGHT, :] = joined(i, MAIN, 128)
        for i in range(10):
            hl[0, i : i + 1, :] = joined(i, MAIN - 1, 1)
            hl[1, i : i + 1, :] = joined(i, RIGHT, 1)

    mean, inverse = all_reduce(0, mean, dev, around_a)

    second_conv(ha, hl, act, gs, hb, wba, wbb, mean, inverse * vec_v[0], vec_v[1], not_first, not_last)
    store = pltpu.make_async_copy(hb, hb_ref, out_sem)
    store.start()
    about = row_mean(hb[0])
    mean, dev = channel_stats(about, *add_rows([hb[i] for i in range(8)], about))
    mean, inverse = all_reduce(1, mean, dev, lambda: None)
    fin_ref[0:1, :] = mean
    fin_ref[1:2, :] = inverse * vec_v[2]
    fin_ref[2:3, :] = vec_v[3]
    store.wait()

    pltpu.make_async_copy(row_in, row_in, send_sem.at[0]).wait()
    pltpu.make_async_copy(choice_in, choice_in, send_sem.at[11]).wait()
    pltpu.make_async_copy(next_in, next_in, send_sem.at[10]).wait()
    for first, sem in ((0, 1), (2, 9)):
        some = corner_in.at[pl.ds(first, 2), pl.ds(0, 5)]
        pltpu.make_async_copy(some, some, send_sem.at[sem]).wait()
    pltpu.make_async_copy(col_in, col_in, send_sem.at[8]).wait()
    pltpu.make_async_copy(mate_in, mate_in, send_sem.at[2]).wait()
    pltpu.make_async_copy(tt.at[pl.ds(0, 4)], tt.at[pl.ds(0, 4)], send_sem.at[7]).wait()
    for turn in range(2):
        pltpu.make_async_copy(buf_z.at[turn], buf_z.at[turn], send_sem.at[3 + 2 * turn]).wait()
        pltpu.make_async_copy(buf_x.at[turn], buf_x.at[turn], send_sem.at[4 + 2 * turn]).wait()


def per_device(
    coarse, src_blocks, slot_counts, remap_tiles, conv_a, conv_b, gain_a, shift_a, gain_b, shift_b
):
    anywhere = pl.BlockSpec(memory_space=pl.ANY)
    vectors = [v.reshape(1, CH) for v in (gain_a, shift_a, gain_b, shift_b)]
    hidden, final = pl.pallas_call(
        kernel,
        name="stem",
        out_shape=(
            pltpu.VMEM((ROWS_DEV, COLS_DEV, CH), F32),
            pltpu.VMEM((3, CH), F32),
        ),
        in_specs=[anywhere, pl.BlockSpec(memory_space=pltpu.SMEM)] + [anywhere] * 8,
        out_specs=(anywhere, pl.BlockSpec(memory_space=pltpu.VMEM)),
        scratch_shapes=[
            pltpu.SMEM((1, SLOTS), jnp.int32),
            pltpu.VMEM((VARS, BLK_DEV, BCELLS), BF16),
            pltpu.VMEM((128, 1024), BF16),
            pltpu.VMEM((3, 3, VARS, CH), F32),
            pltpu.VMEM((3, 3, CH, CH), F32),
            pltpu.VMEM((4, 1, CH), F32),
            pltpu.VMEM((5, 16, 128), BF16),
            pltpu.VMEM((128, 128), BF16),
            pltpu.VMEM((2, 32, 128), BF16),
            pltpu.VMEM((4, 8, 128), F32),
            pltpu.VMEM((2, 16, 128), F32),
            pltpu.VMEM((16, 128), F32),
            pltpu.VMEM((1, 128), F32),
            pltpu.VMEM((128, 128), BF16),
            pltpu.VMEM((2, 32, 128), BF16),
            pltpu.VMEM((4, 8, 128), F32),
            pltpu.VMEM((2, 16, 128), F32),
            pltpu.VMEM((16, 128), F32),
            pltpu.VMEM((1, 128), F32),
            pltpu.VMEM((128, BLK_DEV * 128), BF16),
            pltpu.VMEM((80, BLK_DEV * 128), F32),
            pltpu.VMEM((12, 8, 128), F32),
            pltpu.VMEM((128, 3 * CH), F32),
            pltpu.VMEM((128, 3 * CH), BF16),
            pltpu.VMEM((9 * CH, 2 * CH), BF16),
            pltpu.VMEM((6 * CH, 2 * CH), BF16),
            pltpu.VMEM((12, COLS_DEV, 128), BF16),
            pltpu.VMEM((3, 10, WIDE, CH), F32),
            pltpu.VMEM((10, WIDE, CH), F32),
            pltpu.VMEM((2, 24, CH), F32),
            pltpu.VMEM((10, COLS_DEV, 2 * CH), BF16),
            pltpu.VMEM((ROWS_DEV, COLS_DEV, CH), F32),
            pltpu.VMEM((2, 2, 2, CH), F32),
            pltpu.VMEM((2, 15, 2, CH), F32),
            pltpu.VMEM((2, 31, 2, CH), F32),
            pltpu.SemaphoreType.DMA((9,)),
            pltpu.SemaphoreType.DMA,
            pltpu.SemaphoreType.DMA((12,)),
            pltpu.SemaphoreType.DMA((15,)),
        ],
        compiler_params=pltpu.CompilerParams(
            collective_id=0, has_side_effects=True, vmem_limit_bytes=60 * 1024 * 1024
        ),
    )(
        src_blocks, slot_counts, jnp.transpose(coarse, (1, 0, 2)), remap_tiles.reshape(SLOTS * BCELLS, 1024),
        conv_a, conv_b, *vectors,
    )
    normed = (hidden - final[0]) * final[1] + final[2]
    return jax.nn.silu(normed).astype(BF16)


def solution(mesh):
    return jax.shard_map(
        per_device,
        mesh=mesh,
        in_specs=(
            P("lon", None, None),
            P(("row", "lon"), None),
            P(("row", "lon")),
            P(("row", "lon"), None, None, None),
            P(),
            P(),
            P(),
            P(),
            P(),
            P(),
        ),
        out_specs=P("row", "lon", None),
        check_vma=False,
    )
```

```python
import jax
import jax.numpy as jnp
from jax import lax
from jax.experimental import pallas as pl
from jax.experimental.pallas import tpu as pltpu
from jax.sharding import PartitionSpec as P

ROWS_DEV = 8
COLS_DEV = 128
VARS = 12
CH = 128
GROUPS = 32
SLOTS = 4
BCELLS = 32
BLK_DEV = 4
NBLK = 128
PER_GROUP = CH // GROUPS
MESH = pl.DeviceIdType.MESH
F32 = jnp.float32
BF16 = jnp.bfloat16

eps = 1e-05


def coords():
    row = lax.axis_index("row")
    lon = lax.axis_index("lon")
    core = lax.rem(row, 2)
    z_hi = lax.rem(lax.div(row, 2), 2)
    x = lax.div(row, 4)
    y = lax.div(lon, 8)
    z = z_hi * 8 + lax.rem(lon, 8)
    return row, lon, x, y, z, core


def device_at(x, y, z, core):
    return (x * 4 + lax.div(z, 8) * 2 + core, y * 8 + lax.rem(z, 8))


def moved(value, step, count):
    return lax.rem(value + step, count) if step else value


def along_z(place):
    _, _, x, y, z, core = place
    steps = [(d, c) for d in range(16) for c in range(2) if d or c]
    steps.sort(key=lambda s: -min(s[0], 16 - s[0]))
    return [device_at(x, y, moved(z, d, 16), moved(core, c, 2)) for d, c in steps]


def across(place):
    _, _, x, y, z, core = place
    steps = [(a, b) for a in range(4) for b in range(4) if a or b]
    steps.sort(key=lambda s: -(min(s[0], 4 - s[0]) + min(s[1], 4 - s[1])))
    return [device_at(moved(x, a, 4), moved(y, b, 4), z, core) for a, b in steps]


def coarse_mates(place):
    _, _, x, y, z, core = place
    z_lo = lax.rem(z, 8)
    mates = []
    for step in (2, 1, -1, -2):
        turn = lax.rem(y + 3 + lax.div(z_lo + 8 + step, 8), 4)
        mates.append(device_at(x, turn, lax.rem(z + 16 + step, 16), core))
    return mates


def iota(shape, dim):
    return lax.broadcasted_iota(jnp.int32, shape, dim)


def split(value):
    high = value.astype(BF16)
    low = (value - high.astype(F32)).astype(BF16)
    return high, low


def dot(a, b, dims=((1,), (0,))):
    return lax.dot_general(a, b, (dims, ((), ())), preferred_element_type=F32)


def over_group(row):
    place = iota(row.shape, 1) & (PER_GROUP - 1)
    total = row
    for step in range(1, PER_GROUP):
        after = pltpu.roll(row, CH - step, 1)
        before = pltpu.roll(row, step, 1)
        total = total + jnp.where(place < PER_GROUP - step, after, 0.0) + jnp.where(place >= step, before, 0.0)
    return total


def add_rows(rows, about, first=0.0, second=0.0):
    for r in rows:
        off = r - about
        first = first + off
        second = second + off * off
    return first, second


def row_mean(r):
    return jnp.sum(r, axis=0, keepdims=True) * (1.0 / r.shape[0])


def channel_stats(about, first, second):
    cells = ROWS_DEV * COLS_DEV
    first = jnp.sum(first, axis=0, keepdims=True)
    mean_off = first * (1.0 / cells)
    return about + mean_off, jnp.sum(second, axis=0, keepdims=True) - first * mean_off


def to_groups(mean, dev, cells):
    whole = over_group(mean) * (1.0 / PER_GROUP)
    apart = mean - whole
    spread = over_group(dev + cells * (apart * apart)) * (1.0 / (cells * PER_GROUP))
    return whole, lax.rsqrt(spread + eps)


def merge(mean, dev, others, cells):
    count = others.shape[0] + 1
    off = others[:, 0:1, :] - mean
    first = jnp.sum(off, axis=0)
    second = jnp.sum(others[:, 1:2, :] + cells * (off * off), axis=0)
    mean_off = first * (1.0 / count)
    return mean + mean_off, dev + second - cells * first * mean_off


LEFT, MAIN, RIGHT, WIDE = 8, 16, 144, 160


def prepare_b(cb_v, wba, wbb):
    for dy in range(3):
        for dx in range(2):
            span = slice(dx * CH, (dx + 1) * CH)
            high, low = split(cb_v[dy, dx])
            wba[dy * 256 : dy * 256 + 128, span] = high
            wba[dy * 256 + 128 : dy * 256 + 256, span] = high
            wba[768 + dy * 128 : 896 + dy * 128, span] = low
        high, low = split(cb_v[dy, 2])
        for part, value in enumerate((high, high, low)):
            if dy < 2:
                wbb[part * 256 + dy * 128 : part * 256 + dy * 128 + 128, 0:CH] = value
            else:
                wbb[part * 256 : part * 256 + 128, CH : 2 * CH] = jnp.zeros((CH, CH), BF16)
                wbb[part * 256 + 128 : part * 256 + 256, CH : 2 * CH] = value


def activate(value, mean, scale, shift):
    half = ((value - mean) * scale + shift) * 0.5
    return half + half * jnp.tanh(half)


def second_conv(ha, hl, act, gs, hb, wba, wbb, mean, scale, shift, not_first, not_last):
    for i in range(10):
        value = activate(ha[i, MAIN:RIGHT, :], mean, scale, shift)
        if i == 0:
            value = value * not_first
        if i == 9:
            value = value * not_last
        act[i, :, 0:128], act[i, :, 128:256] = split(value)
    known = iota((16, 1), 0)
    known = jnp.where(known == 0, not_first, jnp.where(known == 9, not_last, 1.0))
    for i in range(2):
        hl[i, 0:16, :] = activate(hl[i, 0:16, :], mean, scale, shift) * known

    def side(i, dy):
        return split(hl[i, dy : dy + 16, :])

    def rows(first, size, part):
        return act[first : first + size, :, part * 128 : part * 128 + 128].reshape(size * 128, 128)

    pieces = [act[dy : dy + 8].reshape(1024, 256) for dy in range(3)] + [rows(dy, 8, 0) for dy in range(3)]
    at_side = [side(0, dy) for dy in range(3)]
    at_side = [part for pair in at_side for part in pair] + [pair[0] for pair in at_side]
    field = jnp.concatenate([jnp.concatenate(pieces, axis=1), jnp.concatenate(at_side, axis=1)], axis=0)
    early = dot(field, wba[...])

    pieces = [rows(0, 9, 0), rows(1, 9, 0), rows(0, 9, 1), rows(1, 9, 1), rows(0, 9, 0), rows(1, 9, 0)]
    (high0, low0), (high1, low1) = side(1, 0), side(1, 1)
    at_side = [high0, high1, low0, low1, high0, high1]
    field = jnp.concatenate([jnp.concatenate(pieces, axis=1), jnp.concatenate(at_side, axis=1)], axis=0)
    late = dot(field, wbb[...])

    for i in range(8):
        gs[0, i, MAIN:RIGHT, :] = early[i * 128 : (i + 1) * 128, 0:128]
        gs[0, i, MAIN - 1 : MAIN, :] = early[1024 + i : 1025 + i, 0:128]
        gs[2, i, MAIN:RIGHT, :] = late[i * 128 : (i + 1) * 128, 0:128] + late[(i + 1) * 128 : (i + 2) * 128, 128:256]
        gs[2, i, RIGHT : RIGHT + 1, :] = late[1152 + i : 1153 + i, 0:128] + late[1153 + i : 1154 + i, 128:256]
        hb[i] = gs[0, i, MAIN - 1 : RIGHT - 1, :] + early[i * 128 : (i + 1) * 128, 128:256] + gs[2, i, MAIN + 1 : RIGHT + 1, :]


def kernel(
    src_hbm, cnt_ref, coarse_ref, remap_ref, ca_ref, cb_ref, gain_a_ref, shift_a_ref, gain_b_ref, shift_b_ref,
    hb_ref, fin_ref,
    src_ref, coarse_v, remap_v, ca_v, cb_v, vec_v,
    tt, row_out, col_out, corner_out, mate_out, next_out, choice_out,
    row_in, col_in, corner_in, mate_in, next_in, choice_in,
    copies, choices, side, wa32, wa, wba, wbb,
    xs, gs, ha, hl, act, hb,
    stat, buf_x, buf_z,
    in_sem, out_sem, send_sem, recv_sem,
):
    place = coords()
    row, lon = place[0], place[1]
    z_mates = along_z(place)
    xy_mates = across(place)
    lon_mates = coarse_mates(place)
    lon_left, lon_right = lax.rem(lon + 31, 32), lax.rem(lon + 1, 32)
    odd = lax.rem(row, 2)
    is_odd = odd == 1
    has_far = jnp.where(is_odd, row < 15, row > 0)
    near_row = row + 1 - 2 * odd
    far_row = lax.rem(row + 2 * odd + 15, 16)
    halo = [
        (far_row, lon), (far_row, lon_right), (far_row, lon_left), (near_row, lon),
        (near_row, lon_right), (near_row, lon_left), (row, lon_right), (row, lon_left),
    ]
    barrier = pltpu.get_barrier_semaphore()
    partners = halo[3:] + lon_mates + z_mates + xy_mates

    @pl.when(has_far)
    def _():
        for mate in halo[:3]:
            pl.semaphore_signal(barrier, inc=1, device_id=mate, device_id_type=MESH)

    for mate in partners:
        pl.semaphore_signal(barrier, inc=1, device_id=mate, device_id_type=MESH)

    loads = [
        pltpu.make_async_copy(coarse_ref, coarse_v, in_sem.at[0]),
        pltpu.make_async_copy(remap_ref, remap_v, in_sem.at[1]),
        pltpu.make_async_copy(ca_ref, ca_v, in_sem.at[2]),
        pltpu.make_async_copy(cb_ref, cb_v, in_sem.at[3]),
    ]
    for i, ref in enumerate((gain_a_ref, shift_a_ref, gain_b_ref, shift_b_ref)):
        loads.append(pltpu.make_async_copy(ref, vec_v.at[i], in_sem.at[4 + i]))
    sources = pltpu.make_async_copy(src_hbm, src_ref, in_sem.at[8])
    for load in [sources] + loads:
        load.start()

    sources.wait()
    lane = iota((1, 128), 1)
    own_choice = jnp.zeros((1, 128), F32)
    for k in range(SLOTS):
        local = lax.rem(src_ref[0, k] - (lon - 1) * BLK_DEV + 2 * NBLK, NBLK)
        local = jnp.where(k < cnt_ref[0], local, -64)
        own_choice = jnp.where((lane >> 5) == k, local.astype(F32), own_choice)
    choice_tile = jnp.broadcast_to(own_choice, (16, 128)).astype(BF16)

    for q in range(BLK_DEV):
        want = q * BCELLS + (lane & (BCELLS - 1))
        copies[:, q * 128 : (q + 1) * 128] = jnp.where(iota((128, 128), 0) == want, 1.0, 0.0).astype(BF16)

    loads[0].wait()
    held = coarse_v[...].astype(F32)
    tile = jnp.zeros((VARS, 128), F32)
    for b in range(BLK_DEV):
        put = jnp.where(iota((BCELLS, 128), 0) + b * BCELLS == iota((BCELLS, 128), 1), 1.0, 0.0)
        tile = tile + dot(held[:, b, :].astype(BF16), put.astype(BF16))
    pad = jnp.concatenate([tile, jnp.zeros((16 - VARS, 128), F32)], axis=0)
    tt[2] = pad.astype(BF16)

    loads[1].wait()
    at = iota((224, 1), 0)
    inner = at & 15
    cell = at + odd * (7 * COLS_DEV)
    column = (inner & 7) * COLS_DEV + (inner >> 3)
    cell = jnp.where((at >= 128) & (at < 144), column + 126, cell)
    cell = jnp.where((at >= 144) & (at < 160), column, cell)
    for i, (row0, col0) in enumerate(((6 * odd, 126), (6 * odd, 0), (6 - 6 * odd, 126), (6 - 6 * odd, 0))):
        here = jnp.where(inner < 4, (row0 + (inner >> 1)) * COLS_DEV + col0 + (inner & 1), -1)
        cell = jnp.where((at >= 160 + 16 * i) & (at < 176 + 16 * i), here, cell)
    pick = jnp.where(iota((224, 1024), 1) == cell, 1.0, 0.0).astype(BF16)
    weights = dot(pick, remap_v[...], ((1,), (1,))).astype(BF16)
    row_out[...] = weights[0:128]
    choice_out[...] = own_choice
    for i in range(2):
        col_out[i, 0:16, :] = weights[128 + 16 * i : 144 + 16 * i]
        col_out[i, 16:32, :] = choice_tile
    for i in range(4):
        cells = weights[160 + 16 * i : 176 + 16 * i].astype(F32)
        corner_out[i] = jnp.where(iota((8, 128), 0) < 4, cells[0:8], own_choice)
    side[...] = jnp.zeros_like(side)
    hl[...] = jnp.zeros_like(hl)
    xs[...] = jnp.zeros_like(xs)

    loads[2].wait()
    wa32[...] = jnp.zeros_like(wa32)
    for dy in range(3):
        for part in range(3):
            first = (dy * 3 + part) * VARS
            for dx in range(3):
                wa32[first : first + VARS, dx * CH : (dx + 1) * CH] = ca_v[dy, dx]
    line = iota((128, 3 * CH), 0)
    twelfth = (line * 43) >> 9
    part_of = twelfth - 3 * ((twelfth * 11) >> 5)
    whole = wa32[...]
    high, low = split(whole)
    wa[...] = jnp.where(part_of == 2, low.astype(F32), high.astype(F32)).astype(BF16)

    twelfth_l = (lane * 43) >> 9
    var_l = jnp.where(lane < 9 * VARS, lane - 12 * twelfth_l, 4096)
    part_l = twelfth_l - 3 * ((twelfth_l * 11) >> 5)
    want = jnp.where(part_l == 1, var_l + 16, var_l)
    spread_msg = jnp.where(iota((32, 128), 0) == want, 1.0, 0.0).astype(BF16)
    spread_var = jnp.where(iota((16, 128), 0) == var_l, 1.0, 0.0).astype(BF16)
    not_first = jnp.where(row > 0, 1.0, 0.0).astype(F32)
    not_last = jnp.where(row < 15, 1.0, 0.0).astype(F32)

    @pl.when(jnp.logical_not(has_far))
    def _():
        row_in[...] = jnp.zeros_like(row_in)
        choice_in[...] = jnp.zeros_like(choice_in)
        next_in[...] = jnp.zeros_like(next_in)
        corner_in[0:2] = jnp.zeros((2, 8, 128), F32)

    pl.semaphore_wait(barrier, len(partners) + 3 * jnp.where(has_far, 1, 0))

    def send(src, dst, mate, out, into):
        copy = pltpu.make_async_remote_copy(
            src_ref=src, dst_ref=dst, send_sem=send_sem.at[out], recv_sem=recv_sem.at[into],
            device_id=mate, device_id_type=MESH,
        )
        copy.start()

    for i in range(2):
        send(col_out.at[i], col_in.at[i], halo[6 + i], 8, 2)
    for i in (2, 3):
        send(corner_out.at[i, pl.ds(0, 5)], corner_in.at[i, pl.ds(0, 5)], halo[2 + i], 9, 12)

    @pl.when(has_far)
    def _():
        for i in (0, 1):
            send(corner_out.at[i, pl.ds(0, 5)], corner_in.at[i, pl.ds(0, 5)], halo[1 + i], 1, 1)
        send(row_out, row_in, halo[0], 0, 0)
        send(choice_out, choice_in, halo[0], 11, 14)

    along_lon = [
        pltpu.make_async_remote_copy(
            src_ref=tt.at[2], dst_ref=tt.at[slot], send_sem=send_sem.at[7], recv_sem=recv_sem.at[8 + i],
            device_id=mate, device_id_type=MESH,
        )
        for i, (slot, mate) in enumerate(zip((0, 1, 3, 4), lon_mates))
    ]
    for copy in along_lon:
        copy.start()

    for copy in along_lon:
        copy.wait_recv()
    choices[...] = dot(tt[...].reshape(80, 128), copies[...])

    def chosen(choice, first_tile):
        total = jnp.zeros((16, 128), F32)
        for j in range(3 * BLK_DEV):
            t, q = first_tile + j // BLK_DEV, j % BLK_DEV
            total = jnp.where(choice == j, choices[t * 16 : t * 16 + 16, q * 128 : (q + 1) * 128], total)
        return total

    blocks = chosen(own_choice, 1).astype(BF16)

    four = jnp.concatenate([remap_v[:, 0:256], remap_v[:, 768:1024]], axis=1)
    four = dot(blocks, four)
    mate_out[0] = jnp.where(is_odd, four[:, 0:128], four[:, 384:512])
    mate_out[1] = jnp.where(is_odd, four[:, 128:256], four[:, 256:384])
    next_out[...] = jnp.where(is_odd, four[:, 256:384], four[:, 128:256])
    send(mate_out, mate_in, halo[3], 2, 3)

    @pl.when(has_far)
    def _():
        send(next_out, next_in, halo[0], 10, 13)


    spread_blocks = dot(blocks, spread_var, ((0,), (0,))).astype(BF16)
    fine = dot(remap_v[...], spread_blocks, ((0,), (0,)))
    high, low = split(fine)
    packed = jnp.where(part_l == 1, low.astype(F32), high.astype(F32)).astype(BF16)
    xs[2:10] = packed.reshape(ROWS_DEV, COLS_DEV, 128)

    third = jnp.broadcast_to(lane, (128, 128))

    def patches(before, here, after, lanes):
        before = jnp.where(lanes < 3 * VARS, before.astype(F32), 0.0)
        here = jnp.where((lanes >= 3 * VARS) & (lanes < 6 * VARS), here.astype(F32), 0.0)
        after = jnp.where(lanes >= 6 * VARS, after.astype(F32), 0.0)
        return (before + here + after).astype(BF16)

    def taps(out_rows):
        field = [patches(xs[i], xs[i + 1], xs[i + 2], third) for i in out_rows]
        result = dot(jnp.concatenate(field, axis=0), wa[...])
        for n, i in enumerate(out_rows):
            for dx in range(3):
                gs[dx, i, MAIN:RIGHT, :] = result[n * 128 : (n + 1) * 128, dx * CH : (dx + 1) * CH]

    def joined(i, first, size):
        return gs[0, i, first - 1 : first - 1 + size, :] + gs[1, i, first : first + size, :] + gs[2, i, first + 1 : first + 1 + size, :]

    taps(list(range(2, 8)))

    def placed(fine):
        high, low = split(fine)
        return dot(jnp.concatenate([high, low], axis=0), spread_msg, ((0,), (0,))).astype(BF16)

    pltpu.make_async_copy(mate_in, mate_in, recv_sem.at[3]).wait()
    xs[10 - 9 * odd] = placed(mate_in[0])
    xs[11 - 11 * odd] = placed(mate_in[1])

    far_known = jnp.where(is_odd, not_last, not_first)

    def fine_of(cells, choice, first_tile, known):
        held = chosen(choice.astype(F32), first_tile) * known
        return dot(cells.astype(BF16), held.astype(BF16), ((1,), (1,)))

    def spread_cells(parts):
        high, low = split(jnp.concatenate(parts, axis=0))
        return dot(jnp.concatenate([high, low], axis=1), spread_msg)

    def put_corner(cells, first_row, place):
        for n in range(4):
            side[first_row + (n >> 1), place + (n & 1) : place + (n & 1) + 1, :] = cells[n : n + 1]

    def corners(first):
        some = corner_in.at[pl.ds(first, 2), pl.ds(0, 5)]
        return pltpu.make_async_copy(some, some, recv_sem.at[1 if first == 0 else 12])

    pltpu.make_async_copy(col_in, col_in, recv_sem.at[2]).wait()
    corners(2).wait()
    cells = spread_cells([
        fine_of(col_in[0, 0:16, :], col_in[0, 16:17, :], 0, 1.0),
        fine_of(col_in[1, 0:16, :], col_in[1, 16:17, :], 2, 1.0),
        fine_of(corner_in[2], corner_in[2, 4:5, :], 0, 1.0),
        fine_of(corner_in[3], corner_in[3, 4:5, :], 2, 1.0),
    ])
    for i, place_at in enumerate((6, 0)):
        for n in range(16):
            at_col = place_at + (n >> 3)
            side[(n & 7) + 2, at_col : at_col + 1, :] = cells[16 * i + n : 16 * i + n + 1]
    put_corner(cells[32:40], 10 - 10 * odd, 6)
    put_corner(cells[40:48], 10 - 10 * odd, 0)
    near_border, far_border, near_beyond, far_beyond = 8 - 7 * odd, 1 + 7 * odd, 9 - 9 * odd, 9 * odd
    taps([near_border])

    def side_taps():
        side_lane = jnp.broadcast_to(lane.reshape(1, 1, 128), (10, 8, 128))
        side_patches = patches(side[0:10], side[1:11], side[2:12], side_lane).reshape(80, 128)
        result = dot(side_patches, wa[...]).reshape(10, 8, 3 * CH)
        for dx in range(3):
            piece = result[:, :, dx * CH : (dx + 1) * CH]
            gs[dx, :, LEFT:MAIN, :] = piece
            gs[dx, :, RIGHT : RIGHT + 8, :] = piece

    side_taps()
    inner_rows = [2, 3, 4, 5, 6, 7, near_border]
    for i in inner_rows:
        ha[i, MAIN:RIGHT, :] = joined(i, MAIN, 128)
    about = row_mean(ha[2, MAIN:RIGHT, :])
    first, second = add_rows([ha[i, MAIN:RIGHT, :] for i in inner_rows], about)

    @pl.when(has_far)
    def _():
        corners(0).wait()
        pltpu.make_async_copy(choice_in, choice_in, recv_sem.at[14]).wait()
        pltpu.make_async_copy(row_in, row_in, recv_sem.at[0]).wait()

    cells = spread_cells([
        fine_of(row_in[...], choice_in[...], 1, far_known),
        fine_of(corner_in[0], corner_in[0, 4:5, :], 0, far_known),
        fine_of(corner_in[1], corner_in[1, 4:5, :], 2, far_known),
    ])
    xs[1 + 9 * odd] = cells[0:128].astype(BF16)
    put_corner(cells[128:136], 10 * odd, 6)
    put_corner(cells[136:144], 10 * odd, 0)
    side_taps()
    taps([far_border])
    border = joined(far_border, MAIN, 128)
    ha[far_border, MAIN:RIGHT, :] = border
    mean, dev = channel_stats(about, *add_rows([border], about, first, second))

    def all_reduce(turn, mean, dev, beside):
        cells = ROWS_DEV * COLS_DEV
        for stage, (mates, buf) in enumerate(((z_mates, buf_z), (xy_mates, buf_x))):
            sem = 4 + turn * 2 + stage
            stat[turn, stage, 0:1, :] = mean
            stat[turn, stage, 1:2, :] = dev
            for j, mate in enumerate(mates):
                pltpu.make_async_remote_copy(
                    src_ref=stat.at[turn, stage], dst_ref=buf.at[turn, j], send_sem=send_sem.at[sem - 1], recv_sem=recv_sem.at[sem],
                    device_id=mate, device_id_type=MESH,
                ).start()
            beside(stage)
            pltpu.make_async_copy(buf.at[turn], buf.at[turn], recv_sem.at[sem]).wait()
            mean, dev = merge(mean, dev, buf[turn], cells)
            cells = cells * (len(mates) + 1)
        return to_groups(mean, dev, cells)

    def around_a(stage):
        if stage == 0:

            for load in loads[3:]:
                load.wait()
            prepare_b(cb_v, wba, wbb)
            new_rows, all_rows = [near_beyond], list(range(1, 9)) + [near_beyond]
        else:

            @pl.when(has_far)
            def _():
                pltpu.make_async_copy(next_in, next_in, recv_sem.at[13]).wait()

            xs[11 * odd] = placed(next_in[...] * far_known)
            new_rows, all_rows = [far_beyond], [far_beyond]
        taps(new_rows)
        for i in new_rows:
            ha[i, MAIN:RIGHT, :] = joined(i, MAIN, 128)
        for i in all_rows:
            hl[0, pl.ds(i, 1), :] = joined(i, MAIN - 1, 1)
            hl[1, pl.ds(i, 1), :] = joined(i, RIGHT, 1)

    mean, inverse = all_reduce(0, mean, dev, around_a)

    second_conv(ha, hl, act, gs, hb, wba, wbb, mean, inverse * vec_v[0], vec_v[1], not_first, not_last)
    store = pltpu.make_async_copy(hb, hb_ref, out_sem)
    store.start()
    about = row_mean(hb[0])
    mean, dev = channel_stats(about, *add_rows([hb[i] for i in range(8)], about))
    mean, inverse = all_reduce(1, mean, dev, lambda stage: None)
    fin_ref[0:1, :] = mean
    fin_ref[1:2, :] = inverse * vec_v[2]
    fin_ref[2:3, :] = vec_v[3]
    store.wait()

    @pl.when(has_far)
    def _():
        pltpu.make_async_copy(row_in, row_in, send_sem.at[0]).wait()
        pltpu.make_async_copy(choice_in, choice_in, send_sem.at[11]).wait()
        pltpu.make_async_copy(next_in, next_in, send_sem.at[10]).wait()
        some = corner_in.at[pl.ds(0, 2), pl.ds(0, 5)]
        pltpu.make_async_copy(some, some, send_sem.at[1]).wait()

    some = corner_in.at[pl.ds(2, 2), pl.ds(0, 5)]
    pltpu.make_async_copy(some, some, send_sem.at[9]).wait()
    pltpu.make_async_copy(col_in, col_in, send_sem.at[8]).wait()
    pltpu.make_async_copy(mate_in, mate_in, send_sem.at[2]).wait()
    pltpu.make_async_copy(tt.at[pl.ds(0, 4)], tt.at[pl.ds(0, 4)], send_sem.at[7]).wait()
    for turn in range(2):
        pltpu.make_async_copy(buf_z.at[turn], buf_z.at[turn], send_sem.at[3 + 2 * turn]).wait()
        pltpu.make_async_copy(buf_x.at[turn], buf_x.at[turn], send_sem.at[4 + 2 * turn]).wait()


def per_device(
    coarse, src_blocks, slot_counts, remap_tiles, conv_a, conv_b, gain_a, shift_a, gain_b, shift_b
):
    anywhere = pl.BlockSpec(memory_space=pl.ANY)
    vectors = [v.reshape(1, CH) for v in (gain_a, shift_a, gain_b, shift_b)]
    hidden, final = pl.pallas_call(
        kernel,
        name="stem",
        out_shape=(
            pltpu.VMEM((ROWS_DEV, COLS_DEV, CH), F32),
            pltpu.VMEM((3, CH), F32),
        ),
        in_specs=[anywhere, pl.BlockSpec(memory_space=pltpu.SMEM)] + [anywhere] * 8,
        out_specs=(anywhere, pl.BlockSpec(memory_space=pltpu.VMEM)),
        scratch_shapes=[
            pltpu.SMEM((1, SLOTS), jnp.int32),
            pltpu.VMEM((VARS, BLK_DEV, BCELLS), BF16),
            pltpu.VMEM((128, 1024), BF16),
            pltpu.VMEM((3, 3, VARS, CH), F32),
            pltpu.VMEM((3, 3, CH, CH), F32),
            pltpu.VMEM((4, 1, CH), F32),
            pltpu.VMEM((5, 16, 128), BF16),
            pltpu.VMEM((128, 128), BF16),
            pltpu.VMEM((2, 32, 128), BF16),
            pltpu.VMEM((4, 8, 128), F32),
            pltpu.VMEM((2, 16, 128), F32),
            pltpu.VMEM((16, 128), F32),
            pltpu.VMEM((1, 128), F32),
            pltpu.VMEM((128, 128), BF16),
            pltpu.VMEM((2, 32, 128), BF16),
            pltpu.VMEM((4, 8, 128), F32),
            pltpu.VMEM((2, 16, 128), F32),
            pltpu.VMEM((16, 128), F32),
            pltpu.VMEM((1, 128), F32),
            pltpu.VMEM((128, BLK_DEV * 128), BF16),
            pltpu.VMEM((80, BLK_DEV * 128), F32),
            pltpu.VMEM((12, 8, 128), F32),
            pltpu.VMEM((128, 3 * CH), F32),
            pltpu.VMEM((128, 3 * CH), BF16),
            pltpu.VMEM((9 * CH, 2 * CH), BF16),
            pltpu.VMEM((6 * CH, 2 * CH), BF16),
            pltpu.VMEM((12, COLS_DEV, 128), BF16),
            pltpu.VMEM((3, 10, WIDE, CH), F32),
            pltpu.VMEM((10, WIDE, CH), F32),
            pltpu.VMEM((2, 24, CH), F32),
            pltpu.VMEM((10, COLS_DEV, 2 * CH), BF16),
            pltpu.VMEM((ROWS_DEV, COLS_DEV, CH), F32),
            pltpu.VMEM((2, 2, 2, CH), F32),
            pltpu.VMEM((2, 15, 2, CH), F32),
            pltpu.VMEM((2, 31, 2, CH), F32),
            pltpu.SemaphoreType.DMA((9,)),
            pltpu.SemaphoreType.DMA,
            pltpu.SemaphoreType.DMA((12,)),
            pltpu.SemaphoreType.DMA((15,)),
        ],
        compiler_params=pltpu.CompilerParams(
            collective_id=0, has_side_effects=True, vmem_limit_bytes=60 * 1024 * 1024
        ),
    )(
        src_blocks, slot_counts, jnp.transpose(coarse, (1, 0, 2)), remap_tiles.reshape(SLOTS * BCELLS, 1024),
        conv_a, conv_b, *vectors,
    )
    normed = (hidden - final[0]) * final[1] + final[2]
    return jax.nn.silu(normed).astype(BF16)


def solution(mesh):
    return jax.shard_map(
        per_device,
        mesh=mesh,
        in_specs=(
            P("lon", None, None),
            P(("row", "lon"), None),
            P(("row", "lon")),
            P(("row", "lon"), None, None, None),
            P(),
            P(),
            P(),
            P(),
            P(),
            P(),
        ),
        out_specs=P("row", "lon", None),
        check_vma=False,
    )
```

```python
import jax
import jax.numpy as jnp
from jax import lax
from jax.experimental import pallas as pl
from jax.experimental.pallas import tpu as pltpu
from jax.sharding import PartitionSpec as P

ROWS_DEV = 8
COLS_DEV = 128
VARS = 12
CH = 128
GROUPS = 32
SLOTS = 4
BCELLS = 32
BLK_DEV = 4
NBLK = 128
PER_GROUP = CH // GROUPS
MESH = pl.DeviceIdType.MESH
F32 = jnp.float32
BF16 = jnp.bfloat16

eps = 1e-05


def coords():
    row = lax.axis_index("row")
    lon = lax.axis_index("lon")
    core = lax.rem(row, 2)
    z_hi = lax.rem(lax.div(row, 2), 2)
    x = lax.div(row, 4)
    y = lax.div(lon, 8)
    z = z_hi * 8 + lax.rem(lon, 8)
    return row, lon, x, y, z, core


def device_at(x, y, z, core):
    return (x * 4 + lax.div(z, 8) * 2 + core, y * 8 + lax.rem(z, 8))


def moved(value, step, count):
    return lax.rem(value + step, count) if step else value


def along_z(place):
    _, _, x, y, z, core = place
    steps = [(d, c) for d in range(16) for c in range(2) if d or c]
    steps.sort(key=lambda s: -min(s[0], 16 - s[0]))
    return [device_at(x, y, moved(z, d, 16), moved(core, c, 2)) for d, c in steps]


def across(place):
    _, _, x, y, z, core = place
    steps = [(a, b) for a in range(4) for b in range(4) if a or b]
    steps.sort(key=lambda s: -(min(s[0], 4 - s[0]) + min(s[1], 4 - s[1])))
    return [device_at(moved(x, a, 4), moved(y, b, 4), z, core) for a, b in steps]


def coarse_mates(place):
    _, _, x, y, z, core = place
    z_lo = lax.rem(z, 8)
    mates = []
    for step in (2, 1, -1, -2):
        turn = lax.rem(y + 3 + lax.div(z_lo + 8 + step, 8), 4)
        mates.append(device_at(x, turn, lax.rem(z + 16 + step, 16), core))
    return mates


def iota(shape, dim):
    return lax.broadcasted_iota(jnp.int32, shape, dim)


def split(value):
    high = value.astype(BF16)
    low = (value - high.astype(F32)).astype(BF16)
    return high, low


def dot(a, b, dims=((1,), (0,))):
    return lax.dot_general(a, b, (dims, ((), ())), preferred_element_type=F32)


def over_group(row):
    place = iota(row.shape, 1) & (PER_GROUP - 1)
    total = row
    for step in range(1, PER_GROUP):
        after = pltpu.roll(row, CH - step, 1)
        before = pltpu.roll(row, step, 1)
        total = total + jnp.where(place < PER_GROUP - step, after, 0.0) + jnp.where(place >= step, before, 0.0)
    return total


def add_rows(rows, about, first=0.0, second=0.0):
    for r in rows:
        off = r - about
        first = first + off
        second = second + off * off
    return first, second


def group_mean(r):
    return over_group(jnp.sum(r, axis=0, keepdims=True)) * (1.0 / (PER_GROUP * r.shape[0]))


def pack(mean, dev):
    place = iota((1, CH), 1) & (PER_GROUP - 1)
    return jnp.where(place == 0, mean, jnp.where(place == 1, dev, 0.0))


def group_stats(about, first, second):
    cells = ROWS_DEV * COLS_DEV * PER_GROUP
    first = over_group(jnp.sum(first, axis=0, keepdims=True))
    second = over_group(jnp.sum(second, axis=0, keepdims=True))
    mean_off = first * (1.0 / cells)
    return pack(about + mean_off, second - first * mean_off)


def merge(packed, others, cells):
    count = others.shape[0] + 1
    off = others - packed
    first = jnp.sum(off, axis=0)
    apart = cells * (jnp.sum(off * off, axis=0) - first * first * (1.0 / count))
    return pack(packed + first * (1.0 / count), packed * count + first + pltpu.roll(apart, 1, 1))


def unpack(packed, cells):
    place = iota((1, CH), 1) & (PER_GROUP - 1)
    mean = over_group(jnp.where(place == 0, packed, 0.0))
    dev = over_group(jnp.where(place == 1, packed, 0.0))
    return mean, lax.rsqrt(dev * (1.0 / cells) + eps)


LEFT, MAIN, RIGHT, WIDE = 8, 16, 144, 160


def prepare_b(cb_v, wba, wbb):
    for dy in range(3):
        for dx in range(2):
            span = slice(dx * CH, (dx + 1) * CH)
            high, low = split(cb_v[dy, dx])
            wba[dy * 256 : dy * 256 + 128, span] = high
            wba[dy * 256 + 128 : dy * 256 + 256, span] = high
            wba[768 + dy * 128 : 896 + dy * 128, span] = low
        high, low = split(cb_v[dy, 2])
        for part, value in enumerate((high, high, low)):
            if dy < 2:
                wbb[part * 256 + dy * 128 : part * 256 + dy * 128 + 128, 0:CH] = value
            else:
                wbb[part * 256 : part * 256 + 128, CH : 2 * CH] = jnp.zeros((CH, CH), BF16)
                wbb[part * 256 + 128 : part * 256 + 256, CH : 2 * CH] = value


def activate(value, mean, scale, shift):
    half = ((value - mean) * scale + shift) * 0.5
    return half + half * jnp.tanh(half)


def second_conv(ha, hl, act, gs, hb, wba, wbb, mean, scale, shift, not_first, not_last):
    for i in range(10):
        value = activate(ha[i, MAIN:RIGHT, :], mean, scale, shift)
        if i == 0:
            value = value * not_first
        if i == 9:
            value = value * not_last
        act[i, :, 0:128], act[i, :, 128:256] = split(value)
    known = iota((16, 1), 0)
    known = jnp.where(known == 0, not_first, jnp.where(known == 9, not_last, 1.0))
    for i in range(2):
        hl[i, 0:16, :] = activate(hl[i, 0:16, :], mean, scale, shift) * known

    def side(i, dy):
        return split(hl[i, dy : dy + 16, :])

    def rows(first, size, part):
        return act[first : first + size, :, part * 128 : part * 128 + 128].reshape(size * 128, 128)

    pieces = [act[dy : dy + 8].reshape(1024, 256) for dy in range(3)] + [rows(dy, 8, 0) for dy in range(3)]
    at_side = [side(0, dy) for dy in range(3)]
    at_side = [part for pair in at_side for part in pair] + [pair[0] for pair in at_side]
    field = jnp.concatenate([jnp.concatenate(pieces, axis=1), jnp.concatenate(at_side, axis=1)], axis=0)
    early = dot(field, wba[...])

    pieces = [rows(0, 9, 0), rows(1, 9, 0), rows(0, 9, 1), rows(1, 9, 1), rows(0, 9, 0), rows(1, 9, 0)]
    (high0, low0), (high1, low1) = side(1, 0), side(1, 1)
    at_side = [high0, high1, low0, low1, high0, high1]
    field = jnp.concatenate([jnp.concatenate(pieces, axis=1), jnp.concatenate(at_side, axis=1)], axis=0)
    late = dot(field, wbb[...])

    for i in range(8):
        gs[0, i, MAIN:RIGHT, :] = early[i * 128 : (i + 1) * 128, 0:128]
        gs[0, i, MAIN - 1 : MAIN, :] = early[1024 + i : 1025 + i, 0:128]
        gs[2, i, MAIN:RIGHT, :] = late[i * 128 : (i + 1) * 128, 0:128] + late[(i + 1) * 128 : (i + 2) * 128, 128:256]
        gs[2, i, RIGHT : RIGHT + 1, :] = late[1152 + i : 1153 + i, 0:128] + late[1153 + i : 1154 + i, 128:256]
        hb[i] = gs[0, i, MAIN - 1 : RIGHT - 1, :] + early[i * 128 : (i + 1) * 128, 128:256] + gs[2, i, MAIN + 1 : RIGHT + 1, :]


def kernel(
    src_hbm, cnt_ref, coarse_ref, remap_ref, ca_ref, cb_ref, gain_a_ref, shift_a_ref, gain_b_ref, shift_b_ref,
    hb_ref, fin_ref,
    src_ref, coarse_v, remap_v, ca_v, cb_v, vec_v,
    tt, row_out, col_out, corner_out, mate_out, next_out, choice_out,
    row_in, col_in, corner_in, mate_in, next_in, choice_in,
    copies, choices, side, wa32, wa, wba, wbb,
    xs, gs, ha, hl, act, hb,
    stat, buf_x, buf_z,
    in_sem, out_sem, send_sem, recv_sem,
):
    place = coords()
    row, lon = place[0], place[1]
    z_mates = along_z(place)
    xy_mates = across(place)
    lon_mates = coarse_mates(place)
    lon_left, lon_right = lax.rem(lon + 31, 32), lax.rem(lon + 1, 32)
    odd = lax.rem(row, 2)
    is_odd = odd == 1
    has_far = jnp.where(is_odd, row < 15, row > 0)
    near_row = row + 1 - 2 * odd
    far_row = lax.rem(row + 2 * odd + 15, 16)
    halo = [
        (far_row, lon), (far_row, lon_right), (far_row, lon_left), (near_row, lon),
        (near_row, lon_right), (near_row, lon_left), (row, lon_right), (row, lon_left),
    ]
    barrier = pltpu.get_barrier_semaphore()
    partners = halo[3:] + lon_mates + z_mates + xy_mates

    @pl.when(has_far)
    def _():
        for mate in halo[:3]:
            pl.semaphore_signal(barrier, inc=1, device_id=mate, device_id_type=MESH)

    for mate in partners:
        pl.semaphore_signal(barrier, inc=1, device_id=mate, device_id_type=MESH)

    loads = [
        pltpu.make_async_copy(coarse_ref, coarse_v, in_sem.at[0]),
        pltpu.make_async_copy(remap_ref, remap_v, in_sem.at[1]),
        pltpu.make_async_copy(ca_ref, ca_v, in_sem.at[2]),
        pltpu.make_async_copy(cb_ref, cb_v, in_sem.at[3]),
    ]
    for i, ref in enumerate((gain_a_ref, shift_a_ref, gain_b_ref, shift_b_ref)):
        loads.append(pltpu.make_async_copy(ref, vec_v.at[i], in_sem.at[4 + i]))
    sources = pltpu.make_async_copy(src_hbm, src_ref, in_sem.at[8])
    for load in [sources] + loads:
        load.start()

    sources.wait()
    lane = iota((1, 128), 1)
    own_choice = jnp.zeros((1, 128), F32)
    for k in range(SLOTS):
        local = lax.rem(src_ref[0, k] - (lon - 1) * BLK_DEV + 2 * NBLK, NBLK)
        local = jnp.where(k < cnt_ref[0], local, -64)
        own_choice = jnp.where((lane >> 5) == k, local.astype(F32), own_choice)
    choice_tile = jnp.broadcast_to(own_choice, (16, 128)).astype(BF16)

    for q in range(BLK_DEV):
        want = q * BCELLS + (lane & (BCELLS - 1))
        copies[:, q * 128 : (q + 1) * 128] = jnp.where(iota((128, 128), 0) == want, 1.0, 0.0).astype(BF16)

    loads[0].wait()
    held = coarse_v[...].astype(F32)
    tile = jnp.zeros((VARS, 128), F32)
    for b in range(BLK_DEV):
        put = jnp.where(iota((BCELLS, 128), 0) + b * BCELLS == iota((BCELLS, 128), 1), 1.0, 0.0)
        tile = tile + dot(held[:, b, :].astype(BF16), put.astype(BF16))
    pad = jnp.concatenate([tile, jnp.zeros((16 - VARS, 128), F32)], axis=0)
    tt[2] = pad.astype(BF16)

    loads[1].wait()
    at = iota((224, 1), 0)
    inner = at & 15
    cell = at + odd * (7 * COLS_DEV)
    column = (inner & 7) * COLS_DEV + (inner >> 3)
    cell = jnp.where((at >= 128) & (at < 144), column + 126, cell)
    cell = jnp.where((at >= 144) & (at < 160), column, cell)
    for i, (row0, col0) in enumerate(((6 * odd, 126), (6 * odd, 0), (6 - 6 * odd, 126), (6 - 6 * odd, 0))):
        here = jnp.where(inner < 4, (row0 + (inner >> 1)) * COLS_DEV + col0 + (inner & 1), -1)
        cell = jnp.where((at >= 160 + 16 * i) & (at < 176 + 16 * i), here, cell)
    pick = jnp.where(iota((224, 1024), 1) == cell, 1.0, 0.0).astype(BF16)
    weights = dot(pick, remap_v[...], ((1,), (1,))).astype(BF16)
    row_out[...] = weights[0:128]
    choice_out[...] = own_choice
    for i in range(2):
        col_out[i, 0:16, :] = weights[128 + 16 * i : 144 + 16 * i]
        col_out[i, 16:32, :] = choice_tile
    for i in range(4):
        cells = weights[160 + 16 * i : 176 + 16 * i].astype(F32)
        corner_out[i] = jnp.where(iota((8, 128), 0) < 4, cells[0:8], own_choice)
    side[...] = jnp.zeros_like(side)
    hl[...] = jnp.zeros_like(hl)
    xs[...] = jnp.zeros_like(xs)

    loads[2].wait()
    wa32[...] = jnp.zeros_like(wa32)
    for dy in range(3):
        for part in range(3):
            first = (dy * 3 + part) * VARS
            for dx in range(3):
                wa32[first : first + VARS, dx * CH : (dx + 1) * CH] = ca_v[dy, dx]
    line = iota((128, 3 * CH), 0)
    twelfth = (line * 43) >> 9
    part_of = twelfth - 3 * ((twelfth * 11) >> 5)
    whole = wa32[...]
    high, low = split(whole)
    wa[...] = jnp.where(part_of == 2, low.astype(F32), high.astype(F32)).astype(BF16)

    twelfth_l = (lane * 43) >> 9
    var_l = jnp.where(lane < 9 * VARS, lane - 12 * twelfth_l, 4096)
    part_l = twelfth_l - 3 * ((twelfth_l * 11) >> 5)
    want = jnp.where(part_l == 1, var_l + 16, var_l)
    spread_msg = jnp.where(iota((32, 128), 0) == want, 1.0, 0.0).astype(BF16)
    spread_var = jnp.where(iota((16, 128), 0) == var_l, 1.0, 0.0).astype(BF16)
    not_first = jnp.where(row > 0, 1.0, 0.0).astype(F32)
    not_last = jnp.where(row < 15, 1.0, 0.0).astype(F32)

    @pl.when(jnp.logical_not(has_far))
    def _():
        row_in[...] = jnp.zeros_like(row_in)
        choice_in[...] = jnp.zeros_like(choice_in)
        next_in[...] = jnp.zeros_like(next_in)
        corner_in[0:2] = jnp.zeros((2, 8, 128), F32)

    pl.semaphore_wait(barrier, len(partners) + 3 * jnp.where(has_far, 1, 0))

    def send(src, dst, mate, out, into):
        copy = pltpu.make_async_remote_copy(
            src_ref=src, dst_ref=dst, send_sem=send_sem.at[out], recv_sem=recv_sem.at[into],
            device_id=mate, device_id_type=MESH,
        )
        copy.start()

    for i in range(2):
        send(col_out.at[i], col_in.at[i], halo[6 + i], 8, 2)
    for i in (2, 3):
        send(corner_out.at[i, pl.ds(0, 5)], corner_in.at[i, pl.ds(0, 5)], halo[2 + i], 9, 12)

    @pl.when(has_far)
    def _():
        for i in (0, 1):
            send(corner_out.at[i, pl.ds(0, 5)], corner_in.at[i, pl.ds(0, 5)], halo[1 + i], 1, 1)
        send(row_out, row_in, halo[0], 0, 0)
        send(choice_out, choice_in, halo[0], 11, 14)

    along_lon = [
        pltpu.make_async_remote_copy(
            src_ref=tt.at[2], dst_ref=tt.at[slot], send_sem=send_sem.at[7], recv_sem=recv_sem.at[8 + i],
            device_id=mate, device_id_type=MESH,
        )
        for i, (slot, mate) in enumerate(zip((0, 1, 3, 4), lon_mates))
    ]
    for copy in along_lon:
        copy.start()

    for copy in along_lon:
        copy.wait_recv()
    choices[...] = dot(tt[...].reshape(80, 128), copies[...])

    def chosen(choice, first_tile):
        total = jnp.zeros((16, 128), F32)
        for j in range(3 * BLK_DEV):
            t, q = first_tile + j // BLK_DEV, j % BLK_DEV
            total = jnp.where(choice == j, choices[t * 16 : t * 16 + 16, q * 128 : (q + 1) * 128], total)
        return total

    blocks = chosen(own_choice, 1).astype(BF16)

    four = jnp.concatenate([remap_v[:, 0:256], remap_v[:, 768:1024]], axis=1)
    four = dot(blocks, four)
    mate_out[0] = jnp.where(is_odd, four[:, 0:128], four[:, 384:512])
    mate_out[1] = jnp.where(is_odd, four[:, 128:256], four[:, 256:384])
    next_out[...] = jnp.where(is_odd, four[:, 256:384], four[:, 128:256])
    send(mate_out, mate_in, halo[3], 2, 3)

    @pl.when(has_far)
    def _():
        send(next_out, next_in, halo[0], 10, 13)


    spread_blocks = dot(blocks, spread_var, ((0,), (0,))).astype(BF16)
    fine = dot(remap_v[...], spread_blocks, ((0,), (0,)))
    high, low = split(fine)
    packed = jnp.where(part_l == 1, low.astype(F32), high.astype(F32)).astype(BF16)
    xs[2:10] = packed.reshape(ROWS_DEV, COLS_DEV, 128)

    third = jnp.broadcast_to(lane, (128, 128))

    def patches(before, here, after, lanes):
        before = jnp.where(lanes < 3 * VARS, before.astype(F32), 0.0)
        here = jnp.where((lanes >= 3 * VARS) & (lanes < 6 * VARS), here.astype(F32), 0.0)
        after = jnp.where(lanes >= 6 * VARS, after.astype(F32), 0.0)
        return (before + here + after).astype(BF16)

    def taps(out_rows):
        field = [patches(xs[i], xs[i + 1], xs[i + 2], third) for i in out_rows]
        result = dot(jnp.concatenate(field, axis=0), wa[...])
        for n, i in enumerate(out_rows):
            for dx in range(3):
                gs[dx, i, MAIN:RIGHT, :] = result[n * 128 : (n + 1) * 128, dx * CH : (dx + 1) * CH]

    def joined(i, first, size):
        return gs[0, i, first - 1 : first - 1 + size, :] + gs[1, i, first : first + size, :] + gs[2, i, first + 1 : first + 1 + size, :]

    taps(list(range(2, 8)))

    def placed(fine):
        high, low = split(fine)
        return dot(jnp.concatenate([high, low], axis=0), spread_msg, ((0,), (0,))).astype(BF16)

    pltpu.make_async_copy(mate_in, mate_in, recv_sem.at[3]).wait()
    xs[10 - 9 * odd] = placed(mate_in[0])
    xs[11 - 11 * odd] = placed(mate_in[1])

    far_known = jnp.where(is_odd, not_last, not_first)

    def fine_of(cells, choice, first_tile, known):
        held = chosen(choice.astype(F32), first_tile) * known
        return dot(cells.astype(BF16), held.astype(BF16), ((1,), (1,)))

    def spread_cells(parts):
        high, low = split(jnp.concatenate(parts, axis=0))
        return dot(jnp.concatenate([high, low], axis=1), spread_msg)

    def put_corner(cells, first_row, place):
        for n in range(4):
            side[first_row + (n >> 1), place + (n & 1) : place + (n & 1) + 1, :] = cells[n : n + 1]

    def corners(first):
        some = corner_in.at[pl.ds(first, 2), pl.ds(0, 5)]
        return pltpu.make_async_copy(some, some, recv_sem.at[1 if first == 0 else 12])

    pltpu.make_async_copy(col_in, col_in, recv_sem.at[2]).wait()
    corners(2).wait()
    cells = spread_cells([
        fine_of(col_in[0, 0:16, :], col_in[0, 16:17, :], 0, 1.0),
        fine_of(col_in[1, 0:16, :], col_in[1, 16:17, :], 2, 1.0),
        fine_of(corner_in[2], corner_in[2, 4:5, :], 0, 1.0),
        fine_of(corner_in[3], corner_in[3, 4:5, :], 2, 1.0),
    ])
    for i, place_at in enumerate((6, 0)):
        for n in range(16):
            at_col = place_at + (n >> 3)
            side[(n & 7) + 2, at_col : at_col + 1, :] = cells[16 * i + n : 16 * i + n + 1]
    put_corner(cells[32:40], 10 - 10 * odd, 6)
    put_corner(cells[40:48], 10 - 10 * odd, 0)
    near_border, far_border, near_beyond, far_beyond = 8 - 7 * odd, 1 + 7 * odd, 9 - 9 * odd, 9 * odd
    taps([near_border])

    def side_taps():
        side_lane = jnp.broadcast_to(lane.reshape(1, 1, 128), (10, 8, 128))
        side_patches = patches(side[0:10], side[1:11], side[2:12], side_lane).reshape(80, 128)
        result = dot(side_patches, wa[...]).reshape(10, 8, 3 * CH)
        for dx in range(3):
            piece = result[:, :, dx * CH : (dx + 1) * CH]
            gs[dx, :, LEFT:MAIN, :] = piece
            gs[dx, :, RIGHT : RIGHT + 8, :] = piece

    side_taps()
    inner_rows = [2, 3, 4, 5, 6, 7, near_border]
    for i in inner_rows:
        ha[i, MAIN:RIGHT, :] = joined(i, MAIN, 128)
    about = group_mean(ha[2, MAIN:RIGHT, :])
    first, second = add_rows([ha[i, MAIN:RIGHT, :] for i in inner_rows], about)

    @pl.when(has_far)
    def _():
        corners(0).wait()
        pltpu.make_async_copy(choice_in, choice_in, recv_sem.at[14]).wait()
        pltpu.make_async_copy(row_in, row_in, recv_sem.at[0]).wait()

    cells = spread_cells([
        fine_of(row_in[...], choice_in[...], 1, far_known),
        fine_of(corner_in[0], corner_in[0, 4:5, :], 0, far_known),
        fine_of(corner_in[1], corner_in[1, 4:5, :], 2, far_known),
    ])
    xs[1 + 9 * odd] = cells[0:128].astype(BF16)
    put_corner(cells[128:136], 10 * odd, 6)
    put_corner(cells[136:144], 10 * odd, 0)
    side_taps()
    taps([far_border])
    border = joined(far_border, MAIN, 128)
    ha[far_border, MAIN:RIGHT, :] = border
    sums = group_stats(about, *add_rows([border], about, first, second))

    def all_reduce(turn, packed, beside):
        cells = ROWS_DEV * COLS_DEV * PER_GROUP
        for stage, (mates, buf) in enumerate(((z_mates, buf_z), (xy_mates, buf_x))):
            sem = 4 + turn * 2 + stage
            stat[turn, stage] = packed
            for j, mate in enumerate(mates):
                pltpu.make_async_remote_copy(
                    src_ref=stat.at[turn, stage], dst_ref=buf.at[turn, j], send_sem=send_sem.at[sem - 1], recv_sem=recv_sem.at[sem],
                    device_id=mate, device_id_type=MESH,
                ).start()
            beside(stage)
            pltpu.make_async_copy(buf.at[turn], buf.at[turn], recv_sem.at[sem]).wait()
            packed = merge(packed, buf[turn], cells)
            cells = cells * (len(mates) + 1)
        return unpack(packed, cells)

    def around_a(stage):
        if stage == 0:

            for load in loads[3:]:
                load.wait()
            prepare_b(cb_v, wba, wbb)
            new_rows, all_rows = [near_beyond], list(range(1, 9)) + [near_beyond]
        else:

            @pl.when(has_far)
            def _():
                pltpu.make_async_copy(next_in, next_in, recv_sem.at[13]).wait()

            xs[11 * odd] = placed(next_in[...] * far_known)
            new_rows, all_rows = [far_beyond], [far_beyond]
        taps(new_rows)
        for i in new_rows:
            ha[i, MAIN:RIGHT, :] = joined(i, MAIN, 128)
        for i in all_rows:
            hl[0, pl.ds(i, 1), :] = joined(i, MAIN - 1, 1)
            hl[1, pl.ds(i, 1), :] = joined(i, RIGHT, 1)

    mean, inverse = all_reduce(0, sums, around_a)

    second_conv(ha, hl, act, gs, hb, wba, wbb, mean, inverse * vec_v[0], vec_v[1], not_first, not_last)
    store = pltpu.make_async_copy(hb, hb_ref, out_sem)
    store.start()
    about = group_mean(hb[0])
    sums = group_stats(about, *add_rows([hb[i] for i in range(8)], about))
    mean, inverse = all_reduce(1, sums, lambda stage: None)
    fin_ref[0:1, :] = mean
    fin_ref[1:2, :] = inverse * vec_v[2]
    fin_ref[2:3, :] = vec_v[3]
    store.wait()

    @pl.when(has_far)
    def _():
        pltpu.make_async_copy(row_in, row_in, send_sem.at[0]).wait()
        pltpu.make_async_copy(choice_in, choice_in, send_sem.at[11]).wait()
        pltpu.make_async_copy(next_in, next_in, send_sem.at[10]).wait()
        some = corner_in.at[pl.ds(0, 2), pl.ds(0, 5)]
        pltpu.make_async_copy(some, some, send_sem.at[1]).wait()

    some = corner_in.at[pl.ds(2, 2), pl.ds(0, 5)]
    pltpu.make_async_copy(some, some, send_sem.at[9]).wait()
    pltpu.make_async_copy(col_in, col_in, send_sem.at[8]).wait()
    pltpu.make_async_copy(mate_in, mate_in, send_sem.at[2]).wait()
    pltpu.make_async_copy(tt.at[pl.ds(0, 4)], tt.at[pl.ds(0, 4)], send_sem.at[7]).wait()
    for turn in range(2):
        pltpu.make_async_copy(buf_z.at[turn], buf_z.at[turn], send_sem.at[3 + 2 * turn]).wait()
        pltpu.make_async_copy(buf_x.at[turn], buf_x.at[turn], send_sem.at[4 + 2 * turn]).wait()


def per_device(
    coarse, src_blocks, slot_counts, remap_tiles, conv_a, conv_b, gain_a, shift_a, gain_b, shift_b
):
    anywhere = pl.BlockSpec(memory_space=pl.ANY)
    vectors = [v.reshape(1, CH) for v in (gain_a, shift_a, gain_b, shift_b)]
    hidden, final = pl.pallas_call(
        kernel,
        name="stem",
        out_shape=(
            pltpu.VMEM((ROWS_DEV, COLS_DEV, CH), F32),
            pltpu.VMEM((3, CH), F32),
        ),
        in_specs=[anywhere, pl.BlockSpec(memory_space=pltpu.SMEM)] + [anywhere] * 8,
        out_specs=(anywhere, pl.BlockSpec(memory_space=pltpu.VMEM)),
        scratch_shapes=[
            pltpu.SMEM((1, SLOTS), jnp.int32),
            pltpu.VMEM((VARS, BLK_DEV, BCELLS), BF16),
            pltpu.VMEM((128, 1024), BF16),
            pltpu.VMEM((3, 3, VARS, CH), F32),
            pltpu.VMEM((3, 3, CH, CH), F32),
            pltpu.VMEM((4, 1, CH), F32),
            pltpu.VMEM((5, 16, 128), BF16),
            pltpu.VMEM((128, 128), BF16),
            pltpu.VMEM((2, 32, 128), BF16),
            pltpu.VMEM((4, 8, 128), F32),
            pltpu.VMEM((2, 16, 128), F32),
            pltpu.VMEM((16, 128), F32),
            pltpu.VMEM((1, 128), F32),
            pltpu.VMEM((128, 128), BF16),
            pltpu.VMEM((2, 32, 128), BF16),
            pltpu.VMEM((4, 8, 128), F32),
            pltpu.VMEM((2, 16, 128), F32),
            pltpu.VMEM((16, 128), F32),
            pltpu.VMEM((1, 128), F32),
            pltpu.VMEM((128, BLK_DEV * 128), BF16),
            pltpu.VMEM((80, BLK_DEV * 128), F32),
            pltpu.VMEM((12, 8, 128), F32),
            pltpu.VMEM((128, 3 * CH), F32),
            pltpu.VMEM((128, 3 * CH), BF16),
            pltpu.VMEM((9 * CH, 2 * CH), BF16),
            pltpu.VMEM((6 * CH, 2 * CH), BF16),
            pltpu.VMEM((12, COLS_DEV, 128), BF16),
            pltpu.VMEM((3, 10, WIDE, CH), F32),
            pltpu.VMEM((10, WIDE, CH), F32),
            pltpu.VMEM((2, 24, CH), F32),
            pltpu.VMEM((10, COLS_DEV, 2 * CH), BF16),
            pltpu.VMEM((ROWS_DEV, COLS_DEV, CH), F32),
            pltpu.VMEM((2, 2, 1, CH), F32),
            pltpu.VMEM((2, 15, 1, CH), F32),
            pltpu.VMEM((2, 31, 1, CH), F32),
            pltpu.SemaphoreType.DMA((9,)),
            pltpu.SemaphoreType.DMA,
            pltpu.SemaphoreType.DMA((12,)),
            pltpu.SemaphoreType.DMA((15,)),
        ],
        compiler_params=pltpu.CompilerParams(
            collective_id=0, has_side_effects=True, vmem_limit_bytes=60 * 1024 * 1024
        ),
    )(
        src_blocks, slot_counts, jnp.transpose(coarse, (1, 0, 2)), remap_tiles.reshape(SLOTS * BCELLS, 1024),
        conv_a, conv_b, *vectors,
    )
    normed = (hidden - final[0]) * final[1] + final[2]
    return jax.nn.silu(normed).astype(BF16)


def solution(mesh):
    return jax.shard_map(
        per_device,
        mesh=mesh,
        in_specs=(
            P("lon", None, None),
            P(("row", "lon"), None),
            P(("row", "lon")),
            P(("row", "lon"), None, None, None),
            P(),
            P(),
            P(),
            P(),
            P(),
            P(),
        ),
        out_specs=P("row", "lon", None),
        check_vma=False,
    )
```

```python
import jax
import jax.numpy as jnp
from jax import lax
from jax.experimental import pallas as pl
from jax.experimental.pallas import tpu as pltpu
from jax.sharding import PartitionSpec as P

ROWS_DEV = 8
COLS_DEV = 128
VARS = 12
CH = 128
GROUPS = 32
SLOTS = 4
BCELLS = 32
BLK_DEV = 4
NBLK = 128
PER_GROUP = CH // GROUPS
MESH = pl.DeviceIdType.MESH
F32 = jnp.float32
BF16 = jnp.bfloat16

eps = 1e-05


def coords():
    row = lax.axis_index("row")
    lon = lax.axis_index("lon")
    core = lax.rem(row, 2)
    z_hi = lax.rem(lax.div(row, 2), 2)
    x = lax.div(row, 4)
    y = lax.div(lon, 8)
    z = z_hi * 8 + lax.rem(lon, 8)
    return row, lon, x, y, z, core


def device_at(x, y, z, core):
    return (x * 4 + lax.div(z, 8) * 2 + core, y * 8 + lax.rem(z, 8))


def moved(value, step, count):
    return lax.rem(value + step, count) if step else value


def along_z(place):
    _, _, x, y, z, core = place
    steps = [(d, c) for d in range(16) for c in range(2) if d or c]
    steps.sort(key=lambda s: -min(s[0], 16 - s[0]))
    return [device_at(x, y, moved(z, d, 16), moved(core, c, 2)) for d, c in steps]


def across(place):
    _, _, x, y, z, core = place
    steps = [(a, b) for a in range(4) for b in range(4) if a or b]
    steps.sort(key=lambda s: -(min(s[0], 4 - s[0]) + min(s[1], 4 - s[1])))
    return [device_at(moved(x, a, 4), moved(y, b, 4), z, core) for a, b in steps]


def coarse_mates(place):
    _, _, x, y, z, core = place
    z_lo = lax.rem(z, 8)
    mates = []
    for step in (2, 1, -1, -2):
        turn = lax.rem(y + 3 + lax.div(z_lo + 8 + step, 8), 4)
        mates.append(device_at(x, turn, lax.rem(z + 16 + step, 16), core))
    return mates


def iota(shape, dim):
    return lax.broadcasted_iota(jnp.int32, shape, dim)


def split(value):
    high = value.astype(BF16)
    low = (value - high.astype(F32)).astype(BF16)
    return high, low


def dot(a, b, dims=((1,), (0,))):
    return lax.dot_general(a, b, (dims, ((), ())), preferred_element_type=F32)


def over_group(row):
    place = iota(row.shape, 1) & (PER_GROUP - 1)
    total = row
    for step in range(1, PER_GROUP):
        after = pltpu.roll(row, CH - step, 1)
        before = pltpu.roll(row, step, 1)
        total = total + jnp.where(place < PER_GROUP - step, after, 0.0) + jnp.where(place >= step, before, 0.0)
    return total


def add_rows(rows, about, first=0.0, second=0.0):
    for r in rows:
        off = r - about
        first = first + off
        second = second + off * off
    return first, second


def group_mean(r):
    return over_group(jnp.sum(r, axis=0, keepdims=True)) * (1.0 / (PER_GROUP * r.shape[0]))


def pack(mean, dev):
    place = iota((1, CH), 1) & (PER_GROUP - 1)
    return jnp.where(place == 0, mean, jnp.where(place == 1, dev, 0.0))


def group_stats(about, first, second):
    cells = ROWS_DEV * COLS_DEV * PER_GROUP
    first = over_group(jnp.sum(first, axis=0, keepdims=True))
    second = over_group(jnp.sum(second, axis=0, keepdims=True))
    mean_off = first * (1.0 / cells)
    return pack(about + mean_off, second - first * mean_off)


def merge(packed, others, cells):
    count = others.shape[0] + 1
    off = others - packed
    first = jnp.sum(off, axis=0)
    apart = cells * (jnp.sum(off * off, axis=0) - first * first * (1.0 / count))
    return pack(packed + first * (1.0 / count), packed * count + first + pltpu.roll(apart, 1, 1))


def unpack(packed, cells):
    place = iota((1, CH), 1) & (PER_GROUP - 1)
    mean = over_group(jnp.where(place == 0, packed, 0.0))
    dev = over_group(jnp.where(place == 1, packed, 0.0))
    return mean, lax.rsqrt(dev * (1.0 / cells) + eps)


LEFT, MAIN, RIGHT, WIDE = 8, 16, 144, 160


def prepare_b(cb_v, wba, wbb):
    for dy in range(3):
        for dx in range(2):
            span = slice(dx * CH, (dx + 1) * CH)
            high, low = split(cb_v[dy, dx])
            wba[dy * 256 : dy * 256 + 128, span] = high
            wba[dy * 256 + 128 : dy * 256 + 256, span] = high
            wba[768 + dy * 128 : 896 + dy * 128, span] = low
        high, low = split(cb_v[dy, 2])
        for part, value in enumerate((high, high, low)):
            if dy < 2:
                wbb[part * 256 + dy * 128 : part * 256 + dy * 128 + 128, 0:CH] = value
            else:
                wbb[part * 256 : part * 256 + 128, CH : 2 * CH] = jnp.zeros((CH, CH), BF16)
                wbb[part * 256 + 128 : part * 256 + 256, CH : 2 * CH] = value


def activate(value, mean, scale, shift):
    half = ((value - mean) * scale + shift) * 0.5
    return half + half * jnp.tanh(half)


def second_conv(ha, hl, act, gs, hb, wba, wbb, mean, scale, shift, not_first, not_last):
    for i in range(10):
        value = activate(ha[i, MAIN:RIGHT, :], mean, scale, shift)
        if i == 0:
            value = value * not_first
        if i == 9:
            value = value * not_last
        act[i, :, 0:128], act[i, :, 128:256] = split(value)
    known = iota((16, 1), 0)
    known = jnp.where(known == 0, not_first, jnp.where(known == 9, not_last, 1.0))
    for i in range(2):
        hl[i, 0:16, :] = activate(hl[i, 0:16, :], mean, scale, shift) * known

    def side(i, dy):
        return split(hl[i, dy : dy + 16, :])

    def rows(first, size, part):
        return act[first : first + size, :, part * 128 : part * 128 + 128].reshape(size * 128, 128)

    pieces = [act[dy : dy + 8].reshape(1024, 256) for dy in range(3)] + [rows(dy, 8, 0) for dy in range(3)]
    at_side = [side(0, dy) for dy in range(3)]
    at_side = [part for pair in at_side for part in pair] + [pair[0] for pair in at_side]
    field = jnp.concatenate([jnp.concatenate(pieces, axis=1), jnp.concatenate(at_side, axis=1)], axis=0)
    early = dot(field, wba[...])

    pieces = [rows(0, 9, 0), rows(1, 9, 0), rows(0, 9, 1), rows(1, 9, 1), rows(0, 9, 0), rows(1, 9, 0)]
    (high0, low0), (high1, low1) = side(1, 0), side(1, 1)
    at_side = [high0, high1, low0, low1, high0, high1]
    field = jnp.concatenate([jnp.concatenate(pieces, axis=1), jnp.concatenate(at_side, axis=1)], axis=0)
    late = dot(field, wbb[...])

    for i in range(8):
        gs[0, i, MAIN:RIGHT, :] = early[i * 128 : (i + 1) * 128, 0:128]
        gs[0, i, MAIN - 1 : MAIN, :] = early[1024 + i : 1025 + i, 0:128]
        gs[2, i, MAIN:RIGHT, :] = late[i * 128 : (i + 1) * 128, 0:128] + late[(i + 1) * 128 : (i + 2) * 128, 128:256]
        gs[2, i, RIGHT : RIGHT + 1, :] = late[1152 + i : 1153 + i, 0:128] + late[1153 + i : 1154 + i, 128:256]
        hb[i] = gs[0, i, MAIN - 1 : RIGHT - 1, :] + early[i * 128 : (i + 1) * 128, 128:256] + gs[2, i, MAIN + 1 : RIGHT + 1, :]


def kernel(
    src_hbm, cnt_ref, coarse_ref, remap_ref, ca_ref, cb_ref, gain_a_ref, shift_a_ref, gain_b_ref, shift_b_ref,
    out_ref,
    src_ref, coarse_v, remap_v, ca_v, cb_v, vec_v,
    tt, row_out, col_out, corner_out, mate_out, next_out, choice_out,
    row_in, col_in, corner_in, mate_in, next_in, choice_in, side_choice,
    copies, choices, side, wa32, wa, wba, wbb,
    xs, gs, ha, hl, act, hb,
    stat, buf_x, buf_z,
    in_sem, send_sem, recv_sem,
):
    place = coords()
    row, lon = place[0], place[1]
    z_mates = along_z(place)
    xy_mates = across(place)
    lon_mates = coarse_mates(place)
    lon_left, lon_right = lax.rem(lon + 31, 32), lax.rem(lon + 1, 32)
    odd = lax.rem(row, 2)
    is_odd = odd == 1
    has_far = jnp.where(is_odd, row < 15, row > 0)
    near_row = row + 1 - 2 * odd
    far_row = lax.rem(row + 2 * odd + 15, 16)
    halo = [
        (far_row, lon), (far_row, lon_right), (far_row, lon_left), (near_row, lon),
        (near_row, lon_right), (near_row, lon_left), (row, lon_right), (row, lon_left),
    ]
    barrier = pltpu.get_barrier_semaphore()
    partners = halo[3:] + lon_mates + z_mates + xy_mates

    @pl.when(has_far)
    def _():
        for mate in halo[:3]:
            pl.semaphore_signal(barrier, inc=1, device_id=mate, device_id_type=MESH)

    for mate in partners:
        pl.semaphore_signal(barrier, inc=1, device_id=mate, device_id_type=MESH)

    loads = [
        pltpu.make_async_copy(coarse_ref, coarse_v, in_sem.at[0]),
        pltpu.make_async_copy(remap_ref, remap_v, in_sem.at[1]),
        pltpu.make_async_copy(ca_ref, ca_v, in_sem.at[2]),
        pltpu.make_async_copy(cb_ref, cb_v, in_sem.at[3]),
    ]
    for i, ref in enumerate((gain_a_ref, shift_a_ref, gain_b_ref, shift_b_ref)):
        loads.append(pltpu.make_async_copy(ref, vec_v.at[i], in_sem.at[4 + i]))
    sources = pltpu.make_async_copy(src_hbm, src_ref, in_sem.at[8])
    for load in [sources] + loads:
        load.start()

    sources.wait()
    lane = iota((1, 128), 1)
    own_choice = jnp.zeros((1, 128), F32)
    for k in range(SLOTS):
        local = lax.rem(src_ref[0, k] - (lon - 1) * BLK_DEV + 2 * NBLK, NBLK)
        local = jnp.where(k < cnt_ref[0], local, -64)
        own_choice = jnp.where((lane >> 5) == k, local.astype(F32), own_choice)

    for q in range(BLK_DEV):
        want = q * BCELLS + (lane & (BCELLS - 1))
        copies[:, q * 128 : (q + 1) * 128] = jnp.where(iota((128, 128), 0) == want, 1.0, 0.0).astype(BF16)

    loads[0].wait()
    held = coarse_v[...].astype(F32)
    tile = jnp.zeros((VARS, 128), F32)
    for b in range(BLK_DEV):
        put = jnp.where(iota((BCELLS, 128), 0) + b * BCELLS == iota((BCELLS, 128), 1), 1.0, 0.0)
        tile = tile + dot(held[:, b, :].astype(BF16), put.astype(BF16))
    pad = jnp.concatenate([tile, jnp.zeros((16 - VARS, 128), F32)], axis=0)
    tt[2] = pad.astype(BF16)

    loads[1].wait()
    at = iota((224, 1), 0)
    inner = at & 15
    cell = at + odd * (7 * COLS_DEV)
    column = (inner & 7) * COLS_DEV + (inner >> 3)
    cell = jnp.where((at >= 128) & (at < 144), column + 126, cell)
    cell = jnp.where((at >= 144) & (at < 160), column, cell)
    for i, (row0, col0) in enumerate(((6 * odd, 126), (6 * odd, 0), (6 - 6 * odd, 126), (6 - 6 * odd, 0))):
        here = jnp.where(inner < 4, (row0 + (inner >> 1)) * COLS_DEV + col0 + (inner & 1), -1)
        cell = jnp.where((at >= 160 + 16 * i) & (at < 176 + 16 * i), here, cell)
    pick = jnp.where(iota((224, 1024), 1) == cell, 1.0, 0.0).astype(BF16)
    weights = dot(pick, remap_v[...], ((1,), (1,))).astype(BF16)
    row_out[...] = weights[0:128]
    choice_out[...] = own_choice
    for i in range(2):
        col_out[i] = weights[128 + 16 * i : 144 + 16 * i]
    for i in range(4):
        cells = weights[160 + 16 * i : 176 + 16 * i].astype(F32)
        corner_out[i] = jnp.where(iota((8, 128), 0) < 4, cells[0:8], own_choice)
    side[...] = jnp.zeros_like(side)
    hl[...] = jnp.zeros_like(hl)
    xs[...] = jnp.zeros_like(xs)

    loads[2].wait()
    wa32[...] = jnp.zeros_like(wa32)
    for dy in range(3):
        for part in range(3):
            first = (dy * 3 + part) * VARS
            for dx in range(3):
                wa32[first : first + VARS, dx * CH : (dx + 1) * CH] = ca_v[dy, dx]
    line = iota((128, 3 * CH), 0)
    twelfth = (line * 43) >> 9
    part_of = twelfth - 3 * ((twelfth * 11) >> 5)
    whole = wa32[...]
    high, low = split(whole)
    wa[...] = jnp.where(part_of == 2, low.astype(F32), high.astype(F32)).astype(BF16)

    twelfth_l = (lane * 43) >> 9
    var_l = jnp.where(lane < 9 * VARS, lane - 12 * twelfth_l, 4096)
    part_l = twelfth_l - 3 * ((twelfth_l * 11) >> 5)
    want = jnp.where(part_l == 1, var_l + 16, var_l)
    spread_msg = jnp.where(iota((32, 128), 0) == want, 1.0, 0.0).astype(BF16)
    spread_var = jnp.where(iota((16, 128), 0) == var_l, 1.0, 0.0).astype(BF16)
    not_first = jnp.where(row > 0, 1.0, 0.0).astype(F32)
    not_last = jnp.where(row < 15, 1.0, 0.0).astype(F32)

    @pl.when(jnp.logical_not(has_far))
    def _():
        row_in[...] = jnp.zeros_like(row_in)
        choice_in[...] = jnp.zeros_like(choice_in)
        next_in[...] = jnp.zeros_like(next_in)
        corner_in[0:2] = jnp.zeros((2, 8, 128), F32)

    pl.semaphore_wait(barrier, len(partners) + 3 * jnp.where(has_far, 1, 0))

    def send(src, dst, mate, out, into):
        copy = pltpu.make_async_remote_copy(
            src_ref=src, dst_ref=dst, send_sem=send_sem.at[out], recv_sem=recv_sem.at[into],
            device_id=mate, device_id_type=MESH,
        )
        copy.start()

    for i in range(2):
        send(col_out.at[i], col_in.at[i], halo[6 + i], 8, 2)
        send(choice_out, side_choice.at[i], halo[6 + i], 12, 15)
    for i in (2, 3):
        send(corner_out.at[i, pl.ds(0, 5)], corner_in.at[i, pl.ds(0, 5)], halo[2 + i], 9, 12)

    @pl.when(has_far)
    def _():
        for i in (0, 1):
            send(corner_out.at[i, pl.ds(0, 5)], corner_in.at[i, pl.ds(0, 5)], halo[1 + i], 1, 1)
        send(row_out, row_in, halo[0], 0, 0)
        send(choice_out, choice_in, halo[0], 11, 14)

    along_lon = [
        pltpu.make_async_remote_copy(
            src_ref=tt.at[2], dst_ref=tt.at[slot], send_sem=send_sem.at[7], recv_sem=recv_sem.at[8 + i],
            device_id=mate, device_id_type=MESH,
        )
        for i, (slot, mate) in enumerate(zip((0, 1, 3, 4), lon_mates))
    ]
    for copy in along_lon:
        copy.start()

    for copy in along_lon:
        copy.wait_recv()
    choices[...] = dot(tt[...].reshape(80, 128), copies[...])

    def chosen(choice, first_tile):
        total = jnp.zeros((16, 128), F32)
        for j in range(3 * BLK_DEV):
            t, q = first_tile + j // BLK_DEV, j % BLK_DEV
            total = jnp.where(choice == j, choices[t * 16 : t * 16 + 16, q * 128 : (q + 1) * 128], total)
        return total

    blocks = chosen(own_choice, 1).astype(BF16)

    four = jnp.concatenate([remap_v[:, 0:256], remap_v[:, 768:1024]], axis=1)
    four = dot(blocks, four)
    mate_out[0] = jnp.where(is_odd, four[:, 0:128], four[:, 384:512])
    mate_out[1] = jnp.where(is_odd, four[:, 128:256], four[:, 256:384])
    next_out[...] = jnp.where(is_odd, four[:, 256:384], four[:, 128:256])
    send(mate_out, mate_in, halo[3], 2, 3)

    @pl.when(has_far)
    def _():
        send(next_out, next_in, halo[0], 10, 13)


    spread_blocks = dot(blocks, spread_var, ((0,), (0,))).astype(BF16)
    fine = dot(remap_v[...], spread_blocks, ((0,), (0,)))
    high, low = split(fine)
    packed = jnp.where(part_l == 1, low.astype(F32), high.astype(F32)).astype(BF16)
    xs[2:10] = packed.reshape(ROWS_DEV, COLS_DEV, 128)

    third = jnp.broadcast_to(lane, (128, 128))

    def patches(before, here, after, lanes):
        before = jnp.where(lanes < 3 * VARS, before.astype(F32), 0.0)
        here = jnp.where((lanes >= 3 * VARS) & (lanes < 6 * VARS), here.astype(F32), 0.0)
        after = jnp.where(lanes >= 6 * VARS, after.astype(F32), 0.0)
        return (before + here + after).astype(BF16)

    def taps(out_rows):
        field = [patches(xs[i], xs[i + 1], xs[i + 2], third) for i in out_rows]
        result = dot(jnp.concatenate(field, axis=0), wa[...])
        for n, i in enumerate(out_rows):
            for dx in range(3):
                gs[dx, i, MAIN:RIGHT, :] = result[n * 128 : (n + 1) * 128, dx * CH : (dx + 1) * CH]

    def joined(i, first, size):
        return gs[0, i, first - 1 : first - 1 + size, :] + gs[1, i, first : first + size, :] + gs[2, i, first + 1 : first + 1 + size, :]

    taps(list(range(2, 8)))

    def placed(fine):
        high, low = split(fine)
        return dot(jnp.concatenate([high, low], axis=0), spread_msg, ((0,), (0,))).astype(BF16)

    pltpu.make_async_copy(mate_in, mate_in, recv_sem.at[3]).wait()
    xs[10 - 9 * odd] = placed(mate_in[0])
    xs[11 - 11 * odd] = placed(mate_in[1])

    far_known = jnp.where(is_odd, not_last, not_first)

    def fine_of(cells, choice, first_tile, known):
        held = chosen(choice.astype(F32), first_tile) * known
        return dot(cells.astype(BF16), held.astype(BF16), ((1,), (1,)))

    def spread_cells(parts):
        high, low = split(jnp.concatenate(parts, axis=0))
        return dot(jnp.concatenate([high, low], axis=1), spread_msg)

    def put_corner(cells, first_row, place):
        for n in range(4):
            side[first_row + (n >> 1), place + (n & 1) : place + (n & 1) + 1, :] = cells[n : n + 1]

    def corners(first):
        some = corner_in.at[pl.ds(first, 2), pl.ds(0, 5)]
        return pltpu.make_async_copy(some, some, recv_sem.at[1 if first == 0 else 12])

    pltpu.make_async_copy(col_in, col_in, recv_sem.at[2]).wait()
    pltpu.make_async_copy(side_choice, side_choice, recv_sem.at[15]).wait()
    corners(2).wait()
    cells = spread_cells([
        fine_of(col_in[0], side_choice[0], 0, 1.0),
        fine_of(col_in[1], side_choice[1], 2, 1.0),
        fine_of(corner_in[2], corner_in[2, 4:5, :], 0, 1.0),
        fine_of(corner_in[3], corner_in[3, 4:5, :], 2, 1.0),
    ])
    for i, place_at in enumerate((6, 0)):
        for n in range(16):
            at_col = place_at + (n >> 3)
            side[(n & 7) + 2, at_col : at_col + 1, :] = cells[16 * i + n : 16 * i + n + 1]
    put_corner(cells[32:40], 10 - 10 * odd, 6)
    put_corner(cells[40:48], 10 - 10 * odd, 0)
    near_border, far_border, near_beyond, far_beyond = 8 - 7 * odd, 1 + 7 * odd, 9 - 9 * odd, 9 * odd
    taps([near_border])

    def side_taps():
        side_lane = jnp.broadcast_to(lane.reshape(1, 1, 128), (10, 8, 128))
        side_patches = patches(side[0:10], side[1:11], side[2:12], side_lane).reshape(80, 128)
        result = dot(side_patches, wa[...]).reshape(10, 8, 3 * CH)
        for dx in range(3):
            piece = result[:, :, dx * CH : (dx + 1) * CH]
            gs[dx, :, LEFT:MAIN, :] = piece
            gs[dx, :, RIGHT : RIGHT + 8, :] = piece

    side_taps()
    inner_rows = [2, 3, 4, 5, 6, 7, near_border]
    for i in inner_rows:
        ha[i, MAIN:RIGHT, :] = joined(i, MAIN, 128)
    about = group_mean(ha[2, MAIN:RIGHT, :])
    first, second = add_rows([ha[i, MAIN:RIGHT, :] for i in inner_rows], about)

    @pl.when(has_far)
    def _():
        corners(0).wait()
        pltpu.make_async_copy(choice_in, choice_in, recv_sem.at[14]).wait()
        pltpu.make_async_copy(row_in, row_in, recv_sem.at[0]).wait()

    cells = spread_cells([
        fine_of(row_in[...], choice_in[...], 1, far_known),
        fine_of(corner_in[0], corner_in[0, 4:5, :], 0, far_known),
        fine_of(corner_in[1], corner_in[1, 4:5, :], 2, far_known),
    ])
    xs[1 + 9 * odd] = cells[0:128].astype(BF16)
    put_corner(cells[128:136], 10 * odd, 6)
    put_corner(cells[136:144], 10 * odd, 0)
    side_taps()
    taps([far_border])
    border = joined(far_border, MAIN, 128)
    ha[far_border, MAIN:RIGHT, :] = border
    sums = group_stats(about, *add_rows([border], about, first, second))

    def all_reduce(turn, packed, beside):
        cells = ROWS_DEV * COLS_DEV * PER_GROUP
        for stage, (mates, buf) in enumerate(((z_mates, buf_z), (xy_mates, buf_x))):
            sem = 4 + turn * 2 + stage
            stat[turn, stage] = packed
            for j, mate in enumerate(mates):
                pltpu.make_async_remote_copy(
                    src_ref=stat.at[turn, stage], dst_ref=buf.at[turn, j], send_sem=send_sem.at[sem - 1], recv_sem=recv_sem.at[sem],
                    device_id=mate, device_id_type=MESH,
                ).start()
            beside(stage)
            pltpu.make_async_copy(buf.at[turn], buf.at[turn], recv_sem.at[sem]).wait()
            packed = merge(packed, buf[turn], cells)
            cells = cells * (len(mates) + 1)
        return unpack(packed, cells)

    def around_a(stage):
        if stage == 0:

            for load in loads[3:]:
                load.wait()
            prepare_b(cb_v, wba, wbb)
            new_rows, all_rows = [near_beyond], list(range(1, 9)) + [near_beyond]
        else:

            @pl.when(has_far)
            def _():
                pltpu.make_async_copy(next_in, next_in, recv_sem.at[13]).wait()

            xs[11 * odd] = placed(next_in[...] * far_known)
            new_rows, all_rows = [far_beyond], [far_beyond]
        taps(new_rows)
        for i in new_rows:
            ha[i, MAIN:RIGHT, :] = joined(i, MAIN, 128)
        for i in all_rows:
            hl[0, pl.ds(i, 1), :] = joined(i, MAIN - 1, 1)
            hl[1, pl.ds(i, 1), :] = joined(i, RIGHT, 1)

    mean, inverse = all_reduce(0, sums, around_a)

    second_conv(ha, hl, act, gs, hb, wba, wbb, mean, inverse * vec_v[0], vec_v[1], not_first, not_last)
    about = group_mean(hb[0])
    sums = group_stats(about, *add_rows([hb[i] for i in range(8)], about))
    mean, inverse = all_reduce(1, sums, lambda stage: None)
    scale = inverse * vec_v[2]
    for i in range(8):
        out_ref[i] = activate(hb[i], mean, scale, vec_v[3]).astype(BF16)

    @pl.when(has_far)
    def _():
        pltpu.make_async_copy(row_in, row_in, send_sem.at[0]).wait()
        pltpu.make_async_copy(choice_in, choice_in, send_sem.at[11]).wait()
        pltpu.make_async_copy(next_in, next_in, send_sem.at[10]).wait()
        some = corner_in.at[pl.ds(0, 2), pl.ds(0, 5)]
        pltpu.make_async_copy(some, some, send_sem.at[1]).wait()

    some = corner_in.at[pl.ds(2, 2), pl.ds(0, 5)]
    pltpu.make_async_copy(some, some, send_sem.at[9]).wait()
    pltpu.make_async_copy(col_in, col_in, send_sem.at[8]).wait()
    pltpu.make_async_copy(side_choice, side_choice, send_sem.at[12]).wait()
    pltpu.make_async_copy(mate_in, mate_in, send_sem.at[2]).wait()
    pltpu.make_async_copy(tt.at[pl.ds(0, 4)], tt.at[pl.ds(0, 4)], send_sem.at[7]).wait()
    for turn in range(2):
        pltpu.make_async_copy(buf_z.at[turn], buf_z.at[turn], send_sem.at[3 + 2 * turn]).wait()
        pltpu.make_async_copy(buf_x.at[turn], buf_x.at[turn], send_sem.at[4 + 2 * turn]).wait()


def per_device(
    coarse, src_blocks, slot_counts, remap_tiles, conv_a, conv_b, gain_a, shift_a, gain_b, shift_b
):
    anywhere = pl.BlockSpec(memory_space=pl.ANY)
    vectors = [v.reshape(1, CH) for v in (gain_a, shift_a, gain_b, shift_b)]
    return pl.pallas_call(
        kernel,
        name="stem",
        out_shape=pltpu.VMEM((ROWS_DEV, COLS_DEV, CH), BF16),
        in_specs=[anywhere, pl.BlockSpec(memory_space=pltpu.SMEM)] + [anywhere] * 8,
        out_specs=pl.BlockSpec(memory_space=pltpu.VMEM),
        scratch_shapes=[
            pltpu.SMEM((1, SLOTS), jnp.int32),
            pltpu.VMEM((VARS, BLK_DEV, BCELLS), BF16),
            pltpu.VMEM((128, 1024), BF16),
            pltpu.VMEM((3, 3, VARS, CH), F32),
            pltpu.VMEM((3, 3, CH, CH), F32),
            pltpu.VMEM((4, 1, CH), F32),
            pltpu.VMEM((5, 16, 128), BF16),
            pltpu.VMEM((128, 128), BF16),
            pltpu.VMEM((2, 16, 128), BF16),
            pltpu.VMEM((4, 8, 128), F32),
            pltpu.VMEM((2, 16, 128), F32),
            pltpu.VMEM((16, 128), F32),
            pltpu.VMEM((1, 128), F32),
            pltpu.VMEM((128, 128), BF16),
            pltpu.VMEM((2, 16, 128), BF16),
            pltpu.VMEM((4, 8, 128), F32),
            pltpu.VMEM((2, 16, 128), F32),
            pltpu.VMEM((16, 128), F32),
            pltpu.VMEM((1, 128), F32),
            pltpu.VMEM((2, 1, 128), F32),
            pltpu.VMEM((128, BLK_DEV * 128), BF16),
            pltpu.VMEM((80, BLK_DEV * 128), F32),
            pltpu.VMEM((12, 8, 128), F32),
            pltpu.VMEM((128, 3 * CH), F32),
            pltpu.VMEM((128, 3 * CH), BF16),
            pltpu.VMEM((9 * CH, 2 * CH), BF16),
            pltpu.VMEM((6 * CH, 2 * CH), BF16),
            pltpu.VMEM((12, COLS_DEV, 128), BF16),
            pltpu.VMEM((3, 10, WIDE, CH), F32),
            pltpu.VMEM((10, WIDE, CH), F32),
            pltpu.VMEM((2, 24, CH), F32),
            pltpu.VMEM((10, COLS_DEV, 2 * CH), BF16),
            pltpu.VMEM((ROWS_DEV, COLS_DEV, CH), F32),
            pltpu.VMEM((2, 2, 1, CH), F32),
            pltpu.VMEM((2, 15, 1, CH), F32),
            pltpu.VMEM((2, 31, 1, CH), F32),
            pltpu.SemaphoreType.DMA((9,)),
            pltpu.SemaphoreType.DMA((13,)),
            pltpu.SemaphoreType.DMA((16,)),
        ],
        compiler_params=pltpu.CompilerParams(
            collective_id=0, has_side_effects=True, vmem_limit_bytes=60 * 1024 * 1024
        ),
    )(
        src_blocks, slot_counts, jnp.transpose(coarse, (1, 0, 2)), remap_tiles.reshape(SLOTS * BCELLS, 1024),
        conv_a, conv_b, *vectors,
    )


def solution(mesh):
    return jax.shard_map(
        per_device,
        mesh=mesh,
        in_specs=(
            P("lon", None, None),
            P(("row", "lon"), None),
            P(("row", "lon")),
            P(("row", "lon"), None, None, None),
            P(),
            P(),
            P(),
            P(),
            P(),
            P(),
        ),
        out_specs=P("row", "lon", None),
        check_vma=False,
    )
```

```python
import jax
import jax.numpy as jnp
from jax import lax
from jax.experimental import pallas as pl
from jax.experimental.pallas import tpu as pltpu
from jax.sharding import PartitionSpec as P

ROWS_DEV = 8
COLS_DEV = 128
VARS = 12
CH = 128
GROUPS = 32
SLOTS = 4
BCELLS = 32
BLK_DEV = 4
NBLK = 128
PER_GROUP = CH // GROUPS
MESH = pl.DeviceIdType.MESH
F32 = jnp.float32
BF16 = jnp.bfloat16

eps = 1e-05


def coords():
    row = lax.axis_index("row")
    lon = lax.axis_index("lon")
    core = lax.rem(row, 2)
    z_hi = lax.rem(lax.div(row, 2), 2)
    x = lax.div(row, 4)
    y = lax.div(lon, 8)
    z = z_hi * 8 + lax.rem(lon, 8)
    return row, lon, x, y, z, core


def device_at(x, y, z, core):
    return (x * 4 + lax.div(z, 8) * 2 + core, y * 8 + lax.rem(z, 8))


def moved(value, step, count):
    return lax.rem(value + step, count) if step else value


def along_z(place):
    _, _, x, y, z, core = place
    steps = [(d, c) for d in range(16) for c in range(2) if d or c]
    steps.sort(key=lambda s: -min(s[0], 16 - s[0]))
    return [device_at(x, y, moved(z, d, 16), moved(core, c, 2)) for d, c in steps]


def across(place):
    _, _, x, y, z, core = place
    steps = [(a, b) for a in range(4) for b in range(4) if a or b]
    steps.sort(key=lambda s: -(min(s[0], 4 - s[0]) + min(s[1], 4 - s[1])))
    return [device_at(moved(x, a, 4), moved(y, b, 4), z, core) for a, b in steps]


def coarse_mates(place):
    _, _, x, y, z, core = place
    z_lo = lax.rem(z, 8)
    mates = []
    for step in (2, 1, -1, -2):
        turn = lax.rem(y + 3 + lax.div(z_lo + 8 + step, 8), 4)
        mates.append(device_at(x, turn, lax.rem(z + 16 + step, 16), core))
    return mates


def iota(shape, dim):
    return lax.broadcasted_iota(jnp.int32, shape, dim)


def split(value):
    high = value.astype(BF16)
    low = (value - high.astype(F32)).astype(BF16)
    return high, low


def dot(a, b, dims=((1,), (0,))):
    return lax.dot_general(a, b, (dims, ((), ())), preferred_element_type=F32)


def over_group(row):
    place = iota(row.shape, 1) & (PER_GROUP - 1)
    total = row
    for step in range(1, PER_GROUP):
        after = pltpu.roll(row, CH - step, 1)
        before = pltpu.roll(row, step, 1)
        total = total + jnp.where(place < PER_GROUP - step, after, 0.0) + jnp.where(place >= step, before, 0.0)
    return total


def add_rows(rows, about, first=0.0, second=0.0):
    for r in rows:
        off = r - about
        first = first + off
        second = second + off * off
    return first, second


def group_mean(r):
    return over_group(jnp.sum(r, axis=0, keepdims=True)) * (1.0 / (PER_GROUP * r.shape[0]))


def pack(mean, dev):
    place = iota((1, CH), 1) & (PER_GROUP - 1)
    return jnp.where(place == 0, mean, jnp.where(place == 1, dev, 0.0))


def group_stats(about, first, second):
    cells = ROWS_DEV * COLS_DEV * PER_GROUP
    first = over_group(jnp.sum(first, axis=0, keepdims=True))
    second = over_group(jnp.sum(second, axis=0, keepdims=True))
    mean_off = first * (1.0 / cells)
    return pack(about + mean_off, second - first * mean_off)


def merge(packed, others, cells):
    count = others.shape[0] + 1
    off = others - packed
    first = jnp.sum(off, axis=0)
    apart = cells * (jnp.sum(off * off, axis=0) - first * first * (1.0 / count))
    return pack(packed + first * (1.0 / count), packed * count + first + pltpu.roll(apart, 1, 1))


def unpack(packed, cells):
    place = iota((1, CH), 1) & (PER_GROUP - 1)
    mean = over_group(jnp.where(place == 0, packed, 0.0))
    dev = over_group(jnp.where(place == 1, packed, 0.0))
    return mean, lax.rsqrt(dev * (1.0 / cells) + eps)


LEFT, MAIN, RIGHT, WIDE = 8, 16, 144, 160


def prepare_b(cb_v, wba, wbb):
    for dy in range(3):
        for dx in range(2):
            span = slice(dx * CH, (dx + 1) * CH)
            high, low = split(cb_v[dy, dx])
            wba[dy * 256 : dy * 256 + 128, span] = high
            wba[dy * 256 + 128 : dy * 256 + 256, span] = high
            wba[768 + dy * 128 : 896 + dy * 128, span] = low
        high, low = split(cb_v[dy, 2])
        for part, value in enumerate((high, high, low)):
            if dy < 2:
                wbb[part * 256 + dy * 128 : part * 256 + dy * 128 + 128, 0:CH] = value
            else:
                wbb[part * 256 : part * 256 + 128, CH : 2 * CH] = jnp.zeros((CH, CH), BF16)
                wbb[part * 256 + 128 : part * 256 + 256, CH : 2 * CH] = value


def activate(value, mean, scale, shift):
    half = ((value - mean) * scale + shift) * 0.5
    return half + half * jnp.tanh(half)


def second_conv(ha, hl, act, gs, hb, wba, wbb, mean, scale, shift, not_first, not_last):
    for i in range(10):
        value = activate(ha[i, MAIN:RIGHT, :], mean, scale, shift)
        if i == 0:
            value = value * not_first
        if i == 9:
            value = value * not_last
        act[i, :, 0:128], act[i, :, 128:256] = split(value)
    known = iota((16, 1), 0)
    known = jnp.where(known == 0, not_first, jnp.where(known == 9, not_last, 1.0))
    for i in range(2):
        hl[i, 0:16, :] = activate(hl[i, 0:16, :], mean, scale, shift) * known

    def side(i, dy):
        return split(hl[i, dy : dy + 16, :])

    def rows(first, size, part):
        return act[first : first + size, :, part * 128 : part * 128 + 128].reshape(size * 128, 128)

    pieces = [act[dy : dy + 8].reshape(1024, 256) for dy in range(3)] + [rows(dy, 8, 0) for dy in range(3)]
    at_side = [side(0, dy) for dy in range(3)]
    at_side = [part for pair in at_side for part in pair] + [pair[0] for pair in at_side]
    field = jnp.concatenate([jnp.concatenate(pieces, axis=1), jnp.concatenate(at_side, axis=1)], axis=0)
    early = dot(field, wba[...])

    pieces = [rows(0, 9, 0), rows(1, 9, 0), rows(0, 9, 1), rows(1, 9, 1), rows(0, 9, 0), rows(1, 9, 0)]
    (high0, low0), (high1, low1) = side(1, 0), side(1, 1)
    at_side = [high0, high1, low0, low1, high0, high1]
    field = jnp.concatenate([jnp.concatenate(pieces, axis=1), jnp.concatenate(at_side, axis=1)], axis=0)
    late = dot(field, wbb[...])

    for i in range(8):
        gs[0, i, MAIN:RIGHT, :] = early[i * 128 : (i + 1) * 128, 0:128]
        gs[0, i, MAIN - 1 : MAIN, :] = early[1024 + i : 1025 + i, 0:128]
        gs[2, i, MAIN:RIGHT, :] = late[i * 128 : (i + 1) * 128, 0:128] + late[(i + 1) * 128 : (i + 2) * 128, 128:256]
        gs[2, i, RIGHT : RIGHT + 1, :] = late[1152 + i : 1153 + i, 0:128] + late[1153 + i : 1154 + i, 128:256]
        hb[i] = gs[0, i, MAIN - 1 : RIGHT - 1, :] + early[i * 128 : (i + 1) * 128, 128:256] + gs[2, i, MAIN + 1 : RIGHT + 1, :]


def kernel(
    src_hbm, cnt_ref, coarse_ref, remap_ref, ca_ref, cb_ref, gain_a_ref, shift_a_ref, gain_b_ref, shift_b_ref,
    out_ref,
    src_ref, coarse_v, remap_v, ca_v, cb_v, vec_v,
    tt, row_out, col_out, corner_out, mate_out, next_out, choice_out,
    row_in, col_in, corner_in, mate_in, next_in, choice_in, side_choice,
    copies, choices, side, wa32, wa, wba, wbb,
    xs, gs, ha, hl, act, hb,
    stat, buf_x, buf_z,
    in_sem, send_sem, recv_sem,
):
    place = coords()
    row, lon = place[0], place[1]
    z_mates = along_z(place)
    xy_mates = across(place)
    lon_mates = coarse_mates(place)
    lon_left, lon_right = lax.rem(lon + 31, 32), lax.rem(lon + 1, 32)
    odd = lax.rem(row, 2)
    is_odd = odd == 1
    has_far = jnp.where(is_odd, row < 15, row > 0)
    near_row = row + 1 - 2 * odd
    far_row = lax.rem(row + 2 * odd + 15, 16)
    halo = [
        (far_row, lon), (far_row, lon_right), (far_row, lon_left), (near_row, lon),
        (near_row, lon_right), (near_row, lon_left), (row, lon_right), (row, lon_left),
    ]
    barrier = pltpu.get_barrier_semaphore()
    partners = halo[3:] + lon_mates + z_mates + xy_mates

    @pl.when(has_far)
    def _():
        for mate in halo[:3]:
            pl.semaphore_signal(barrier, inc=1, device_id=mate, device_id_type=MESH)

    for mate in partners:
        pl.semaphore_signal(barrier, inc=1, device_id=mate, device_id_type=MESH)

    loads = [
        pltpu.make_async_copy(coarse_ref, coarse_v, in_sem.at[0]),
        pltpu.make_async_copy(remap_ref, remap_v, in_sem.at[1]),
        pltpu.make_async_copy(ca_ref, ca_v, in_sem.at[2]),
        pltpu.make_async_copy(cb_ref, cb_v, in_sem.at[3]),
    ]
    for i, ref in enumerate((gain_a_ref, shift_a_ref, gain_b_ref, shift_b_ref)):
        loads.append(pltpu.make_async_copy(ref, vec_v.at[i], in_sem.at[4 + i]))
    sources = pltpu.make_async_copy(src_hbm, src_ref, in_sem.at[8])
    for load in [sources] + loads:
        load.start()

    sources.wait()
    lane = iota((1, 128), 1)
    own_choice = jnp.zeros((1, 128), F32)
    for k in range(SLOTS):
        local = lax.rem(src_ref[0, k] - (lon - 1) * BLK_DEV + 2 * NBLK, NBLK)
        local = jnp.where(k < cnt_ref[0], local, -64)
        own_choice = jnp.where((lane >> 5) == k, local.astype(F32), own_choice)

    for q in range(BLK_DEV):
        want = q * BCELLS + (lane & (BCELLS - 1))
        copies[:, q * 128 : (q + 1) * 128] = jnp.where(iota((128, 128), 0) == want, 1.0, 0.0).astype(BF16)

    loads[0].wait()
    held = coarse_v[...].astype(F32)
    tile = jnp.zeros((VARS, 128), F32)
    for b in range(BLK_DEV):
        put = jnp.where(iota((BCELLS, 128), 0) + b * BCELLS == iota((BCELLS, 128), 1), 1.0, 0.0)
        tile = tile + dot(held[:, b, :].astype(BF16), put.astype(BF16))
    pad = jnp.concatenate([tile, jnp.zeros((16 - VARS, 128), F32)], axis=0)
    tt[2] = pad.astype(BF16)

    loads[1].wait()
    at = iota((224, 1), 0)
    inner = at & 15
    cell = at + odd * (7 * COLS_DEV)
    column = (inner & 7) * COLS_DEV + (inner >> 3)
    cell = jnp.where((at >= 128) & (at < 144), column + 126, cell)
    cell = jnp.where((at >= 144) & (at < 160), column, cell)
    for i, (row0, col0) in enumerate(((6 * odd, 126), (6 * odd, 0), (6 - 6 * odd, 126), (6 - 6 * odd, 0))):
        here = jnp.where(inner < 4, (row0 + (inner >> 1)) * COLS_DEV + col0 + (inner & 1), -1)
        cell = jnp.where((at >= 160 + 16 * i) & (at < 176 + 16 * i), here, cell)
    pick = jnp.where(iota((224, 1024), 1) == cell, 1.0, 0.0).astype(BF16)
    weights = dot(pick, remap_v[...], ((1,), (1,))).astype(BF16)
    row_out[...] = weights[0:128]
    choice_out[...] = own_choice
    for i in range(2):
        col_out[i] = weights[128 + 16 * i : 144 + 16 * i]
    for i in range(4):
        cells = weights[160 + 16 * i : 176 + 16 * i].astype(F32)
        corner_out[i] = jnp.where(iota((8, 128), 0) < 4, cells[0:8], own_choice)
    side[...] = jnp.zeros_like(side)
    hl[...] = jnp.zeros_like(hl)
    xs[...] = jnp.zeros_like(xs)

    twelfth_l = (lane * 43) >> 9
    var_l = jnp.where(lane < 9 * VARS, lane - 12 * twelfth_l, 4096)
    part_l = twelfth_l - 3 * ((twelfth_l * 11) >> 5)
    want = jnp.where(part_l == 1, var_l + 16, var_l)
    spread_msg = jnp.where(iota((32, 128), 0) == want, 1.0, 0.0).astype(BF16)
    spread_var = jnp.where(iota((16, 128), 0) == var_l, 1.0, 0.0).astype(BF16)
    not_first = jnp.where(row > 0, 1.0, 0.0).astype(F32)
    not_last = jnp.where(row < 15, 1.0, 0.0).astype(F32)

    @pl.when(jnp.logical_not(has_far))
    def _():
        row_in[...] = jnp.zeros_like(row_in)
        choice_in[...] = jnp.zeros_like(choice_in)
        next_in[...] = jnp.zeros_like(next_in)
        corner_in[0:2] = jnp.zeros((2, 8, 128), F32)

    pl.semaphore_wait(barrier, len(partners) + 3 * jnp.where(has_far, 1, 0))

    def send(src, dst, mate, out, into):
        copy = pltpu.make_async_remote_copy(
            src_ref=src, dst_ref=dst, send_sem=send_sem.at[out], recv_sem=recv_sem.at[into],
            device_id=mate, device_id_type=MESH,
        )
        copy.start()

    for i in range(2):
        send(col_out.at[i], col_in.at[i], halo[6 + i], 8, 2)
        send(choice_out, side_choice.at[i], halo[6 + i], 12, 15)
    for i in (2, 3):
        send(corner_out.at[i, pl.ds(0, 5)], corner_in.at[i, pl.ds(0, 5)], halo[2 + i], 9, 12)

    @pl.when(has_far)
    def _():
        for i in (0, 1):
            send(corner_out.at[i, pl.ds(0, 5)], corner_in.at[i, pl.ds(0, 5)], halo[1 + i], 1, 1)
        send(row_out, row_in, halo[0], 0, 0)
        send(choice_out, choice_in, halo[0], 11, 14)

    along_lon = [
        pltpu.make_async_remote_copy(
            src_ref=tt.at[2], dst_ref=tt.at[slot], send_sem=send_sem.at[7], recv_sem=recv_sem.at[8 + i],
            device_id=mate, device_id_type=MESH,
        )
        for i, (slot, mate) in enumerate(zip((0, 1, 3, 4), lon_mates))
    ]
    for copy in along_lon:
        copy.start()

    loads[2].wait()
    wa32[...] = jnp.zeros_like(wa32)
    for dy in range(3):
        for part in range(3):
            first = (dy * 3 + part) * VARS
            for dx in range(3):
                wa32[first : first + VARS, dx * CH : (dx + 1) * CH] = ca_v[dy, dx]
    line = iota((128, 3 * CH), 0)
    twelfth = (line * 43) >> 9
    part_of = twelfth - 3 * ((twelfth * 11) >> 5)
    whole = wa32[...]
    high, low = split(whole)
    wa[...] = jnp.where(part_of == 2, low.astype(F32), high.astype(F32)).astype(BF16)

    for copy in along_lon:
        copy.wait_recv()
    choices[...] = dot(tt[...].reshape(80, 128), copies[...])

    def chosen(choice, first_tile):
        total = jnp.zeros((16, 128), F32)
        for j in range(3 * BLK_DEV):
            t, q = first_tile + j // BLK_DEV, j % BLK_DEV
            total = jnp.where(choice == j, choices[t * 16 : t * 16 + 16, q * 128 : (q + 1) * 128], total)
        return total

    blocks = chosen(own_choice, 1).astype(BF16)

    four = jnp.concatenate([remap_v[:, 0:256], remap_v[:, 768:1024]], axis=1)
    four = dot(blocks, four)
    mate_out[0] = jnp.where(is_odd, four[:, 0:128], four[:, 384:512])
    mate_out[1] = jnp.where(is_odd, four[:, 128:256], four[:, 256:384])
    next_out[...] = jnp.where(is_odd, four[:, 256:384], four[:, 128:256])
    send(mate_out, mate_in, halo[3], 2, 3)

    @pl.when(has_far)
    def _():
        send(next_out, next_in, halo[0], 10, 13)


    spread_blocks = dot(blocks, spread_var, ((0,), (0,))).astype(BF16)
    fine = dot(remap_v[...], spread_blocks, ((0,), (0,)))
    high, low = split(fine)
    packed = jnp.where(part_l == 1, low.astype(F32), high.astype(F32)).astype(BF16)
    xs[2:10] = packed.reshape(ROWS_DEV, COLS_DEV, 128)

    third = jnp.broadcast_to(lane, (128, 128))

    def patches(before, here, after, lanes):
        before = jnp.where(lanes < 3 * VARS, before.astype(F32), 0.0)
        here = jnp.where((lanes >= 3 * VARS) & (lanes < 6 * VARS), here.astype(F32), 0.0)
        after = jnp.where(lanes >= 6 * VARS, after.astype(F32), 0.0)
        return (before + here + after).astype(BF16)

    def taps(out_rows):
        field = [patches(xs[i], xs[i + 1], xs[i + 2], third) for i in out_rows]
        result = dot(jnp.concatenate(field, axis=0), wa[...])
        for n, i in enumerate(out_rows):
            for dx in range(3):
                gs[dx, i, MAIN:RIGHT, :] = result[n * 128 : (n + 1) * 128, dx * CH : (dx + 1) * CH]

    def joined(i, first, size):
        return gs[0, i, first - 1 : first - 1 + size, :] + gs[1, i, first : first + size, :] + gs[2, i, first + 1 : first + 1 + size, :]

    taps(list(range(2, 8)))

    def placed(fine):
        high, low = split(fine)
        return dot(jnp.concatenate([high, low], axis=0), spread_msg, ((0,), (0,))).astype(BF16)

    pltpu.make_async_copy(mate_in, mate_in, recv_sem.at[3]).wait()
    xs[10 - 9 * odd] = placed(mate_in[0])
    xs[11 - 11 * odd] = placed(mate_in[1])

    far_known = jnp.where(is_odd, not_last, not_first)

    def fine_of(cells, choice, first_tile, known):
        held = chosen(choice.astype(F32), first_tile) * known
        return dot(cells.astype(BF16), held.astype(BF16), ((1,), (1,)))

    def spread_cells(parts):
        high, low = split(jnp.concatenate(parts, axis=0))
        return dot(jnp.concatenate([high, low], axis=1), spread_msg)

    def put_corner(cells, first_row, place):
        for n in range(4):
            side[first_row + (n >> 1), place + (n & 1) : place + (n & 1) + 1, :] = cells[n : n + 1]

    def corners(first):
        some = corner_in.at[pl.ds(first, 2), pl.ds(0, 5)]
        return pltpu.make_async_copy(some, some, recv_sem.at[1 if first == 0 else 12])

    pltpu.make_async_copy(col_in, col_in, recv_sem.at[2]).wait()
    pltpu.make_async_copy(side_choice, side_choice, recv_sem.at[15]).wait()
    corners(2).wait()
    cells = spread_cells([
        fine_of(col_in[0], side_choice[0], 0, 1.0),
        fine_of(col_in[1], side_choice[1], 2, 1.0),
        fine_of(corner_in[2], corner_in[2, 4:5, :], 0, 1.0),
        fine_of(corner_in[3], corner_in[3, 4:5, :], 2, 1.0),
    ])
    for i, place_at in enumerate((6, 0)):
        for n in range(16):
            at_col = place_at + (n >> 3)
            side[(n & 7) + 2, at_col : at_col + 1, :] = cells[16 * i + n : 16 * i + n + 1]
    put_corner(cells[32:40], 10 - 10 * odd, 6)
    put_corner(cells[40:48], 10 - 10 * odd, 0)
    near_border, far_border, near_beyond, far_beyond = 8 - 7 * odd, 1 + 7 * odd, 9 - 9 * odd, 9 * odd
    taps([near_border])

    def side_taps():
        side_lane = jnp.broadcast_to(lane.reshape(1, 1, 128), (10, 8, 128))
        side_patches = patches(side[0:10], side[1:11], side[2:12], side_lane).reshape(80, 128)
        result = dot(side_patches, wa[...]).reshape(10, 8, 3 * CH)
        for dx in range(3):
            piece = result[:, :, dx * CH : (dx + 1) * CH]
            gs[dx, :, LEFT:MAIN, :] = piece
            gs[dx, :, RIGHT : RIGHT + 8, :] = piece

    side_taps()
    inner_rows = [2, 3, 4, 5, 6, 7, near_border]
    for i in inner_rows:
        ha[i, MAIN:RIGHT, :] = joined(i, MAIN, 128)
    about = group_mean(ha[2, MAIN:RIGHT, :])
    first, second = add_rows([ha[i, MAIN:RIGHT, :] for i in inner_rows], about)

    @pl.when(has_far)
    def _():
        corners(0).wait()
        pltpu.make_async_copy(choice_in, choice_in, recv_sem.at[14]).wait()
        pltpu.make_async_copy(row_in, row_in, recv_sem.at[0]).wait()

    cells = spread_cells([
        fine_of(row_in[...], choice_in[...], 1, far_known),
        fine_of(corner_in[0], corner_in[0, 4:5, :], 0, far_known),
        fine_of(corner_in[1], corner_in[1, 4:5, :], 2, far_known),
    ])
    xs[1 + 9 * odd] = cells[0:128].astype(BF16)
    put_corner(cells[128:136], 10 * odd, 6)
    put_corner(cells[136:144], 10 * odd, 0)
    side_taps()
    taps([far_border])
    border = joined(far_border, MAIN, 128)
    ha[far_border, MAIN:RIGHT, :] = border
    sums = group_stats(about, *add_rows([border], about, first, second))

    def all_reduce(turn, packed, beside):
        cells = ROWS_DEV * COLS_DEV * PER_GROUP
        for stage, (mates, buf) in enumerate(((z_mates, buf_z), (xy_mates, buf_x))):
            sem = 4 + turn * 2 + stage
            stat[turn, stage] = packed
            for j, mate in enumerate(mates):
                pltpu.make_async_remote_copy(
                    src_ref=stat.at[turn, stage], dst_ref=buf.at[turn, j], send_sem=send_sem.at[sem - 1], recv_sem=recv_sem.at[sem],
                    device_id=mate, device_id_type=MESH,
                ).start()
            beside(stage)
            pltpu.make_async_copy(buf.at[turn], buf.at[turn], recv_sem.at[sem]).wait()
            packed = merge(packed, buf[turn], cells)
            cells = cells * (len(mates) + 1)
        return unpack(packed, cells)

    def around_a(stage):
        if stage == 0:

            for load in loads[3:]:
                load.wait()
            prepare_b(cb_v, wba, wbb)
            new_rows, all_rows = [near_beyond], list(range(1, 9)) + [near_beyond]
        else:

            @pl.when(has_far)
            def _():
                pltpu.make_async_copy(next_in, next_in, recv_sem.at[13]).wait()

            xs[11 * odd] = placed(next_in[...] * far_known)
            new_rows, all_rows = [far_beyond], [far_beyond]
        taps(new_rows)
        for i in new_rows:
            ha[i, MAIN:RIGHT, :] = joined(i, MAIN, 128)
        for i in all_rows:
            hl[0, pl.ds(i, 1), :] = joined(i, MAIN - 1, 1)
            hl[1, pl.ds(i, 1), :] = joined(i, RIGHT, 1)

    mean, inverse = all_reduce(0, sums, around_a)

    second_conv(ha, hl, act, gs, hb, wba, wbb, mean, inverse * vec_v[0], vec_v[1], not_first, not_last)
    about = group_mean(hb[0])
    sums = group_stats(about, *add_rows([hb[i] for i in range(8)], about))
    mean, inverse = all_reduce(1, sums, lambda stage: None)
    scale = inverse * vec_v[2]
    for i in range(8):
        out_ref[i] = activate(hb[i], mean, scale, vec_v[3]).astype(BF16)

    @pl.when(has_far)
    def _():
        pltpu.make_async_copy(row_in, row_in, send_sem.at[0]).wait()
        pltpu.make_async_copy(choice_in, choice_in, send_sem.at[11]).wait()
        pltpu.make_async_copy(next_in, next_in, send_sem.at[10]).wait()
        some = corner_in.at[pl.ds(0, 2), pl.ds(0, 5)]
        pltpu.make_async_copy(some, some, send_sem.at[1]).wait()

    some = corner_in.at[pl.ds(2, 2), pl.ds(0, 5)]
    pltpu.make_async_copy(some, some, send_sem.at[9]).wait()
    pltpu.make_async_copy(col_in, col_in, send_sem.at[8]).wait()
    pltpu.make_async_copy(side_choice, side_choice, send_sem.at[12]).wait()
    pltpu.make_async_copy(mate_in, mate_in, send_sem.at[2]).wait()
    pltpu.make_async_copy(tt.at[pl.ds(0, 4)], tt.at[pl.ds(0, 4)], send_sem.at[7]).wait()
    for turn in range(2):
        pltpu.make_async_copy(buf_z.at[turn], buf_z.at[turn], send_sem.at[3 + 2 * turn]).wait()
        pltpu.make_async_copy(buf_x.at[turn], buf_x.at[turn], send_sem.at[4 + 2 * turn]).wait()


def per_device(
    coarse, src_blocks, slot_counts, remap_tiles, conv_a, conv_b, gain_a, shift_a, gain_b, shift_b
):
    anywhere = pl.BlockSpec(memory_space=pl.ANY)
    vectors = [v.reshape(1, CH) for v in (gain_a, shift_a, gain_b, shift_b)]
    return pl.pallas_call(
        kernel,
        name="stem",
        out_shape=pltpu.VMEM((ROWS_DEV, COLS_DEV, CH), BF16),
        in_specs=[anywhere, pl.BlockSpec(memory_space=pltpu.SMEM)] + [anywhere] * 8,
        out_specs=pl.BlockSpec(memory_space=pltpu.VMEM),
        scratch_shapes=[
            pltpu.SMEM((1, SLOTS), jnp.int32),
            pltpu.VMEM((VARS, BLK_DEV, BCELLS), BF16),
            pltpu.VMEM((128, 1024), BF16),
            pltpu.VMEM((3, 3, VARS, CH), F32),
            pltpu.VMEM((3, 3, CH, CH), F32),
            pltpu.VMEM((4, 1, CH), F32),
            pltpu.VMEM((5, 16, 128), BF16),
            pltpu.VMEM((128, 128), BF16),
            pltpu.VMEM((2, 16, 128), BF16),
            pltpu.VMEM((4, 8, 128), F32),
            pltpu.VMEM((2, 16, 128), F32),
            pltpu.VMEM((16, 128), F32),
            pltpu.VMEM((1, 128), F32),
            pltpu.VMEM((128, 128), BF16),
            pltpu.VMEM((2, 16, 128), BF16),
            pltpu.VMEM((4, 8, 128), F32),
            pltpu.VMEM((2, 16, 128), F32),
            pltpu.VMEM((16, 128), F32),
            pltpu.VMEM((1, 128), F32),
            pltpu.VMEM((2, 1, 128), F32),
            pltpu.VMEM((128, BLK_DEV * 128), BF16),
            pltpu.VMEM((80, BLK_DEV * 128), F32),
            pltpu.VMEM((12, 8, 128), F32),
            pltpu.VMEM((128, 3 * CH), F32),
            pltpu.VMEM((128, 3 * CH), BF16),
            pltpu.VMEM((9 * CH, 2 * CH), BF16),
            pltpu.VMEM((6 * CH, 2 * CH), BF16),
            pltpu.VMEM((12, COLS_DEV, 128), BF16),
            pltpu.VMEM((3, 10, WIDE, CH), F32),
            pltpu.VMEM((10, WIDE, CH), F32),
            pltpu.VMEM((2, 24, CH), F32),
            pltpu.VMEM((10, COLS_DEV, 2 * CH), BF16),
            pltpu.VMEM((ROWS_DEV, COLS_DEV, CH), F32),
            pltpu.VMEM((2, 2, 1, CH), F32),
            pltpu.VMEM((2, 15, 1, CH), F32),
            pltpu.VMEM((2, 31, 1, CH), F32),
            pltpu.SemaphoreType.DMA((9,)),
            pltpu.SemaphoreType.DMA((13,)),
            pltpu.SemaphoreType.DMA((16,)),
        ],
        compiler_params=pltpu.CompilerParams(
            collective_id=0, has_side_effects=True, vmem_limit_bytes=60 * 1024 * 1024
        ),
    )(
        src_blocks, slot_counts, jnp.transpose(coarse, (1, 0, 2)), remap_tiles.reshape(SLOTS * BCELLS, 1024),
        conv_a, conv_b, *vectors,
    )


def solution(mesh):
    return jax.shard_map(
        per_device,
        mesh=mesh,
        in_specs=(
            P("lon", None, None),
            P(("row", "lon"), None),
            P(("row", "lon")),
            P(("row", "lon"), None, None, None),
            P(),
            P(),
            P(),
            P(),
            P(),
            P(),
        ),
        out_specs=P("row", "lon", None),
        check_vma=False,
    )
```
